512 devices in a mesh: group: 4 (over x_hi, core), slab: 128 (over z, y, x_lo).
Axes of the slice: x: 4 (x_hi: 2, x_lo: 2; x = x_hi * 2 + x_lo), y: 4, z: 16, core: 2. Of those that a mesh axis runs over, the one named last changes fastest.
Arguments:
- populations: float32 [19, 2048, 16, 128], P(None, ('group', 'slab')), may hold values from 0 to 1, as said below
- cell_kind: int32 [2048, 16, 128], P(('group', 'slab')), may hold values from 0 to 2, as said below
- snapshot_order: int32 [4], replicated, may hold values from 0 to 3, each once
- sample_phase: int32 [3], replicated, may hold values from 0 to 3
- slab_map: int32 [384], replicated, may hold values from 0 to 383, each once
- weighted_modes: float32 [589824, 252], P(('group', 'slab')), may hold values from -0.6 to 0.6
Outputs:
- lattice: float32 [19, 2048, 16, 128], P(None, ('group', 'slab'))
- basis_rows: float32 [589824, 256], P(('group', 'slab'))
The draws below stay inside these ranges and needn't reach their ends.
Inputs may be any that keep to these rules, and one draw needn't show every extreme that they name: `populations`: each population lies between 0.4 and 1.6 times the weight of its direction. `cell_kind`: 0 marks a fluid cell, 1 a wall cell, 2 an inlet cell. `snapshot_order`: a permutation of the steps. `slab_map`: a permutation of the row blocks.
All inputs are finite; a program needn't handle non-finite values.
Results may differ from the reference program's by a relative error of at most 0.0003.
Values sent between devices are 32-bit elements; how exact they have to be, the bound alone decides.
A program may use at most 64 MiB of HBM per device.

```python
import math
import jax
import jax.numpy as jnp
from jax import lax

DIRS = 19
CX = 4
NY = 16
NZ = 128
STEPS = 4
SNAPS = 4
SUB = 4
MODES = 252
RANK = 256
SLABS = 384
NXC = 1536
XALL = 2048
BLOCK = 384
ROWS = 147456
ROWS_ALL = 589824


lattice_weights = [1.0 / 3.0] + [1.0 / 18.0] * 6 + [1.0 / 36.0] * 12


def draw_populations(key, part):
    key = jax.random.fold_in(key, 11)
    shape = (DIRS, XALL, NY, NZ)
    weights = jnp.array(lattice_weights, jnp.float32)[:, None, None, None]
    values = 1.0 + 0.2 * jnp.clip(jax.random.normal(key, shape, jnp.float32), -3.0, 3.0)
    return weights * values


def draw_cell_kind(key, part):
    key = jax.random.fold_in(key, 23)
    shape = (XALL, NY, NZ)
    obstacle = jax.random.randint(key, shape, 0, 16) == 0
    across = jnp.arange(NY, dtype=jnp.int32)[None, :, None]
    along = jnp.arange(XALL, dtype=jnp.int32)[:, None, None]
    walled = obstacle | (across == 0) | (across == NY - 1)
    inflow = (along == 0) & jnp.logical_not(walled)
    return jnp.where(walled, 1, jnp.where(inflow, 2, 0)).astype(jnp.int32)


def shard_levels(stream_key, shape, split, least, largest):
    loudness = 1.0
    for position, shards_of in split:
        steps = jax.random.uniform(jax.random.fold_in(jax.random.fold_in(stream_key, 6), position), (shards_of,), jnp.float32, least / len(split), largest / len(split))
        loudness = loudness * jnp.repeat(jnp.exp(steps), shape[position] // shards_of).reshape((-1,) + (1,) * (len(shape) - 1 - position))
    return loudness


def scatter_about(stream_key, extent, spread, bound, split=(), held_as=jnp.bfloat16):
    values = spread * jax.random.normal(stream_key, extent, jnp.float32)
    if split:
        values = values * shard_levels(stream_key, extent, split, -0.22, 0.18)
    return jnp.clip(values, -bound, bound).astype(held_as)


def setup_inputs(seed: int = 0) -> dict:
    key_of = jax.random.split(jax.random.key(seed), 7)
    return {
        "populations": draw_populations(jax.random.fold_in(key_of[6], 71), 0),
        "cell_kind": draw_cell_kind(jax.random.fold_in(key_of[6], 71), 0),
        "snapshot_order": jax.random.permutation(key_of[2], STEPS).astype(jnp.int32),
        "sample_phase": jax.random.randint(key_of[3], (3,), 0, SUB).astype(jnp.int32),
        "slab_map": jax.random.permutation(key_of[4], SLABS).astype(jnp.int32),
        "weighted_modes": scatter_about(key_of[5], (ROWS_ALL, MODES), 0.1, 0.6, ((0, 512),), jnp.float32),
    }


lattice_dirs = [(0, 0, 0), (1, 0, 0), (-1, 0, 0), (0, 1, 0), (0, -1, 0), (0, 0, 1), (0, 0, -1), (1, 1, 0), (-1, -1, 0), (1, -1, 0), (-1, 1, 0), (1, 0, 1), (-1, 0, -1), (1, 0, -1), (-1, 0, 1), (0, 1, 1), (0, -1, -1), (0, 1, -1), (0, -1, 1)]
lattice_weights = [1.0 / 3.0] + [1.0 / 18.0] * 6 + [1.0 / 36.0] * 12
opposite_dir = [0, 2, 1, 4, 3, 6, 5, 8, 7, 10, 9, 12, 11, 14, 13, 16, 15, 18, 17]
omega_rate = 0.9
inlet_speed = 0.05

def equilibrium(density, speeds):
    first, second, third = speeds
    square = first * first + second * second + third * third
    terms = []
    for direction in range(19):
        east, north, upward = lattice_dirs[direction]
        along = east * first + north * second + upward * third
        terms.append(lattice_weights[direction] * density * (1.0 + 3.0 * along + 4.5 * along * along - 1.5 * square))
    return jnp.stack(terms)

def moments(field):
    density = lax.optimization_barrier(jnp.sum(field, axis=0))
    speeds = []
    for axis_pos in range(3):
        total = jnp.zeros_like(density)
        for direction in range(19):
            factor = lattice_dirs[direction][axis_pos]
            if factor != 0:
                total = total + factor * field[direction]
        speeds.append(total / density)
    return (density, speeds)

def collide(field, kind):
    density, speeds = moments(field)
    relaxed = field - omega_rate * (field - equilibrium(density, speeds))
    unity = jnp.ones_like(density)
    inflow = equilibrium(unity, (inlet_speed * unity, 0.0 * unity, 0.0 * unity))
    return jnp.where(kind == 0, relaxed, jnp.where(kind == 2, inflow, field))

def stream(padded, post, kind_pad, kind):
    width = post.shape[1]
    result = []
    for direction in range(19):
        east, north, upward = lattice_dirs[direction]
        source = jnp.roll(padded[direction, 1 - east:1 - east + width], (north, upward), (1, 2))
        source_kind = jnp.roll(kind_pad[1 - east:1 - east + width], (north, upward), (1, 2))
        bounced = jnp.where(source_kind == 1, post[opposite_dir[direction]], source)
        result.append(jnp.where(kind == 1, post[direction], bounced))
    return jnp.stack(result)

def sample(field, kind, phase):
    density, speeds = moments(field)
    speed = jnp.where(kind == 1, 0.0, jnp.stack(speeds))
    shape = speed.shape
    grid = speed.reshape(3, shape[1] // SUB, SUB, shape[2] // SUB, SUB, shape[3] // SUB, SUB)
    grid = lax.dynamic_index_in_dim(grid, phase[2], 6, keepdims=False)
    grid = lax.dynamic_index_in_dim(grid, phase[1], 4, keepdims=False)
    grid = lax.dynamic_index_in_dim(grid, phase[0], 2, keepdims=False)
    return grid

def gram_of(left, right):
    return lax.dot_general(left.astype(jnp.float32), right.astype(jnp.float32), (((0,), (0,)), ((), ())), precision=lax.Precision.HIGHEST, preferred_element_type=jnp.float32)

def reference(populations, cell_kind, snapshot_order, sample_phase, slab_map, weighted_modes):
    field = populations[:, :NXC]
    kind = cell_kind[:NXC]
    kind_pad = jnp.pad(kind, ((1, 1), (0, 0), (0, 0)), constant_values=1)
    samples = []
    for step in range(STEPS):
        post = collide(field, kind)
        padded = jnp.pad(post, ((0, 0), (1, 1), (0, 0), (0, 0)))
        field = stream(padded, post, kind_pad, kind)
        samples.append(sample(field, kind, sample_phase))
    chosen = jnp.take(jnp.stack(samples), snapshot_order, axis=0)
    blocks = chosen.reshape(SNAPS, 3, SLABS, CX // SUB, NY // SUB, NZ // SUB)
    blocks = jnp.transpose(blocks, (2, 0, 1, 3, 4, 5)).reshape(SLABS, SNAPS, BLOCK)
    inverse = jnp.zeros((SLABS,), jnp.int32).at[slab_map].set(jnp.arange(SLABS, dtype=jnp.int32))
    ordered = jnp.take(blocks, inverse, axis=0)
    snaps = jnp.transpose(ordered, (0, 2, 1)).reshape(ROWS, SNAPS)
    stacked = jnp.concatenate([weighted_modes[ROWS_ALL - ROWS:], snaps], axis=1)
    lower = jnp.linalg.cholesky(gram_of(stacked, stacked))
    solved = lax.linalg.triangular_solve(lower, stacked, left_side=False, lower=True, transpose_a=True)
    basis = jnp.concatenate([jnp.zeros((ROWS_ALL - ROWS, RANK), jnp.float32), solved * math.sqrt(ROWS)], axis=0)
    lattice = jnp.concatenate([field, jnp.zeros((DIRS, XALL - NXC, NY, NZ), jnp.float32)], axis=1)
    return (lattice, basis)
```

```python
import functools
import math

import jax
import jax.numpy as jnp
from jax import lax
from jax.experimental import pallas as pl
from jax.experimental.pallas import tpu as pltpu
from jax.sharding import PartitionSpec as P

MESH = pl.DeviceIdType.MESH
STEPS = 4
SUB = 4
OMEGA = 0.9
INLET = 0.05
BIG = 1e30

DIRS = [
    (0, 0, 0),
    (1, 0, 0),
    (-1, 0, 0),
    (0, 1, 0),
    (0, -1, 0),
    (0, 0, 1),
    (0, 0, -1),
    (1, 1, 0),
    (-1, -1, 0),
    (1, -1, 0),
    (-1, 1, 0),
    (1, 0, 1),
    (-1, 0, -1),
    (1, 0, -1),
    (-1, 0, 1),
    (0, 1, 1),
    (0, -1, -1),
    (0, 1, -1),
    (0, -1, 1),
]
WEIGHTS = [1.0 / 3.0] + [1.0 / 18.0] * 6 + [1.0 / 36.0] * 12
OPP = [0, 2, 1, 4, 3, 6, 5, 8, 7, 10, 9, 12, 11, 14, 13, 16, 15, 18, 17]
EAST = [i for i in range(19) if DIRS[i][0] == 1]
WEST = [i for i in range(19) if DIRS[i][0] == -1]
REST = [i for i in range(19) if DIRS[i][0] == 0]

CX, NY, NZ = 4, 16, 128
NLINE = 16
NPLANE = 8
RANK = 256
MODES = 252
ROWS_DEV = 1152


def mm(a, b, dims):
    return lax.dot_general(
        a,
        b,
        (dims, ((), ())),
        precision=lax.Precision.HIGHEST,
        preferred_element_type=jnp.float32,
    )


def inflow_value(i):
    along = DIRS[i][0] * INLET
    return WEIGHTS[i] * (1.0 + 3.0 * along + 4.5 * along * along - 1.5 * INLET * INLET)


def moments(f):
    density = f[0]
    for i in range(1, 19):
        density = density + f[i]
    inverse = 1.0 / density
    speeds = []
    for axis in range(3):
        plus = [f[i] for i in range(19) if DIRS[i][axis] == 1]
        minus = [f[i] for i in range(19) if DIRS[i][axis] == -1]
        total = functools.reduce(lambda a, b: a + b, [a - b for a, b in zip(plus, minus)])
        speeds.append(total * inverse)
    return density, speeds


def collide(f, kind):
    density, u = moments(f)
    square = 1.0 - 1.5 * (u[0] * u[0] + u[1] * u[1] + u[2] * u[2])
    fluid = kind == 0
    inlet = kind == 2
    scaled = {w: (OMEGA * w) * density for w in (1.0 / 3.0, 1.0 / 18.0, 1.0 / 36.0)}
    fallback = {}
    post = [None] * 19
    for i in range(19):
        value = inflow_value(i)
        if value not in fallback:
            fallback[value] = jnp.where(inlet, value, BIG)
    for i in range(19):
        if post[i] is not None:
            continue
        w = scaled[WEIGHTS[i]]
        if i == 0:
            post[0] = jnp.where(fluid, (1.0 - OMEGA) * f[0] + w * square, fallback[inflow_value(0)])
            continue
        along = None
        for axis in range(3):
            if DIRS[i][axis] != 0:
                term = u[axis] if DIRS[i][axis] == 1 else -u[axis]
                along = term if along is None else along + term
        even = w * (square + 4.5 * along * along)
        odd = w * (3.0 * along)
        j = OPP[i]
        post[i] = jnp.where(fluid, (1.0 - OMEGA) * f[i] + (even + odd), fallback[inflow_value(i)])
        post[j] = jnp.where(fluid, (1.0 - OMEGA) * f[j] + (even - odd), fallback[inflow_value(j)])
    return post, u


def shifted(plane, i):
    _, north, upward = DIRS[i]
    if north:
        plane = pltpu.roll(plane, north % NY, 0)
    if upward:
        plane = pltpu.roll(plane, upward % NZ, 1)
    return plane


def first_kernel(
    pop,
    kind_ref,
    phase,
    order,
    table,
    modes,
    field,
    gram_out,
    cross_out,
    self_out,
    snaps_out,
    east,
    west,
    rest,
    speeds,
    samples,
    message,
    line,
    staging,
    picks,
    landed,
    gpart,
    slot_a,
    slot_b,
    rows_a,
    rows_b,
    cross_own,
    cross_a,
    cross_mid,
    cross_b,
    halo_send,
    halo_recv,
    line_send,
    line_recv,
    route_send,
    route_recv,
    ga_send,
    ga_recv,
    gb_send,
    gb_recv,
    gd_send,
    gd_recv,
    ca_send,
    ca_recv,
    cb_send,
    cb_recv,
):
    group = lax.axis_index("group")
    slab = lax.axis_index("slab")
    zpos = slab // NPLANE
    ppos = slab % NPLANE
    position = group * 128 + slab
    channel = group < 3
    has_west = jnp.logical_and(channel, position > 0)
    has_east = jnp.logical_and(channel, position < 383)
    west_id = ((position - 1) // 128, (position + 127) % 128)
    east_id = ((position + 1) // 128, (position + 1) % 128)

    barrier = pltpu.get_barrier_semaphore()

    def hello(target):
        pl.semaphore_signal(barrier, inc=1, device_id=target, device_id_type=MESH)

    def line_peer(d):
        return (group, ((zpos + d) % NLINE) * NPLANE + ppos)

    def greet_line(d, c):
        hello(line_peer(d))
        return c

    lax.fori_loop(1, NLINE, greet_line, 0)

    def gather_plane(post, x, store_slot):
        for n, i in enumerate(EAST):
            east[store_slot, x + 1, n] = post[i]
        for n, i in enumerate(WEST):
            west[store_slot, x + 1, n] = post[i]
        for n, i in enumerate(REST):
            rest[store_slot, x, n] = post[i]

    def streamed(slot, x):
        f = [None] * 19
        for n, i in enumerate(REST):
            if i == 0:
                f[0] = rest[slot, x, 0]
                continue
            source = shifted(rest[slot, x, n], i)
            f[i] = jnp.where(source >= 0.5 * BIG, rest[slot, x, REST.index(OPP[i])], source)
        for n, i in enumerate(EAST):
            source = shifted(east[slot, x, n], i)
            f[i] = jnp.where(source >= 0.5 * BIG, west[slot, x + 1, WEST.index(OPP[i])], source)
        for n, i in enumerate(WEST):
            source = shifted(west[slot, x + 2, n], i)
            f[i] = jnp.where(source >= 0.5 * BIG, east[slot, x + 1, EAST.index(OPP[i])], source)
        return f

    def keep_speeds(u, kind, x):
        for c in range(3):
            speeds[x, c] = jnp.where(kind == 1, 0.0, u[c])

    def halo(slot):
        go_east = pltpu.make_async_remote_copy(
            src_ref=east.at[slot, CX],
            dst_ref=east.at[slot, 0],
            send_sem=halo_send.at[slot, 0],
            recv_sem=halo_recv.at[slot, 0],
            device_id=east_id,
            device_id_type=MESH,
        )
        go_west = pltpu.make_async_remote_copy(
            src_ref=west.at[slot, 1],
            dst_ref=west.at[slot, CX + 1],
            send_sem=halo_send.at[slot, 1],
            recv_sem=halo_recv.at[slot, 1],
            device_id=west_id,
            device_id_type=MESH,
        )
        return go_east, go_west

    def send_halo(slot):
        go_east, go_west = halo(slot)

        @pl.when(has_east)
        def _():
            go_east.start()

        @pl.when(has_west)
        def _():
            go_west.start()

    def take_halo(slot):
        go_east, go_west = halo(slot)

        @pl.when(has_west)
        def _():
            go_east.wait_recv()

        @pl.when(has_east)
        def _():
            go_west.wait_recv()

    def first_plane(x):
        kind = kind_ref[x]
        post, _ = collide([pop[i, x] for i in range(19)], kind)
        gather_plane(post, x, 0)

    def middle_plane(slot, x):
        kind = kind_ref[x]
        f = streamed(slot, x)
        post, u = collide(f, kind)
        keep_speeds(u, kind, x)
        gather_plane(post, x, slot + 1)

    def last_plane(slot, x):
        kind = kind_ref[x]
        f = streamed(slot, x)
        _, u = moments(f)
        keep_speeds(u, kind, x)
        for i in range(19):
            field[i, x] = jnp.where(kind == 1, pop[i, x], f[i])

    @pl.when(channel)
    def _():
        @pl.when(has_east)
        def _():
            hello(east_id)

        @pl.when(has_west)
        def _():
            hello(west_id)

        def greet_analysis(p, c):
            hello((3, zpos * NPLANE + p))
            return c

        lax.fori_loop(0, NPLANE, greet_analysis, 0)

        samples[...] = jnp.zeros((STEPS, 8, NZ), jnp.float32)

        @pl.when(position == 0)
        def _():
            east[:, 0] = jnp.full((STEPS, 5, NY, NZ), BIG, jnp.float32)

        @pl.when(position == 383)
        def _():
            west[:, CX + 1] = jnp.full((STEPS, 5, NY, NZ), BIG, jnp.float32)

        def edges_first(n, c):
            first_plane(3 * n)
            return c

        lax.fori_loop(0, 2, edges_first, 0)
        edge = jnp.logical_or(position == 0, position == 383)

        @pl.when(edge)
        def _():
            pl.semaphore_wait(barrier, 15 + 8 + 1)

        @pl.when(jnp.logical_not(edge))
        def _():
            pl.semaphore_wait(barrier, 15 + 8 + 2)

        send_halo(0)

        def inner_first(n, c):
            first_plane(1 + n)
            return c

        lax.fori_loop(0, 2, inner_first, 0)

        def pick(q, c):
            found = jnp.int32(-1)
            for z in range(NLINE):
                row = table[group * 128 + z * NPLANE + ppos]
                found = jnp.where(row == 24 * zpos + q, z, found)
            picks[q] = found
            return c

        lax.fori_loop(0, 24, pick, 0)

        lanes = lax.broadcasted_iota(jnp.int32, (NZ, NZ), 1)
        depth = lax.broadcasted_iota(jnp.int32, (NZ, NZ), 0)
        pick_z = (depth == phase[2] + SUB * (lanes % 32)).astype(jnp.float32)
        lane3 = lax.broadcasted_iota(jnp.int32, (3, NY, NZ), 2)
        row3 = lax.broadcasted_iota(jnp.int32, (3, NY, NZ), 1)
        pick_y = row3 == phase[1] + SUB * (lane3 // 32)

        def sample(step):
            plane = speeds[phase[0]].reshape(3 * NY, NZ)
            along = mm(plane, pick_z, ((1,), (0,))).reshape(3, NY, NZ)
            samples[step, 0:3] = jnp.sum(jnp.where(pick_y, along, 0.0), axis=1)

        def one_step(slot, c):
            def inner(n, c):
                middle_plane(slot, 1 + n)
                return c

            lax.fori_loop(0, 2, inner, 0)
            take_halo(slot)

            def edges(n, c):
                middle_plane(slot, 3 * n)
                return c

            lax.fori_loop(0, 2, edges, 0)
            send_halo(slot + 1)
            sample(slot)
            return c

        lax.fori_loop(0, STEPS - 1, one_step, 0)

        def inner_last(n, c):
            last_plane(STEPS - 1, 1 + n)
            return c

        lax.fori_loop(0, 2, inner_last, 0)
        take_halo(STEPS - 1)

        def edges_last(n, c):
            last_plane(STEPS - 1, 3 * n)
            return c

        lax.fori_loop(0, 2, edges_last, 0)
        sample(STEPS - 1)

        for k in range(STEPS):
            message[4 * k : 4 * k + 4] = samples[order[k], 0:4]
        line[zpos] = message[...]

        def send_line(d, c):
            pltpu.make_async_remote_copy(
                src_ref=message,
                dst_ref=line.at[zpos],
                send_sem=line_send,
                recv_sem=line_recv,
                device_id=line_peer(d),
                device_id_type=MESH,
            ).start()
            return c

        lax.fori_loop(1, NLINE, send_line, 0)
        pltpu.make_async_copy(line.at[0:15], line.at[0:15], line_recv).wait()

        def place(q, c):
            z = picks[q]
            block = line[jnp.maximum(z, 0)]
            staging[q] = jnp.where(z >= 0, block, 0.0)
            return c

        lax.fori_loop(0, 24, place, 0)

        def send_route(p, c):
            pltpu.make_async_remote_copy(
                src_ref=staging.at[pl.ds(3 * p, 3)],
                dst_ref=landed.at[group * NPLANE + ppos],
                send_sem=route_send,
                recv_sem=route_recv,
                device_id=(3, zpos * NPLANE + p),
                device_id_type=MESH,
            ).start()
            return c

        lax.fori_loop(0, NPLANE, send_route, 0)

        def sent(slot, c):
            go_east, go_west = halo(slot)

            @pl.when(has_east)
            def _():
                go_east.wait_send()

            @pl.when(has_west)
            def _():
                go_west.wait_send()

            return c

        lax.fori_loop(0, STEPS, sent, 0)
        pltpu.make_async_copy(line.at[0:15], line.at[0:15], line_send).wait()
        pltpu.make_async_copy(staging, staging, route_send).wait()

    @pl.when(jnp.logical_not(channel))
    def _():
        def greet_channel(n, c):
            hello((n // NPLANE, zpos * NPLANE + n % NPLANE))
            return c

        lax.fori_loop(0, 24, greet_channel, 0)

        def plane_peer(d):
            return (3, zpos * NPLANE + (ppos + d) % NPLANE)

        def greet_plane(d, c):
            hello(plane_peer(d))
            return c

        lax.fori_loop(1, NPLANE, greet_plane, 0)

        part = mm(modes[...], modes[...], ((0,), (0,)))
        gpart[...] = jnp.zeros((NLINE, 16, RANK), jnp.float32)
        for n in range(NLINE):
            count = min(16, MODES - 16 * n)
            gpart[n, 0:count, 0:MODES] = part[16 * n : 16 * n + count]
        pl.semaphore_wait(barrier, 15 + 24 + 7)

        slot_a[zpos] = gpart[zpos]

        def send_a(d, c):
            pltpu.make_async_remote_copy(
                src_ref=gpart.at[(zpos + d) % NLINE],
                dst_ref=slot_a.at[zpos],
                send_sem=ga_send,
                recv_sem=ga_recv,
                device_id=line_peer(d),
                device_id_type=MESH,
            ).start()
            return c

        lax.fori_loop(1, NLINE, send_a, 0)
        pltpu.make_async_copy(slot_a.at[0:15], slot_a.at[0:15], ga_recv).wait()
        rows_a[...] = jnp.sum(slot_a[...], axis=0)
        slot_b[ppos] = rows_a[...]

        def send_b(d, c):
            pltpu.make_async_remote_copy(
                src_ref=rows_a,
                dst_ref=slot_b.at[ppos],
                send_sem=gb_send,
                recv_sem=gb_recv,
                device_id=plane_peer(d),
                device_id_type=MESH,
            ).start()
            return c

        lax.fori_loop(1, NPLANE, send_b, 0)
        pltpu.make_async_copy(slot_b.at[0:7], slot_b.at[0:7], gb_recv).wait()
        rows_b[...] = jnp.sum(slot_b[...], axis=0)
        gram_out[zpos] = rows_b[...]

        def send_d(d, c):
            pltpu.make_async_remote_copy(
                src_ref=rows_b,
                dst_ref=gram_out.at[zpos],
                send_sem=gd_send,
                recv_sem=gd_recv,
                device_id=line_peer(d),
                device_id_type=MESH,
            ).start()
            return c

        lax.fori_loop(1, NLINE, send_d, 0)
        pltpu.make_async_copy(gram_out.at[0:15], gram_out.at[0:15], gd_recv).wait()

        pltpu.make_async_copy(landed, landed, route_recv).wait()
        total = landed[0]
        for n in range(1, 24):
            total = total + landed[n]
        snaps = jnp.concatenate(
            [
                jnp.concatenate([total[t, 4 * k + c : 4 * k + c + 1] for k in range(4)], axis=0)
                for t in range(3)
                for c in range(3)
            ],
            axis=1,
        )
        snaps_out[0:4] = snaps
        snaps_out[4:8] = jnp.zeros((4, ROWS_DEV), jnp.float32)
        whole = snaps_out[...]
        cross_own[0, :, 0:MODES] = mm(whole, modes[...], ((1,), (0,)))
        cross_own[0, :, MODES:RANK] = jnp.zeros((8, RANK - MODES), jnp.float32)
        cross_own[1] = jnp.zeros((8, RANK), jnp.float32)
        cross_own[1, :, 0:8] = mm(whole, whole, ((1,), (1,)))
        cross_a[zpos] = cross_own[...]

        def send_ca(d, c):
            pltpu.make_async_remote_copy(
                src_ref=cross_own,
                dst_ref=cross_a.at[zpos],
                send_sem=ca_send,
                recv_sem=ca_recv,
                device_id=line_peer(d),
                device_id_type=MESH,
            ).start()
            return c

        lax.fori_loop(1, NLINE, send_ca, 0)
        pltpu.make_async_copy(cross_a.at[0:15], cross_a.at[0:15], ca_recv).wait()
        cross_mid[...] = jnp.sum(cross_a[...], axis=0)
        cross_b[ppos] = cross_mid[...]

        def send_cb(d, c):
            pltpu.make_async_remote_copy(
                src_ref=cross_mid,
                dst_ref=cross_b.at[ppos],
                send_sem=cb_send,
                recv_sem=cb_recv,
                device_id=plane_peer(d),
                device_id_type=MESH,
            ).start()
            return c

        lax.fori_loop(1, NPLANE, send_cb, 0)
        pltpu.make_async_copy(cross_b.at[0:7], cross_b.at[0:7], cb_recv).wait()
        both = jnp.sum(cross_b[...], axis=0)
        cross_out[...] = both[0]
        self_out[...] = both[1]

        pltpu.make_async_copy(slot_a.at[0:15], slot_a.at[0:15], ga_send).wait()
        pltpu.make_async_copy(slot_b.at[0:7], slot_b.at[0:7], gb_send).wait()
        pltpu.make_async_copy(gram_out.at[0:15], gram_out.at[0:15], gd_send).wait()
        pltpu.make_async_copy(cross_a.at[0:15], cross_a.at[0:15], ca_send).wait()
        pltpu.make_async_copy(cross_b.at[0:7], cross_b.at[0:7], cb_send).wait()


def lower_half(error, row, col):
    return jnp.where(row > col, error, jnp.where(row == col, 0.5 * error, 0.0))


def second_kernel(field, modes, gram, cross, self_ref, snaps, lattice, basis, scaled, inverse, left, pivots):
    group = lax.axis_index("group")

    @pl.when(group < 3)
    def _():
        lattice[...] = field[...]
        basis[...] = jnp.zeros((ROWS_DEV, RANK), jnp.float32)

    @pl.when(group == 3)
    def _():
        lattice[...] = jnp.zeros((19, CX, NY, NZ), jnp.float32)
        row = lax.broadcasted_iota(jnp.int32, (RANK, RANK), 0)
        col = lax.broadcasted_iota(jnp.int32, (RANK, RANK), 1)
        eye = (row == col).astype(jnp.float32)
        pad = jnp.logical_and(row == col, row >= MODES)
        whole = jnp.where(pad, 1.0, gram[...].reshape(RANK, RANK))
        diagonal = jnp.where(row == col, whole, 0.0)
        rs_row = 1.0 / jnp.sqrt(jnp.sum(diagonal, axis=0, keepdims=True))
        rs_col = 1.0 / jnp.sqrt(jnp.sum(diagonal, axis=1, keepdims=True))
        scaled[...] = whole * rs_row * rs_col
        inverse[...] = eye - lower_half(scaled[...] - eye, row, col)

        def go_on(state):
            count, size = state
            return jnp.logical_and(count < 6, jnp.logical_not(size < 1e-6))

        def newton(state):
            count, _ = state
            here = inverse[...]
            error = mm(mm(here, scaled[...], ((1,), (0,))), here, ((1,), (1,))) - eye
            inverse[...] = here - mm(lower_half(error, row, col), here, ((1,), (0,)))
            return count + 1, jnp.sum(error * error)

        _, size = lax.while_loop(go_on, newton, (jnp.int32(0), jnp.float32(1.0)))

        @pl.when(jnp.logical_not(size < 1e-6))
        def _():
            left[...] = scaled[...]
            inverse[...] = eye
            pivots[...] = jnp.ones((RANK, 128), jnp.float32)

            def eliminate(j, c):
                line = left[pl.ds(j, 1), :]
                mine = inverse[pl.ds(j, 1), :]
                lane = lax.broadcasted_iota(jnp.int32, (1, RANK), 1)
                pivot = jnp.sum(jnp.where(lane == j, line, 0.0), axis=1, keepdims=True)
                column = jnp.sum(jnp.where(col == j, left[...], 0.0), axis=1, keepdims=True)
                below = lax.broadcasted_iota(jnp.int32, (RANK, 1), 0) > j
                factor = jnp.where(below, column / pivot, 0.0)
                left[...] = left[...] - factor * line
                inverse[...] = inverse[...] - factor * mine
                pivots[pl.ds(j, 1), :] = jnp.broadcast_to(pivot, (1, 128))
                return c

            lax.fori_loop(0, RANK, eliminate, 0)
            inverse[...] = inverse[...] / jnp.sqrt(pivots[:, 0:1])

        factor = inverse[...] * rs_row
        tail = mm(cross[...], factor, ((1,), (1,)))
        rest = self_ref[:, 0:8] - mm(tail, tail, ((1,), (1,)))
        lane = lax.broadcasted_iota(jnp.int32, (8, RANK), 1)
        sub = lax.broadcasted_iota(jnp.int32, (8, RANK), 0)
        unit = (lane == MODES + sub).astype(jnp.float32)
        right = unit - mm(tail, factor, ((1,), (0,)))
        entry = [[rest[i : i + 1, j : j + 1] for j in range(4)] for i in range(4)]
        low = [[None] * 4 for _ in range(4)]
        lines = []
        for i in range(4):
            for j in range(i + 1):
                value = entry[i][j]
                for k in range(j):
                    value = value - low[i][k] * low[j][k]
                low[i][j] = jnp.sqrt(value) if i == j else value / low[j][j]
            line = right[i : i + 1]
            for k in range(i):
                line = line - low[i][k] * lines[k]
            lines.append(line / low[i][i])
        inverse[...] = factor
        inverse[MODES:RANK] = jnp.concatenate(lines, axis=0)
        scale = math.sqrt(128 * ROWS_DEV)
        final = inverse[...] * scale
        first = final[:, 0:MODES]
        second = jnp.concatenate([final[MODES:RANK, MODES:RANK], jnp.zeros((4, 4), jnp.float32)], axis=0)
        second = jnp.concatenate([second, jnp.zeros((8, 4), jnp.float32)], axis=1)
        placed = mm(second, unit[:, 128:RANK], ((0,), (0,)))

        for n in range(9):
            block = pl.ds(128 * n, 128)
            out = mm(modes[block, :], first, ((1,), (1,)))
            mine = snaps[:, 128 * n : 128 * (n + 1)]
            basis[block, 0:128] = out[:, 0:128]
            basis[block, 128:RANK] = out[:, 128:RANK] + mm(mine, placed, ((0,), (0,)))


def local(populations, cell_kind, snapshot_order, sample_phase, slab_map, weighted_modes):
    f32 = jnp.float32
    vmem = pl.BlockSpec(memory_space=pltpu.VMEM)
    smem = pl.BlockSpec(memory_space=pltpu.SMEM)
    dma = pltpu.SemaphoreType.DMA
    field, gram, cross, own, snaps = pl.pallas_call(
        first_kernel,
        out_shape=(
            jax.ShapeDtypeStruct((19, CX, NY, NZ), f32),
            jax.ShapeDtypeStruct((NLINE, 16, RANK), f32),
            jax.ShapeDtypeStruct((8, RANK), f32),
            jax.ShapeDtypeStruct((8, RANK), f32),
            jax.ShapeDtypeStruct((8, ROWS_DEV), f32),
        ),
        in_specs=[vmem, vmem, smem, smem, smem, vmem],
        out_specs=(vmem,) * 5,
        scratch_shapes=[
            pltpu.VMEM((STEPS, CX + 2, 5, NY, NZ), f32),
            pltpu.VMEM((STEPS, CX + 2, 5, NY, NZ), f32),
            pltpu.VMEM((STEPS, CX, 9, NY, NZ), f32),
            pltpu.VMEM((CX, 3, NY, NZ), f32),
            pltpu.VMEM((STEPS, 8, NZ), f32),
            pltpu.VMEM((16, NZ), f32),
            pltpu.VMEM((NLINE, 16, NZ), f32),
            pltpu.VMEM((24, 16, NZ), f32),
            pltpu.SMEM((24,), jnp.int32),
            pltpu.VMEM((24, 3, 16, NZ), f32),
            pltpu.VMEM((NLINE, 16, RANK), f32),
            pltpu.VMEM((NLINE, 16, RANK), f32),
            pltpu.VMEM((NPLANE, 16, RANK), f32),
            pltpu.VMEM((16, RANK), f32),
            pltpu.VMEM((16, RANK), f32),
            pltpu.VMEM((2, 8, RANK), f32),
            pltpu.VMEM((NLINE, 2, 8, RANK), f32),
            pltpu.VMEM((2, 8, RANK), f32),
            pltpu.VMEM((NPLANE, 2, 8, RANK), f32),
            dma((STEPS, 2)),
            dma((STEPS, 2)),
        ]
        + [dma] * 14,
        compiler_params=pltpu.CompilerParams(
            collective_id=0, has_side_effects=True, vmem_limit_bytes=32 * 1024 * 1024
        ),
    )(populations, cell_kind, sample_phase, snapshot_order, slab_map, weighted_modes)
    return pl.pallas_call(
        second_kernel,
        out_shape=(
            jax.ShapeDtypeStruct((19, CX, NY, NZ), f32),
            jax.ShapeDtypeStruct((ROWS_DEV, RANK), f32),
        ),
        in_specs=[vmem] * 6,
        out_specs=(vmem, vmem),
        scratch_shapes=[
            pltpu.VMEM((RANK, RANK), f32),
            pltpu.VMEM((RANK, RANK), f32),
            pltpu.VMEM((RANK, RANK), f32),
            pltpu.VMEM((RANK, 128), f32),
        ],
        compiler_params=pltpu.CompilerParams(vmem_limit_bytes=32 * 1024 * 1024),
    )(field, weighted_modes, gram, cross, own, snaps)


def solution(mesh):
    return jax.shard_map(
        local,
        mesh=mesh,
        in_specs=(
            P(None, ("group", "slab"), None, None),
            P(("group", "slab"), None, None),
            P(),
            P(),
            P(),
            P(("group", "slab"), None),
        ),
        out_specs=(P(None, ("group", "slab"), None, None), P(("group", "slab"), None)),
        check_vma=False,
    )
```

```python
import functools
import math

import jax
import jax.numpy as jnp
from jax import lax
from jax.experimental import pallas as pl
from jax.experimental.pallas import tpu as pltpu
from jax.sharding import PartitionSpec as P

MESH = pl.DeviceIdType.MESH
STEPS = 4
SUB = 4
OMEGA = 0.9
INLET = 0.05
BIG = 1e30

DIRS = [
    (0, 0, 0),
    (1, 0, 0),
    (-1, 0, 0),
    (0, 1, 0),
    (0, -1, 0),
    (0, 0, 1),
    (0, 0, -1),
    (1, 1, 0),
    (-1, -1, 0),
    (1, -1, 0),
    (-1, 1, 0),
    (1, 0, 1),
    (-1, 0, -1),
    (1, 0, -1),
    (-1, 0, 1),
    (0, 1, 1),
    (0, -1, -1),
    (0, 1, -1),
    (0, -1, 1),
]
WEIGHTS = [1.0 / 3.0] + [1.0 / 18.0] * 6 + [1.0 / 36.0] * 12
OPP = [0, 2, 1, 4, 3, 6, 5, 8, 7, 10, 9, 12, 11, 14, 13, 16, 15, 18, 17]
EAST = [i for i in range(19) if DIRS[i][0] == 1]
WEST = [i for i in range(19) if DIRS[i][0] == -1]
REST = [i for i in range(19) if DIRS[i][0] == 0]

CX, NY, NZ = 4, 16, 128
NLINE = 16
NPLANE = 8
RANK = 256
MODES = 252
ROWS_DEV = 1152
ROWS_ALL = 128 * ROWS_DEV
SCALE = math.sqrt(ROWS_ALL)
NEWTON = 3
ROOM = 60 * 1024 * 1024
LINE_FAR = [8, 7, 9, 6, 10, 5, 11, 4, 12, 3, 13, 2, 14, 1, 15]
PLANE_FAR = [4, 5, 3, 6, 2, 7, 1]


def mm(a, b, dims):
    return lax.dot_general(
        a,
        b,
        (dims, ((), ())),
        precision=lax.Precision.HIGHEST,
        preferred_element_type=jnp.float32,
    )


def inflow_value(i):
    along = DIRS[i][0] * INLET
    return WEIGHTS[i] * (1.0 + 3.0 * along + 4.5 * along * along - 1.5 * INLET * INLET)


def moments(f):
    density = f[0]
    for i in range(1, 19):
        density = density + f[i]
    inverse = 1.0 / density
    speeds = []
    for axis in range(3):
        plus = [f[i] for i in range(19) if DIRS[i][axis] == 1]
        minus = [f[i] for i in range(19) if DIRS[i][axis] == -1]
        total = functools.reduce(lambda a, b: a + b, [a - b for a, b in zip(plus, minus)])
        speeds.append(total * inverse)
    return density, speeds


def collide(f, kind):
    density, u = moments(f)
    square = 1.0 - 1.5 * (u[0] * u[0] + u[1] * u[1] + u[2] * u[2])
    fluid = kind == 0
    inlet = kind == 2
    scaled = {w: (OMEGA * w) * density for w in (1.0 / 3.0, 1.0 / 18.0, 1.0 / 36.0)}
    fallback = {}
    post = [None] * 19
    for i in range(19):
        value = inflow_value(i)
        if value not in fallback:
            fallback[value] = jnp.where(inlet, value, BIG)
    for i in range(19):
        if post[i] is not None:
            continue
        w = scaled[WEIGHTS[i]]
        if i == 0:
            post[0] = jnp.where(fluid, (1.0 - OMEGA) * f[0] + w * square, fallback[inflow_value(0)])
            continue
        along = None
        for axis in range(3):
            if DIRS[i][axis] != 0:
                term = u[axis] if DIRS[i][axis] == 1 else -u[axis]
                along = term if along is None else along + term
        even = w * (square + 4.5 * along * along)
        odd = w * (3.0 * along)
        j = OPP[i]
        post[i] = jnp.where(fluid, (1.0 - OMEGA) * f[i] + (even + odd), fallback[inflow_value(i)])
        post[j] = jnp.where(fluid, (1.0 - OMEGA) * f[j] + (even - odd), fallback[inflow_value(j)])
    return post, u


def shifted(plane, i):
    _, north, upward = DIRS[i]
    if north:
        plane = pltpu.roll(plane, north % NY, 0)
    if upward:
        plane = pltpu.roll(plane, upward % NZ, 1)
    return plane


def lower_half(error, row, col):
    return jnp.where(row > col, error, jnp.where(row == col, 0.5 * error, 0.0))


def square_iota():
    row = lax.broadcasted_iota(jnp.int32, (RANK, RANK), 0)
    col = lax.broadcasted_iota(jnp.int32, (RANK, RANK), 1)
    return row, col, (row == col).astype(jnp.float32)


def unit_diagonal(gram):
    row, col, _ = square_iota()
    whole = jnp.where(jnp.logical_and(row == col, row >= MODES), 1.0, gram)
    diagonal = jnp.where(row == col, whole, 0.0)
    along_row = jnp.sum(diagonal, axis=0, keepdims=True)
    rs_row = 1.0 / jnp.sqrt(along_row)
    rs_col = 1.0 / jnp.sqrt(jnp.sum(diagonal, axis=1, keepdims=True))
    return whole * rs_row * rs_col, rs_row, along_row


def last_columns(lines, is_step):
    lane = lax.broadcasted_iota(jnp.int32, (1, RANK), 1)
    old = [jnp.where(lane < MODES, line, 0.0) for line in lines]
    gram = [[None] * 4 for _ in range(4)]
    for s in range(4):
        for t in range(s + 1):
            own = jnp.where(lane == MODES + t, lines[s], 0.0)
            gram[s][t] = jnp.sum(own - old[s] * old[t] * (1.0 / ROWS_ALL), axis=1, keepdims=True)
            gram[t][s] = gram[s][t]

    def chosen(k, values):
        result = values[3]
        for s in range(3):
            result = jnp.where(is_step(k, s), values[s], result)
        return result

    half = [[chosen(k, [gram[s][t] for s in range(4)]) for t in range(4)] for k in range(4)]
    entry = [[chosen(j, half[k]) for j in range(k + 1)] for k in range(4)]
    start = []
    for s in range(4):
        start.append(SCALE * (lane == MODES + s).astype(jnp.float32) - old[s] * (SCALE / ROWS_ALL))
    low = [[None] * 4 for _ in range(4)]
    result = []
    for k in range(4):
        for j in range(k + 1):
            value = entry[k][j]
            for m in range(j):
                value = value - low[k][m] * low[j][m]
            low[k][j] = jnp.sqrt(value) if k == j else value / low[j][j]
        line = chosen(k, start)
        for m in range(k):
            line = line - low[k][m] * result[m]
        result.append(line / low[k][k])
    return result


def first_kernel(
    pop_hbm,
    kind_hbm,
    phase_hbm,
    order_hbm,
    table_hbm,
    modes_hbm,
    field_hbm,
    gram_hbm,
    q_hbm,
    small_hbm,
    field,
    gram,
    q,
    small,
    pop,
    kind_ref,
    phase,
    order,
    table,
    modes,
    east,
    west,
    rest,
    speeds,
    samples,
    early,
    line_a,
    line_b,
    staging_a,
    staging_b,
    picks,
    landed_a,
    landed_b,
    gpart,
    slot_a,
    slot_b,
    rows_a,
    rows_b,
    scaled,
    inverse,
    snaps,
    cross_own,
    cross_a,
    cross_mid,
    cross_b,
    load_sem,
    store_sem,
    halo_send,
    halo_recv,
    send_sem,
    recv_sem,
):
    group = lax.axis_index("group")
    slab = lax.axis_index("slab")
    zpos = slab // NPLANE
    ppos = slab % NPLANE
    position = group * 128 + slab
    channel = group < 3
    has_west = jnp.logical_and(channel, position > 0)
    has_east = jnp.logical_and(channel, position < 383)
    west_id = ((position - 1) // 128, (position + 127) % 128)
    east_id = ((position + 1) // 128, (position + 1) % 128)
    LINE_A, LINE_B, ROUTE_A, ROUTE_B, GRAM_A, GRAM_B, GRAM_D, CROSS_A, CROSS_B = range(9)

    barrier = pltpu.get_barrier_semaphore()

    def hello(target):
        pl.semaphore_signal(barrier, inc=1, device_id=target, device_id_type=MESH)

    loads = [
        pltpu.make_async_copy(a, b, load_sem.at[n])
        for n, (a, b) in enumerate(
            [
                (pop_hbm, pop),
                (kind_hbm, kind_ref),
                (phase_hbm, phase),
                (table_hbm, table),
                (order_hbm, order),
                (modes_hbm, modes),
            ]
        )
    ]

    stores = [
        pltpu.make_async_copy(a, b, store_sem.at[n])
        for n, (a, b) in enumerate(
            [
                (field, field_hbm),
                (gram, gram_hbm),
                (q.at[:, 0:128], q_hbm.at[:, 0:128]),
                (q.at[:, 128:RANK], q_hbm.at[:, 128:RANK]),
                (small, small_hbm),
            ]
        )
    ]

    @pl.when(channel)
    def _():
        for n in range(4):
            loads[n].start()

    @pl.when(jnp.logical_not(channel))
    def _():
        loads[5].start()
        loads[4].start()

    def line_peer(d):
        return (group, ((zpos + d) % NLINE) * NPLANE + ppos)

    def plane_peer(d):
        return (3, zpos * NPLANE + (ppos + d) % NPLANE)

    def push(source, target, peer, n):
        pltpu.make_async_remote_copy(
            src_ref=source,
            dst_ref=target,
            send_sem=send_sem.at[n],
            recv_sem=recv_sem.at[n],
            device_id=peer,
            device_id_type=MESH,
        ).start()

    def to_line(source, target, n):
        for d in LINE_FAR:
            push(source, target, line_peer(d), n)

    def to_plane(source, target, n):
        for d in PLANE_FAR:
            push(source, target, plane_peer(d), n)

    def arrived(ref, n):
        pltpu.make_async_copy(ref, ref, recv_sem.at[n]).wait()

    def left_here(ref, n):
        pltpu.make_async_copy(ref, ref, send_sem.at[n]).wait()

    for d in LINE_FAR:
        hello(line_peer(d))

    def keep_post(post, x, slot):
        for n, i in enumerate(EAST):
            east[slot, x + 1, n] = post[i]
        for n, i in enumerate(WEST):
            west[slot, x + 1, n] = post[i]
        for n, i in enumerate(REST):
            rest[slot, x, n] = post[i]

    def streamed(slot, x):
        f = [None] * 19
        for n, i in enumerate(REST):
            if i == 0:
                f[0] = rest[slot, x, 0]
                continue
            source = shifted(rest[slot, x, n], i)
            f[i] = jnp.where(source >= 0.5 * BIG, rest[slot, x, REST.index(OPP[i])], source)
        for n, i in enumerate(EAST):
            source = shifted(east[slot, x, n], i)
            f[i] = jnp.where(source >= 0.5 * BIG, west[slot, x + 1, WEST.index(OPP[i])], source)
        for n, i in enumerate(WEST):
            source = shifted(west[slot, x + 2, n], i)
            f[i] = jnp.where(source >= 0.5 * BIG, east[slot, x + 1, EAST.index(OPP[i])], source)
        return f

    def keep_speeds(u, kind, x):
        for c in range(3):
            speeds[x, c] = jnp.where(kind == 1, 0.0, u[c])

    def halo(slot):
        go_east = pltpu.make_async_remote_copy(
            src_ref=east.at[slot, CX],
            dst_ref=east.at[slot, 0],
            send_sem=halo_send.at[slot, 0],
            recv_sem=halo_recv.at[slot, 0],
            device_id=east_id,
            device_id_type=MESH,
        )
        go_west = pltpu.make_async_remote_copy(
            src_ref=west.at[slot, 1],
            dst_ref=west.at[slot, CX + 1],
            send_sem=halo_send.at[slot, 1],
            recv_sem=halo_recv.at[slot, 1],
            device_id=west_id,
            device_id_type=MESH,
        )
        return go_east, go_west

    def send_halo(slot):
        go_east, go_west = halo(slot)
        odd = slab % 2 == 1

        @pl.when(jnp.logical_and(has_east, odd))
        def _():
            go_east.start()

        @pl.when(has_west)
        def _():
            go_west.start()

        @pl.when(jnp.logical_and(has_east, jnp.logical_not(odd)))
        def _():
            go_east.start()

    def take_halo(slot):
        go_east, go_west = halo(slot)

        @pl.when(has_west)
        def _():
            go_east.wait_recv()

        @pl.when(has_east)
        def _():
            go_west.wait_recv()

    def first_plane(x):
        post, _ = collide([pop[i, x] for i in range(19)], kind_ref[x])
        keep_post(post, x, 0)

    def middle_plane(slot, x):
        kind = kind_ref[x]
        post, u = collide(streamed(slot, x), kind)
        keep_speeds(u, kind, x)
        keep_post(post, x, slot + 1)

    def last_plane(slot, x):
        kind = kind_ref[x]
        f = streamed(slot, x)
        _, u = moments(f)
        keep_speeds(u, kind, x)
        for i in range(19):
            field[i, x] = jnp.where(kind == 1, pop[i, x], f[i])

    def pair(fn):
        def body(n, c):
            fn(n)
            return c

        lax.fori_loop(0, 2, body, 0)

    @pl.when(channel)
    def _():
        for p in range(NPLANE):
            hello((3, zpos * NPLANE + p))

        @pl.when(has_east)
        def _():
            hello(east_id)

        @pl.when(has_west)
        def _():
            hello(west_id)

        samples[...] = jnp.zeros((STEPS, 8, NZ), jnp.float32)
        early[...] = jnp.zeros((16, NZ), jnp.float32)
        staging_b[...] = jnp.zeros((NPLANE, 16, NZ), jnp.float32)

        @pl.when(position == 0)
        def _():
            east[:, 0] = jnp.full((STEPS, 5, NY, NZ), BIG, jnp.float32)

        @pl.when(position == 383)
        def _():
            west[:, CX + 1] = jnp.full((STEPS, 5, NY, NZ), BIG, jnp.float32)

        loads[0].wait()
        loads[1].wait()
        pair(lambda n: first_plane(3 * n))
        edge = jnp.logical_or(position == 0, position == 383)

        @pl.when(edge)
        def _():
            pl.semaphore_wait(barrier, 15 + 8 + 1)

        @pl.when(jnp.logical_not(edge))
        def _():
            pl.semaphore_wait(barrier, 15 + 8 + 2)

        send_halo(0)
        pair(lambda n: first_plane(1 + n))
        loads[2].wait()
        loads[3].wait()

        def pick(n, c):
            found = jnp.int32(-1)
            for z in range(NLINE):
                row = table[group * 128 + z * NPLANE + ppos]
                found = jnp.where(row == 24 * zpos + n, z, found)
            picks[n] = found
            return c

        lax.fori_loop(0, 24, pick, 0)

        lanes = lax.broadcasted_iota(jnp.int32, (NZ, NZ), 1)
        depth = lax.broadcasted_iota(jnp.int32, (NZ, NZ), 0)
        pick_z = (depth == phase[2] + SUB * (lanes % 32)).astype(jnp.float32)
        lane3 = lax.broadcasted_iota(jnp.int32, (3, NY, NZ), 2)
        row3 = lax.broadcasted_iota(jnp.int32, (3, NY, NZ), 1)
        pick_y = row3 == phase[1] + SUB * (lane3 // 32)

        def sample(step):
            plane = speeds[phase[0]].reshape(3 * NY, NZ)
            along = mm(plane, pick_z, ((1,), (0,))).reshape(3, NY, NZ)
            samples[step, 0:3] = jnp.sum(jnp.where(pick_y, along, 0.0), axis=1)

        def one_step(slot, c):
            pair(lambda n: middle_plane(slot, 1 + n))
            take_halo(slot)
            pair(lambda n: middle_plane(slot, 3 * n))
            send_halo(slot + 1)
            sample(slot)
            return c

        lax.fori_loop(0, STEPS - 1, one_step, 0)

        for s in range(3):
            early[4 * s : 4 * s + 4] = samples[s, 0:4]
        line_a[zpos] = early[...]
        to_line(early, line_a.at[zpos], LINE_A)
        pair(lambda n: last_plane(STEPS - 1, 1 + n))
        take_halo(STEPS - 1)
        pair(lambda n: last_plane(STEPS - 1, 3 * n))
        sample(STEPS - 1)
        line_b[zpos] = samples[3]
        to_line(samples.at[3], line_b.at[zpos], LINE_B)

        stores[0].start()
        arrived(line_a.at[0:15], LINE_A)

        def place_a(n, c):
            z = picks[n]
            staging_a[n] = jnp.where(z >= 0, line_a[jnp.maximum(z, 0)], 0.0)
            return c

        lax.fori_loop(0, 24, place_a, 0)
        for p in range(NPLANE):
            push(
                staging_a.at[3 * p : 3 * p + 3],
                landed_a.at[group * NPLANE + ppos],
                (3, zpos * NPLANE + p),
                ROUTE_A,
            )
        arrived(line_b.at[0:15], LINE_B)

        def place_b(p, c):
            for t in range(3):
                z = picks[3 * p + t]
                block = line_b[jnp.maximum(z, 0)]
                staging_b[p, 4 * t : 4 * t + 4] = jnp.where(z >= 0, block, 0.0)[0:4]
            return c

        lax.fori_loop(0, NPLANE, place_b, 0)
        for p in range(NPLANE):
            push(
                staging_b.at[p],
                landed_b.at[group * NPLANE + ppos],
                (3, zpos * NPLANE + p),
                ROUTE_B,
            )

        def sent(slot, c):
            go_east, go_west = halo(slot)

            @pl.when(has_east)
            def _():
                go_east.wait_send()

            @pl.when(has_west)
            def _():
                go_west.wait_send()

            return c

        lax.fori_loop(0, STEPS, sent, 0)
        left_here(line_a.at[0:15], LINE_A)
        left_here(line_b.at[0:15], LINE_B)
        left_here(staging_a, ROUTE_A)
        left_here(staging_b, ROUTE_B)
        stores[0].wait()

    @pl.when(jnp.logical_not(channel))
    def _():
        for n in range(24):
            hello((n // NPLANE, zpos * NPLANE + n % NPLANE))
        for d in PLANE_FAR:
            hello(plane_peer(d))

        loads[5].wait()
        part = mm(modes[...], modes[...], ((0,), (0,)))
        gpart[...] = jnp.zeros((NLINE, 16, RANK), jnp.float32)
        for n in range(NLINE):
            count = min(16, MODES - 16 * n)
            gpart[n, 0:count, 0:MODES] = part[16 * n : 16 * n + count]
        pl.semaphore_wait(barrier, 15 + 24 + 7)

        slot_a[zpos] = gpart[zpos]
        for d in LINE_FAR:
            push(gpart.at[(zpos + d) % NLINE], slot_a.at[zpos], line_peer(d), GRAM_A)
        arrived(slot_a.at[0:15], GRAM_A)
        rows_a[...] = jnp.sum(slot_a[...], axis=0)
        slot_b[ppos] = rows_a[...]
        to_plane(rows_a, slot_b.at[ppos], GRAM_B)
        arrived(slot_b.at[0:7], GRAM_B)
        rows_b[...] = jnp.sum(slot_b[...], axis=0)
        gram[zpos] = rows_b[...]
        to_line(rows_b, gram.at[zpos], GRAM_D)
        arrived(gram.at[0:15], GRAM_D)
        stores[1].start()

        row, col, eye = square_iota()
        matrix, rs_row, _ = unit_diagonal(gram[...].reshape(RANK, RANK))
        scaled[...] = matrix
        inverse[...] = eye - lower_half(matrix - eye, row, col)

        def newton(n, size):
            here = inverse[...]
            error = mm(mm(here, scaled[...], ((1,), (0,))), here, ((1,), (1,))) - eye
            inverse[...] = here - mm(lower_half(error, row, col), here, ((1,), (0,)))
            return jnp.sum(jnp.sum(error * error, axis=0, keepdims=True), axis=1, keepdims=True)

        size = lax.fori_loop(0, NEWTON, newton, jnp.ones((1, 1), jnp.float32))
        good = jnp.broadcast_to(size < 1e-6, (RANK, RANK))
        factor = jnp.where(good, inverse[...], eye) * rs_row
        inverse[...] = factor * SCALE
        q[...] = mm(modes[...], inverse[:, 0:MODES], ((1,), (1,)))
        stores[2].start()
        loads[4].wait()
        small[...] = jnp.zeros((4, 8, NZ), jnp.float32)
        small[0] = jnp.broadcast_to(size, (8, NZ))
        for k in range(4):
            small[0, k + 1 : k + 2] = jnp.full((1, NZ), 1.0, jnp.float32) * order[k].astype(jnp.float32)

        arrived(landed_a, ROUTE_A)
        total = landed_a[0]
        for n in range(1, 24):
            total = total + landed_a[n]
        where_to = lax.broadcasted_iota(jnp.int32, (16, NZ), 1)
        where_from = lax.broadcasted_iota(jnp.int32, (16, NZ), 0)
        for t in range(3):
            for c in range(3):
                n = 3 * t + c
                put = jnp.logical_and(where_from % 4 == c, where_to == 124 + where_from // 4)
                put = jnp.logical_and(put, where_from < 12).astype(jnp.float32)
                block = pl.ds(128 * n, 128)
                q[block, 128:RANK] = q[block, 128:RANK] + mm(total[t], put, ((0,), (0,)))
        snaps[...] = jnp.zeros((8, ROWS_DEV), jnp.float32)
        for t in range(3):
            for c in range(3):
                n = 3 * t + c
                for s in range(3):
                    snaps[s : s + 1, 128 * n : 128 * n + 128] = total[t, 4 * s + c : 4 * s + c + 1]
        product = mm(snaps[...], q[...], ((1,), (0,)))
        cross_own[0:3] = product[0:3, 0:128]
        cross_own[4:7] = product[0:3, 128:RANK]

        arrived(landed_b, ROUTE_B)
        final = landed_b[0]
        for n in range(1, 24):
            final = final + landed_b[n]
        tall = jnp.concatenate([final, jnp.zeros((NZ - 16, NZ), jnp.float32)], axis=0).T
        lane = lax.broadcasted_iota(jnp.int32, (NZ, NZ), 1)
        low_sum = jnp.zeros((8, NZ), jnp.float32)
        high_sum = jnp.zeros((8, NZ), jnp.float32)
        for t in range(3):
            for c in range(3):
                n = 3 * t + c
                block = pl.ds(128 * n, 128)
                column = jnp.broadcast_to(tall[:, 4 * t + c : 4 * t + c + 1], (NZ, NZ))
                high = jnp.where(lane == NZ - 1, column, q[block, 128:RANK])
                q[block, 128:RANK] = high
                low_sum = low_sum + jnp.sum((column * q[block, 0:128]).reshape(16, 8, NZ), axis=0)
                high_sum = high_sum + jnp.sum((column * high).reshape(16, 8, NZ), axis=0)
        cross_own[3:4] = jnp.sum(low_sum, axis=0, keepdims=True)
        cross_own[7:8] = jnp.sum(high_sum, axis=0, keepdims=True)

        cross_a[zpos] = cross_own[...]
        to_line(cross_own, cross_a.at[zpos], CROSS_A)
        stores[3].start()
        arrived(cross_a.at[0:15], CROSS_A)
        cross_mid[...] = jnp.sum(cross_a[...], axis=0)
        cross_b[ppos] = cross_mid[...]
        to_plane(cross_mid, cross_b.at[ppos], CROSS_B)
        arrived(cross_b.at[0:7], CROSS_B)
        both = jnp.sum(cross_b[...], axis=0)
        small[1] = both
        lines = [jnp.concatenate([both[s : s + 1], both[s + 4 : s + 5]], axis=1) for s in range(4)]
        for k, tail in enumerate(last_columns(lines, lambda k, s: order[k] == s)):
            small[2, k : k + 1] = tail[:, 0:128]
            small[3, k : k + 1] = tail[:, 128:RANK]
        stores[4].start()

        left_here(slot_a.at[0:15], GRAM_A)
        left_here(slot_b.at[0:7], GRAM_B)
        left_here(gram.at[0:15], GRAM_D)
        left_here(cross_a.at[0:15], CROSS_A)
        left_here(cross_b.at[0:7], CROSS_B)
        for n in range(1, 5):
            stores[n].wait()


def second_kernel(
    modes_hbm, field, gram_hbm, q_hbm, small_hbm, lattice, basis, passing, q, small, ends, blank, modes, gram, left, inverse, pivots, sem
):
    group = lax.axis_index("group")

    @pl.when(group < 3)
    def _():
        load = pltpu.make_async_copy(field, passing, sem.at[0])
        load.start()
        q[...] = jnp.zeros((ROWS_DEV, RANK), jnp.float32)
        clear = pltpu.make_async_copy(q, basis, sem.at[1])
        clear.start()
        load.wait()
        store = pltpu.make_async_copy(passing, lattice, sem.at[2])
        store.start()
        store.wait()
        clear.wait()

    @pl.when(group == 3)
    def _():
        load_q = pltpu.make_async_copy(q_hbm, q, sem.at[0])
        load_small = pltpu.make_async_copy(small_hbm, small, sem.at[1])
        load_q.start()
        load_small.start()
        blank[...] = jnp.zeros((CX, NY, NZ), jnp.float32)
        clears = [pltpu.make_async_copy(blank, lattice.at[n], sem.at[4 + n]) for n in range(19)]
        for clear in clears:
            clear.start()
        lane = lax.broadcasted_iota(jnp.int32, (ROWS_DEV, 128), 1)
        load_small.wait()
        load_q.wait()

        @pl.when(jnp.logical_not(small[0, 0, 0] < 1e-6))
        def _():
            load = pltpu.make_async_copy(modes_hbm, modes, sem.at[2])
            load.start()
            load_gram = pltpu.make_async_copy(gram_hbm, gram, sem.at[3])
            load_gram.start()
            load_gram.wait()
            row, col, eye = square_iota()
            matrix, rs_row, diagonal = unit_diagonal(gram[...].reshape(RANK, RANK))
            left[...] = matrix
            inverse[...] = eye
            pivots[...] = jnp.ones((RANK, 128), jnp.float32)

            def eliminate(j, c):
                line = left[pl.ds(j, 1), :]
                mine = inverse[pl.ds(j, 1), :]
                along = lax.broadcasted_iota(jnp.int32, (1, RANK), 1)
                pivot = jnp.sum(jnp.where(along == j, line, 0.0), axis=1, keepdims=True)
                column = jnp.sum(jnp.where(col == j, left[...], 0.0), axis=1, keepdims=True)
                below = lax.broadcasted_iota(jnp.int32, (RANK, 1), 0) > j
                factor = jnp.where(below, column / pivot, 0.0)
                left[...] = left[...] - factor * line
                inverse[...] = inverse[...] - factor * mine
                pivots[pl.ds(j, 1), :] = jnp.broadcast_to(pivot, (1, 128))
                return c

            lax.fori_loop(0, RANK, eliminate, 0)
            inverse[...] = inverse[...] / jnp.sqrt(pivots[:, 0:1]) * rs_row
            raw = jnp.concatenate([small[1, 0:4], small[1, 4:8]], axis=1)
            along = lax.broadcasted_iota(jnp.int32, (4, RANK), 1)
            old = jnp.where(along < MODES, raw * jnp.sqrt(diagonal), 0.0)
            old = jnp.concatenate([old, jnp.zeros((4, RANK), jnp.float32)], axis=0)
            fresh = mm(old, inverse[...], ((1,), (1,)))[0:4]
            fresh = jnp.where(along < MODES, fresh, raw)

            def is_step(k, s):
                return small[0, k + 1 : k + 2, 0:1] == float(s)

            rows = last_columns([fresh[s : s + 1] for s in range(4)], is_step)
            for k in range(4):
                small[2, k : k + 1] = rows[k][:, 0:128]
                small[3, k : k + 1] = rows[k][:, 128:RANK]
            load.wait()
            inverse[...] = inverse[...] * SCALE
            whole = mm(modes[...], inverse[:, 0:MODES], ((1,), (1,)))
            wide = lax.broadcasted_iota(jnp.int32, (ROWS_DEV, RANK), 1)
            q[...] = jnp.where(wide < MODES, whole, q[...])

        first = pltpu.make_async_copy(q.at[:, 0:128], basis.at[:, 0:128], sem.at[0])
        first.start()
        rows = jnp.concatenate([small[2, 0:4], small[3, 0:4]], axis=1)
        rows = jnp.concatenate([jnp.zeros((124, RANK), jnp.float32), rows], axis=0)
        ends[...] = jnp.where(lane < 124, q[:, 128:RANK], mm(q[...], rows, ((1,), (1,))))
        second = pltpu.make_async_copy(ends, basis.at[:, 128:RANK], sem.at[1])
        second.start()
        for clear in clears:
            clear.wait()
        first.wait()
        second.wait()


def local(populations, cell_kind, snapshot_order, sample_phase, slab_map, weighted_modes):
    f32 = jnp.float32
    hbm = pl.BlockSpec(memory_space=pltpu.HBM)
    dma = pltpu.SemaphoreType.DMA

    def buffer(*shape):
        return pltpu.VMEM(shape, f32)

    field, gram, q, small = pl.pallas_call(
        first_kernel,
        out_shape=(
            jax.ShapeDtypeStruct((19, CX, NY, NZ), f32),
            jax.ShapeDtypeStruct((NLINE, 16, RANK), f32),
            jax.ShapeDtypeStruct((ROWS_DEV, RANK), f32),
            jax.ShapeDtypeStruct((4, 8, NZ), f32),
        ),
        in_specs=[hbm] * 6,
        out_specs=(hbm,) * 4,
        scratch_shapes=[
            buffer(19, CX, NY, NZ),
            buffer(NLINE, 16, RANK),
            buffer(ROWS_DEV, RANK),
            buffer(4, 8, NZ),
            buffer(19, CX, NY, NZ),
            pltpu.VMEM((CX, NY, NZ), jnp.int32),
            pltpu.SMEM((3,), jnp.int32),
            pltpu.SMEM((4,), jnp.int32),
            pltpu.SMEM((384,), jnp.int32),
            buffer(ROWS_DEV, MODES),
            buffer(STEPS, CX + 2, 5, NY, NZ),
            buffer(STEPS, CX + 2, 5, NY, NZ),
            buffer(STEPS, CX, 9, NY, NZ),
            buffer(CX, 3, NY, NZ),
            buffer(STEPS, 8, NZ),
            buffer(16, NZ),
            buffer(NLINE, 16, NZ),
            buffer(NLINE, 8, NZ),
            buffer(24, 16, NZ),
            buffer(NPLANE, 16, NZ),
            pltpu.SMEM((24,), jnp.int32),
            buffer(24, 3, 16, NZ),
            buffer(24, 16, NZ),
            buffer(NLINE, 16, RANK),
            buffer(NLINE, 16, RANK),
            buffer(NPLANE, 16, RANK),
            buffer(16, RANK),
            buffer(16, RANK),
            buffer(RANK, RANK),
            buffer(RANK, RANK),
            buffer(8, ROWS_DEV),
            buffer(8, NZ),
            buffer(NLINE, 8, NZ),
            buffer(8, NZ),
            buffer(NPLANE, 8, NZ),
            dma((6,)),
            dma((5,)),
            dma((STEPS, 2)),
            dma((STEPS, 2)),
            dma((9,)),
            dma((9,)),
        ],
        compiler_params=pltpu.CompilerParams(
            collective_id=0, has_side_effects=True, vmem_limit_bytes=ROOM
        ),
    )(populations, cell_kind, sample_phase, snapshot_order, slab_map, weighted_modes)
    return pl.pallas_call(
        second_kernel,
        out_shape=(
            jax.ShapeDtypeStruct((19, CX, NY, NZ), f32),
            jax.ShapeDtypeStruct((ROWS_DEV, RANK), f32),
        ),
        in_specs=[hbm] * 5,
        out_specs=(hbm, hbm),
        scratch_shapes=[
            buffer(19, CX, NY, NZ),
            buffer(ROWS_DEV, RANK),
            buffer(4, 8, NZ),
            buffer(ROWS_DEV, 128),
            buffer(CX, NY, NZ),
            buffer(ROWS_DEV, MODES),
            buffer(NLINE, 16, RANK),
            buffer(RANK, RANK),
            buffer(RANK, RANK),
            buffer(RANK, 128),
            dma((4 + 19,)),
        ],
        compiler_params=pltpu.CompilerParams(vmem_limit_bytes=ROOM),
    )(weighted_modes, field, gram, q, small)


def solution(mesh):
    return jax.shard_map(
        local,
        mesh=mesh,
        in_specs=(
            P(None, ("group", "slab"), None, None),
            P(("group", "slab"), None, None),
            P(),
            P(),
            P(),
            P(("group", "slab"), None),
        ),
        out_specs=(P(None, ("group", "slab"), None, None), P(("group", "slab"), None)),
        check_vma=False,
    )
```

```python
import functools
import math

import jax
import jax.numpy as jnp
from jax import lax
from jax.experimental import pallas as pl
from jax.experimental.pallas import tpu as pltpu
from jax.sharding import PartitionSpec as P

MESH = pl.DeviceIdType.MESH
STEPS = 4
SUB = 4
OMEGA = 0.9
INLET = 0.05
BIG = 1e30

DIRS = [
    (0, 0, 0),
    (1, 0, 0),
    (-1, 0, 0),
    (0, 1, 0),
    (0, -1, 0),
    (0, 0, 1),
    (0, 0, -1),
    (1, 1, 0),
    (-1, -1, 0),
    (1, -1, 0),
    (-1, 1, 0),
    (1, 0, 1),
    (-1, 0, -1),
    (1, 0, -1),
    (-1, 0, 1),
    (0, 1, 1),
    (0, -1, -1),
    (0, 1, -1),
    (0, -1, 1),
]
WEIGHTS = [1.0 / 3.0] + [1.0 / 18.0] * 6 + [1.0 / 36.0] * 12
OPP = [0, 2, 1, 4, 3, 6, 5, 8, 7, 10, 9, 12, 11, 14, 13, 16, 15, 18, 17]
EAST = [i for i in range(19) if DIRS[i][0] == 1]
WEST = [i for i in range(19) if DIRS[i][0] == -1]
REST = [i for i in range(19) if DIRS[i][0] == 0]

CX, NY, NZ = 4, 16, 128
NLINE = 16
NPLANE = 8
RANK = 256
MODES = 252
ROWS_DEV = 1152
ROWS_ALL = 128 * ROWS_DEV
SCALE = math.sqrt(ROWS_ALL)
NEWTON = 3
ROOM = 60 * 1024 * 1024
LINE_FAR = [8, 7, 9, 6, 10, 5, 11, 4, 12, 3, 13, 2, 14, 1, 15]
PLANE_FAR = [4, 5, 3, 6, 2, 7, 1]


def mm(a, b, dims):
    return lax.dot_general(
        a,
        b,
        (dims, ((), ())),
        precision=lax.Precision.HIGHEST,
        preferred_element_type=jnp.float32,
    )


def inflow_value(i):
    along = DIRS[i][0] * INLET
    return WEIGHTS[i] * (1.0 + 3.0 * along + 4.5 * along * along - 1.5 * INLET * INLET)


def moments(f):
    density = f[0]
    for i in range(1, 19):
        density = density + f[i]
    inverse = 1.0 / density
    speeds = []
    for axis in range(3):
        plus = [f[i] for i in range(19) if DIRS[i][axis] == 1]
        minus = [f[i] for i in range(19) if DIRS[i][axis] == -1]
        total = functools.reduce(lambda a, b: a + b, [a - b for a, b in zip(plus, minus)])
        speeds.append(total * inverse)
    return density, speeds


def collide(f, kind):
    density, u = moments(f)
    square = 1.0 - 1.5 * (u[0] * u[0] + u[1] * u[1] + u[2] * u[2])
    fluid = kind == 0
    inlet = kind == 2
    scaled = {w: (OMEGA * w) * density for w in (1.0 / 3.0, 1.0 / 18.0, 1.0 / 36.0)}
    fallback = {}
    post = [None] * 19
    for i in range(19):
        value = inflow_value(i)
        if value not in fallback:
            fallback[value] = jnp.where(inlet, value, BIG)
    for i in range(19):
        if post[i] is not None:
            continue
        w = scaled[WEIGHTS[i]]
        if i == 0:
            post[0] = jnp.where(fluid, (1.0 - OMEGA) * f[0] + w * square, fallback[inflow_value(0)])
            continue
        along = None
        for axis in range(3):
            if DIRS[i][axis] != 0:
                term = u[axis] if DIRS[i][axis] == 1 else -u[axis]
                along = term if along is None else along + term
        even = w * (square + 4.5 * along * along)
        odd = w * (3.0 * along)
        j = OPP[i]
        post[i] = jnp.where(fluid, (1.0 - OMEGA) * f[i] + (even + odd), fallback[inflow_value(i)])
        post[j] = jnp.where(fluid, (1.0 - OMEGA) * f[j] + (even - odd), fallback[inflow_value(j)])
    return post, u


def shifted(plane, i):
    _, north, upward = DIRS[i]
    if north:
        plane = pltpu.roll(plane, north % NY, 0)
    if upward:
        plane = pltpu.roll(plane, upward % NZ, 1)
    return plane


def lower_half(error, row, col):
    return jnp.where(row > col, error, jnp.where(row == col, 0.5 * error, 0.0))


def square_iota():
    row = lax.broadcasted_iota(jnp.int32, (RANK, RANK), 0)
    col = lax.broadcasted_iota(jnp.int32, (RANK, RANK), 1)
    return row, col, (row == col).astype(jnp.float32)


def unit_diagonal(gram):
    row, col, _ = square_iota()
    whole = jnp.where(jnp.logical_and(row == col, row >= MODES), 1.0, gram)
    diagonal = jnp.where(row == col, whole, 0.0)
    along_row = jnp.sum(diagonal, axis=0, keepdims=True)
    rs_row = 1.0 / jnp.sqrt(along_row)
    rs_col = 1.0 / jnp.sqrt(jnp.sum(diagonal, axis=1, keepdims=True))
    return whole * rs_row * rs_col, rs_row, along_row


def last_columns(lines, is_step):
    lane = lax.broadcasted_iota(jnp.int32, (1, RANK), 1)
    old = [jnp.where(lane < MODES, line, 0.0) for line in lines]
    gram = [[None] * 4 for _ in range(4)]
    for s in range(4):
        for t in range(s + 1):
            own = jnp.where(lane == MODES + t, lines[s], 0.0)
            gram[s][t] = jnp.sum(own - old[s] * old[t] * (1.0 / ROWS_ALL), axis=1, keepdims=True)
            gram[t][s] = gram[s][t]

    def chosen(k, values):
        result = values[3]
        for s in range(3):
            result = jnp.where(is_step(k, s), values[s], result)
        return result

    half = [[chosen(k, [gram[s][t] for s in range(4)]) for t in range(4)] for k in range(4)]
    entry = [[chosen(j, half[k]) for j in range(k + 1)] for k in range(4)]
    start = []
    for s in range(4):
        start.append(SCALE * (lane == MODES + s).astype(jnp.float32) - old[s] * (SCALE / ROWS_ALL))
    low = [[None] * 4 for _ in range(4)]
    result = []
    for k in range(4):
        for j in range(k + 1):
            value = entry[k][j]
            for m in range(j):
                value = value - low[k][m] * low[j][m]
            low[k][j] = jnp.sqrt(value) if k == j else value / low[j][j]
        line = chosen(k, start)
        for m in range(k):
            line = line - low[k][m] * result[m]
        result.append(line / low[k][k])
    return result


def first_kernel(
    pop_hbm,
    kind_hbm,
    phase_hbm,
    order_hbm,
    table_hbm,
    modes_hbm,
    field_hbm,
    gram_hbm,
    q_hbm,
    small_hbm,
    field,
    gram,
    q,
    small,
    pop,
    kind_ref,
    phase,
    order,
    table,
    modes,
    east,
    west,
    rest,
    speeds,
    samples,
    early,
    final,
    picks,
    landed_a,
    landed_c,
    landed_b,
    ready_a,
    ready_c,
    ready_b,
    got_a,
    got_c,
    got_b,
    pack,
    slot_a,
    rows_a,
    slot_b,
    rows_b,
    column,
    square,
    scaled,
    inverse,
    snaps,
    cross_own,
    cross_a,
    cross_mid,
    cross_b,
    load_sem,
    store_sem,
    halo_send,
    halo_recv,
    send_sem,
    recv_sem,
):
    group = lax.axis_index("group")
    slab = lax.axis_index("slab")
    zpos = slab // NPLANE
    ppos = slab % NPLANE
    position = group * 128 + slab
    channel = group < 3
    has_west = jnp.logical_and(channel, position > 0)
    has_east = jnp.logical_and(channel, position < 383)
    west_id = ((position - 1) // 128, (position + 127) % 128)
    east_id = ((position + 1) // 128, (position + 1) % 128)
    ROUTE_A, ROUTE_C, ROUTE_B, LINE_A, LINE_C, LINE_B, GRAM_A, GRAM_B, GRAM_C, GRAM_D, CROSS_A, CROSS_B = range(12)
    odd = slab % 2

    barrier = pltpu.get_barrier_semaphore()

    def hello(target):
        pl.semaphore_signal(barrier, inc=1, device_id=target, device_id_type=MESH)

    loads = [
        pltpu.make_async_copy(a, b, load_sem.at[n])
        for n, (a, b) in enumerate(
            [
                (pop_hbm, pop),
                (kind_hbm, kind_ref),
                (phase_hbm, phase),
                (table_hbm, table),
                (order_hbm, order),
                (modes_hbm, modes),
            ]
        )
    ]

    stores = [
        pltpu.make_async_copy(a, b, store_sem.at[n])
        for n, (a, b) in enumerate(
            [
                (field, field_hbm),
                (square, gram_hbm),
                (q.at[:, 0:128], q_hbm.at[:, 0:128]),
                (q.at[:, 128:RANK], q_hbm.at[:, 128:RANK]),
                (small, small_hbm),
            ]
        )
    ]

    @pl.when(channel)
    def _():
        for n in range(3):
            loads[n].start()

    @pl.when(jnp.logical_not(channel))
    def _():
        loads[5].start()
        loads[4].start()
        loads[3].start()

    def line_peer(d):
        return (group, ((zpos + d) % NLINE) * NPLANE + ppos)

    def plane_peer(d):
        return (3, zpos * NPLANE + (ppos + d) % NPLANE)

    def push(source, target, peer, n):
        pltpu.make_async_remote_copy(
            src_ref=source,
            dst_ref=target,
            send_sem=send_sem.at[n],
            recv_sem=recv_sem.at[n],
            device_id=peer,
            device_id_type=MESH,
        ).start()

    def to_line(source, target, n):
        for d in LINE_FAR:
            push(source, target, line_peer(d), n)

    def to_plane(source, target, n):
        for d in PLANE_FAR:
            push(source, target, plane_peer(d), n)

    def arrived(ref, n):
        pltpu.make_async_copy(ref, ref, recv_sem.at[n]).wait()

    def left_here(ref, n):
        pltpu.make_async_copy(ref, ref, send_sem.at[n]).wait()

    def keep_post(post, x, slot):
        for n, i in enumerate(EAST):
            east[slot, x + 1, n] = post[i]
        for n, i in enumerate(WEST):
            west[slot, x + 1, n] = post[i]
        for n, i in enumerate(REST):
            rest[slot, x, n] = post[i]

    def streamed(slot, x):
        f = [None] * 19
        for n, i in enumerate(REST):
            if i == 0:
                f[0] = rest[slot, x, 0]
                continue
            source = shifted(rest[slot, x, n], i)
            f[i] = jnp.where(source >= 0.5 * BIG, rest[slot, x, REST.index(OPP[i])], source)
        for n, i in enumerate(EAST):
            source = shifted(east[slot, x, n], i)
            f[i] = jnp.where(source >= 0.5 * BIG, west[slot, x + 1, WEST.index(OPP[i])], source)
        for n, i in enumerate(WEST):
            source = shifted(west[slot, x + 2, n], i)
            f[i] = jnp.where(source >= 0.5 * BIG, east[slot, x + 1, EAST.index(OPP[i])], source)
        return f

    def keep_speeds(u, kind, x):
        for c in range(3):
            speeds[x, c] = jnp.where(kind == 1, 0.0, u[c])

    def halo(slot):
        go_east = pltpu.make_async_remote_copy(
            src_ref=east.at[slot, CX],
            dst_ref=east.at[slot, 0],
            send_sem=halo_send.at[slot, 0],
            recv_sem=halo_recv.at[slot, 0],
            device_id=east_id,
            device_id_type=MESH,
        )
        go_west = pltpu.make_async_remote_copy(
            src_ref=west.at[slot, 1],
            dst_ref=west.at[slot, CX + 1],
            send_sem=halo_send.at[slot, 1],
            recv_sem=halo_recv.at[slot, 1],
            device_id=west_id,
            device_id_type=MESH,
        )
        return go_east, go_west

    def send_side(slot, side):
        go_east, go_west = halo(slot)

        @pl.when(jnp.logical_and(has_east, side == 1))
        def _():
            go_east.start()

        @pl.when(jnp.logical_and(has_west, side == 0))
        def _():
            go_west.start()

    def take_side(slot, side):
        go_east, go_west = halo(slot)

        @pl.when(jnp.logical_and(has_east, side == 1))
        def _():
            go_west.wait_recv()

        @pl.when(jnp.logical_and(has_west, side == 0))
        def _():
            go_east.wait_recv()

    def sides(fn):
        def body(n, c):
            fn((odd + n) % 2)
            return c

        lax.fori_loop(0, 2, body, 0)

    def first_plane(x):
        post, _ = collide([pop[i, x] for i in range(19)], kind_ref[x])
        keep_post(post, x, 0)

    def middle_plane(slot, x):
        kind = kind_ref[x]
        post, u = collide(streamed(slot, x), kind)
        keep_speeds(u, kind, x)
        keep_post(post, x, slot + 1)

    def last_plane(slot, x):
        kind = kind_ref[x]
        f = streamed(slot, x)
        _, u = moments(f)
        keep_speeds(u, kind, x)
        for i in range(19):
            field[i, x] = jnp.where(kind == 1, pop[i, x], f[i])

    def pair(fn):
        def body(n, c):
            fn(n)
            return c

        lax.fori_loop(0, 2, body, 0)

    @pl.when(channel)
    def _():
        @pl.when(has_east)
        def _():
            hello(east_id)

        @pl.when(has_west)
        def _():
            hello(west_id)

        samples[...] = jnp.zeros((STEPS, 4, NZ), jnp.float32)

        @pl.when(position == 0)
        def _():
            east[:, 0] = jnp.full((STEPS, 5, NY, NZ), BIG, jnp.float32)

        @pl.when(position == 383)
        def _():
            west[:, CX + 1] = jnp.full((STEPS, 5, NY, NZ), BIG, jnp.float32)

        loads[0].wait()
        loads[1].wait()
        sides(lambda side: first_plane(3 * side))
        edge = jnp.logical_or(position == 0, position == 383)

        @pl.when(edge)
        def _():
            pl.semaphore_wait(barrier, 8 + 1)

        @pl.when(jnp.logical_not(edge))
        def _():
            pl.semaphore_wait(barrier, 8 + 2)

        sides(lambda side: send_side(0, side))
        pair(lambda n: first_plane(1 + n))
        loads[2].wait()

        lanes = lax.broadcasted_iota(jnp.int32, (NZ, NZ), 1)
        depth = lax.broadcasted_iota(jnp.int32, (NZ, NZ), 0)
        pick_z = (depth == phase[2] + SUB * (lanes % 32)).astype(jnp.float32)
        lane3 = lax.broadcasted_iota(jnp.int32, (3, NY, NZ), 2)
        row3 = lax.broadcasted_iota(jnp.int32, (3, NY, NZ), 1)
        pick_y = row3 == phase[1] + SUB * (lane3 // 32)

        def sample(step):
            plane = speeds[phase[0]].reshape(3 * NY, NZ)
            along = mm(plane, pick_z, ((1,), (0,))).reshape(3, NY, NZ)
            samples[step, 0:3] = jnp.sum(jnp.where(pick_y, along, 0.0), axis=1)

        def to_analysis(source, target, n):
            for d in [4, 5, 3, 6, 2, 7, 1, 0]:
                push(source, target.at[group * NPLANE + ppos], (3, zpos * NPLANE + (ppos + d) % NPLANE), n)

        def one_step(slot, c):
            pair(lambda n: middle_plane(slot, 1 + n))

            def one_side(side):
                take_side(slot, side)
                middle_plane(slot, 3 * side)
                send_side(slot + 1, side)

            sides(one_side)
            sample(slot)
            return c

        lax.fori_loop(0, 2, one_step, 0)
        to_analysis(samples.at[0:2], landed_a, ROUTE_A)
        one_step(2, 0)
        to_analysis(samples.at[2], landed_c, ROUTE_C)
        pair(lambda n: last_plane(STEPS - 1, 1 + n))

        def last_side(side):
            take_side(STEPS - 1, side)
            last_plane(STEPS - 1, 3 * side)

        sides(last_side)
        sample(STEPS - 1)
        to_analysis(samples.at[3], landed_b, ROUTE_B)
        stores[0].start()

        def sent(slot, c):
            go_east, go_west = halo(slot)

            @pl.when(has_east)
            def _():
                go_east.wait_send()

            @pl.when(has_west)
            def _():
                go_west.wait_send()

            return c

        lax.fori_loop(0, STEPS, sent, 0)
        left_here(landed_a.at[0:8], ROUTE_A)
        left_here(landed_c.at[0:8], ROUTE_C)
        left_here(landed_b.at[0:8], ROUTE_B)
        stores[0].wait()

    @pl.when(jnp.logical_not(channel))
    def _():
        for n in range(24):
            hello((n // NPLANE, zpos * NPLANE + n % NPLANE))
        for d in LINE_FAR:
            hello(line_peer(d))
        for d in PLANE_FAR:
            hello(plane_peer(d))

        square[...] = jnp.zeros((RANK, RANK), jnp.float32)
        loads[5].wait()
        square[0:MODES, 0:MODES] = mm(modes[...], modes[...], ((0,), (0,)))
        for p in range(NPLANE):
            for z in range(NLINE):
                down, across = 32 * p + 4 * (z // 2), 128 * (z % 2)
                pack[p, z] = square[down : down + 4, across : across + 128]
        pl.semaphore_wait(barrier, 15 + 7)

        slot_a[ppos] = pack[ppos]
        for d in PLANE_FAR:
            push(pack.at[(ppos + d) % NPLANE], slot_a.at[ppos], plane_peer(d), GRAM_A)

        loads[3].wait()

        def pick(n, c):
            found = jnp.int32(-1)
            wanted = 24 * (n // 3) + 3 * ppos + n % 3
            for g in range(3):
                for p in range(NPLANE):
                    row = table[g * 128 + zpos * NPLANE + p]
                    found = jnp.where(row == wanted, g * NPLANE + p, found)
            picks[n] = found
            return c

        lax.fori_loop(0, 48, pick, 0)

        def forward(landed, ready, got, from_sem, to_sem):
            arrived(landed, from_sem)

            def place(n, c):
                source = picks[n]
                ready[n] = jnp.where(source >= 0, landed[jnp.maximum(source, 0)], 0.0)
                return c

            lax.fori_loop(0, 48, place, 0)
            got[zpos] = ready[pl.ds(3 * zpos, 3)]
            for d in LINE_FAR:
                push(ready.at[pl.ds(3 * ((zpos + d) % NLINE), 3)], got.at[zpos], line_peer(d), to_sem)

        arrived(slot_a.at[0:7], GRAM_A)
        rows_a[...] = jnp.sum(slot_a[...], axis=0)
        slot_b[zpos] = rows_a[zpos]
        for d in LINE_FAR:
            push(rows_a.at[(zpos + d) % NLINE], slot_b.at[zpos], line_peer(d), GRAM_B)
        arrived(slot_b.at[0:15], GRAM_B)
        rows_b[...] = jnp.sum(slot_b[...], axis=0)
        column[zpos] = rows_b[...]
        to_line(rows_b, column.at[zpos], GRAM_C)
        forward(landed_a, ready_a, got_a, ROUTE_A, LINE_A)
        arrived(column.at[0:15], GRAM_C)
        gram[ppos] = column[...]
        to_plane(column, gram.at[ppos], GRAM_D)
        forward(landed_c, ready_c, got_c, ROUTE_C, LINE_C)
        arrived(gram.at[0:7], GRAM_D)
        forward(landed_b, ready_b, got_b, ROUTE_B, LINE_B)
        for p in range(NPLANE):
            for z in range(NLINE):
                down, across = 32 * p + 4 * (z // 2), 128 * (z % 2)
                square[down : down + 4, across : across + 128] = gram[p, z]
        stores[1].start()

        row, col, eye = square_iota()
        matrix, rs_row, _ = unit_diagonal(square[...])
        scaled[...] = matrix
        inverse[...] = eye - lower_half(matrix - eye, row, col)

        def newton(n, size):
            here = inverse[...]
            error = mm(mm(here, scaled[...], ((1,), (0,))), here, ((1,), (1,))) - eye
            inverse[...] = here - mm(lower_half(error, row, col), here, ((1,), (0,)))
            return jnp.sum(jnp.sum(error * error, axis=0, keepdims=True), axis=1, keepdims=True)

        size = lax.fori_loop(0, NEWTON, newton, jnp.ones((1, 1), jnp.float32))
        good = jnp.broadcast_to(size < 1e-6, (RANK, RANK))
        factor = jnp.where(good, inverse[...], eye) * rs_row
        inverse[...] = factor * SCALE
        q[...] = mm(modes[...], inverse[:, 0:MODES], ((1,), (1,)))
        stores[2].start()
        loads[4].wait()
        small[...] = jnp.zeros((4, 8, NZ), jnp.float32)
        small[0] = jnp.broadcast_to(size, (8, NZ))
        for k in range(4):
            small[0, k + 1 : k + 2] = jnp.full((1, NZ), 1.0, jnp.float32) * order[k].astype(jnp.float32)

        arrived(got_a.at[0:15], LINE_A)
        arrived(got_c.at[0:15], LINE_C)
        sum_a = jnp.sum(got_a[...], axis=0)
        sum_c = jnp.sum(got_c[...], axis=0)
        early[...] = jnp.zeros((3, 16, NZ), jnp.float32)
        for t in range(3):
            early[t, 0:4] = sum_a[t, 0]
            early[t, 4:8] = sum_a[t, 1]
            early[t, 8:12] = sum_c[t]
        where_to = lax.broadcasted_iota(jnp.int32, (16, NZ), 1)
        where_from = lax.broadcasted_iota(jnp.int32, (16, NZ), 0)
        for t in range(3):
            for c in range(3):
                n = 3 * t + c
                put = jnp.logical_and(where_from % 4 == c, where_to == 124 + where_from // 4)
                put = jnp.logical_and(put, where_from < 12).astype(jnp.float32)
                block = pl.ds(128 * n, 128)
                q[block, 128:RANK] = q[block, 128:RANK] + mm(early[t], put, ((0,), (0,)))
        snaps[...] = jnp.zeros((8, ROWS_DEV), jnp.float32)
        for t in range(3):
            for c in range(3):
                n = 3 * t + c
                for s in range(3):
                    snaps[s : s + 1, 128 * n : 128 * n + 128] = early[t, 4 * s + c : 4 * s + c + 1]
        product = mm(snaps[...], q[...], ((1,), (0,)))
        cross_own[0:3] = product[0:3, 0:128]
        cross_own[4:7] = product[0:3, 128:RANK]

        arrived(got_b.at[0:15], LINE_B)
        sum_b = jnp.sum(got_b[...], axis=0)
        final[...] = jnp.zeros((NZ, NZ), jnp.float32)
        for t in range(3):
            final[4 * t : 4 * t + 4] = sum_b[t]
        tall = final[...].T
        lane = lax.broadcasted_iota(jnp.int32, (NZ, NZ), 1)
        low_sum = jnp.zeros((8, NZ), jnp.float32)
        high_sum = jnp.zeros((8, NZ), jnp.float32)
        for t in range(3):
            for c in range(3):
                n = 3 * t + c
                block = pl.ds(128 * n, 128)
                wide = jnp.broadcast_to(tall[:, 4 * t + c : 4 * t + c + 1], (NZ, NZ))
                high = jnp.where(lane == NZ - 1, wide, q[block, 128:RANK])
                q[block, 128:RANK] = high
                low_sum = low_sum + jnp.sum((wide * q[block, 0:128]).reshape(16, 8, NZ), axis=0)
                high_sum = high_sum + jnp.sum((wide * high).reshape(16, 8, NZ), axis=0)
        cross_own[3:4] = jnp.sum(low_sum, axis=0, keepdims=True)
        cross_own[7:8] = jnp.sum(high_sum, axis=0, keepdims=True)

        cross_a[zpos] = cross_own[...]
        to_line(cross_own, cross_a.at[zpos], CROSS_A)
        stores[3].start()
        arrived(cross_a.at[0:15], CROSS_A)
        cross_mid[...] = jnp.sum(cross_a[...], axis=0)
        cross_b[ppos] = cross_mid[...]
        to_plane(cross_mid, cross_b.at[ppos], CROSS_B)
        arrived(cross_b.at[0:7], CROSS_B)
        both = jnp.sum(cross_b[...], axis=0)
        small[1] = both
        lines = [jnp.concatenate([both[s : s + 1], both[s + 4 : s + 5]], axis=1) for s in range(4)]
        for k, tail in enumerate(last_columns(lines, lambda k, s: order[k] == s)):
            small[2, k : k + 1] = tail[:, 0:128]
            small[3, k : k + 1] = tail[:, 128:RANK]
        stores[4].start()

        left_here(slot_a.at[0:7], GRAM_A)
        left_here(slot_b.at[0:15], GRAM_B)
        left_here(column.at[0:15], GRAM_C)
        left_here(gram.at[0:7], GRAM_D)
        left_here(got_a.at[0:15], LINE_A)
        left_here(got_c.at[0:15], LINE_C)
        left_here(got_b.at[0:15], LINE_B)
        left_here(cross_a.at[0:15], CROSS_A)
        left_here(cross_b.at[0:7], CROSS_B)
        for n in range(1, 5):
            stores[n].wait()


def second_kernel(
    modes_hbm, field, gram_hbm, q_hbm, small_hbm, lattice, basis, passing, q, small, ends, blank, modes, gram, left, inverse, pivots, sem
):
    group = lax.axis_index("group")

    @pl.when(group < 3)
    def _():
        load = pltpu.make_async_copy(field, passing, sem.at[0])
        load.start()
        q[...] = jnp.zeros((ROWS_DEV, RANK), jnp.float32)
        clear = pltpu.make_async_copy(q, basis, sem.at[1])
        clear.start()
        load.wait()
        store = pltpu.make_async_copy(passing, lattice, sem.at[2])
        store.start()
        store.wait()
        clear.wait()

    @pl.when(group == 3)
    def _():
        load_q = pltpu.make_async_copy(q_hbm, q, sem.at[0])
        load_small = pltpu.make_async_copy(small_hbm, small, sem.at[1])
        load_q.start()
        load_small.start()
        blank[...] = jnp.zeros((CX, NY, NZ), jnp.float32)
        clears = [pltpu.make_async_copy(blank, lattice.at[n], sem.at[4 + n]) for n in range(19)]
        for clear in clears:
            clear.start()
        lane = lax.broadcasted_iota(jnp.int32, (ROWS_DEV, 128), 1)
        load_small.wait()
        load_q.wait()

        @pl.when(jnp.logical_not(small[0, 0, 0] < 1e-6))
        def _():
            load = pltpu.make_async_copy(modes_hbm, modes, sem.at[2])
            load.start()
            load_gram = pltpu.make_async_copy(gram_hbm, gram, sem.at[3])
            load_gram.start()
            load_gram.wait()
            row, col, eye = square_iota()
            matrix, rs_row, diagonal = unit_diagonal(gram[...])
            left[...] = matrix
            inverse[...] = eye
            pivots[...] = jnp.ones((RANK, 128), jnp.float32)

            def eliminate(j, c):
                line = left[pl.ds(j, 1), :]
                mine = inverse[pl.ds(j, 1), :]
                along = lax.broadcasted_iota(jnp.int32, (1, RANK), 1)
                pivot = jnp.sum(jnp.where(along == j, line, 0.0), axis=1, keepdims=True)
                column = jnp.sum(jnp.where(col == j, left[...], 0.0), axis=1, keepdims=True)
                below = lax.broadcasted_iota(jnp.int32, (RANK, 1), 0) > j
                factor = jnp.where(below, column / pivot, 0.0)
                left[...] = left[...] - factor * line
                inverse[...] = inverse[...] - factor * mine
                pivots[pl.ds(j, 1), :] = jnp.broadcast_to(pivot, (1, 128))
                return c

            lax.fori_loop(0, RANK, eliminate, 0)
            inverse[...] = inverse[...] / jnp.sqrt(pivots[:, 0:1]) * rs_row
            raw = jnp.concatenate([small[1, 0:4], small[1, 4:8]], axis=1)
            along = lax.broadcasted_iota(jnp.int32, (4, RANK), 1)
            old = jnp.where(along < MODES, raw * jnp.sqrt(diagonal), 0.0)
            old = jnp.concatenate([old, jnp.zeros((4, RANK), jnp.float32)], axis=0)
            fresh = mm(old, inverse[...], ((1,), (1,)))[0:4]
            fresh = jnp.where(along < MODES, fresh, raw)

            def is_step(k, s):
                return small[0, k + 1 : k + 2, 0:1] == float(s)

            rows = last_columns([fresh[s : s + 1] for s in range(4)], is_step)
            for k in range(4):
                small[2, k : k + 1] = rows[k][:, 0:128]
                small[3, k : k + 1] = rows[k][:, 128:RANK]
            load.wait()
            inverse[...] = inverse[...] * SCALE
            whole = mm(modes[...], inverse[:, 0:MODES], ((1,), (1,)))
            wide = lax.broadcasted_iota(jnp.int32, (ROWS_DEV, RANK), 1)
            q[...] = jnp.where(wide < MODES, whole, q[...])

        first = pltpu.make_async_copy(q.at[:, 0:128], basis.at[:, 0:128], sem.at[0])
        first.start()
        rows = jnp.concatenate([small[2, 0:4], small[3, 0:4]], axis=1)
        rows = jnp.concatenate([jnp.zeros((124, RANK), jnp.float32), rows], axis=0)
        ends[...] = jnp.where(lane < 124, q[:, 128:RANK], mm(q[...], rows, ((1,), (1,))))
        second = pltpu.make_async_copy(ends, basis.at[:, 128:RANK], sem.at[1])
        second.start()
        for clear in clears:
            clear.wait()
        first.wait()
        second.wait()


def local(populations, cell_kind, snapshot_order, sample_phase, slab_map, weighted_modes):
    f32 = jnp.float32
    hbm = pl.BlockSpec(memory_space=pltpu.HBM)
    dma = pltpu.SemaphoreType.DMA

    def buffer(*shape):
        return pltpu.VMEM(shape, f32)

    field, gram, q, small = pl.pallas_call(
        first_kernel,
        out_shape=(
            jax.ShapeDtypeStruct((19, CX, NY, NZ), f32),
            jax.ShapeDtypeStruct((RANK, RANK), f32),
            jax.ShapeDtypeStruct((ROWS_DEV, RANK), f32),
            jax.ShapeDtypeStruct((4, 8, NZ), f32),
        ),
        in_specs=[hbm] * 6,
        out_specs=(hbm,) * 4,
        scratch_shapes=[
            buffer(19, CX, NY, NZ),
            buffer(NPLANE, NLINE, 4, NZ),
            buffer(ROWS_DEV, RANK),
            buffer(4, 8, NZ),
            buffer(19, CX, NY, NZ),
            pltpu.VMEM((CX, NY, NZ), jnp.int32),
            pltpu.SMEM((3,), jnp.int32),
            pltpu.SMEM((4,), jnp.int32),
            pltpu.SMEM((384,), jnp.int32),
            buffer(ROWS_DEV, MODES),
            buffer(STEPS, CX + 2, 5, NY, NZ),
            buffer(STEPS, CX + 2, 5, NY, NZ),
            buffer(STEPS, CX, 9, NY, NZ),
            buffer(CX, 3, NY, NZ),
            buffer(STEPS, 4, NZ),
            buffer(3, 16, NZ),
            buffer(NZ, NZ),
            pltpu.SMEM((48,), jnp.int32),
            buffer(24, 2, 4, NZ),
            buffer(24, 4, NZ),
            buffer(24, 4, NZ),
            buffer(48, 2, 4, NZ),
            buffer(48, 4, NZ),
            buffer(48, 4, NZ),
            buffer(NLINE, 3, 2, 4, NZ),
            buffer(NLINE, 3, 4, NZ),
            buffer(NLINE, 3, 4, NZ),
            buffer(NPLANE, NLINE, 4, NZ),
            buffer(NPLANE, NLINE, 4, NZ),
            buffer(NLINE, 4, NZ),
            buffer(NLINE, 4, NZ),
            buffer(4, NZ),
            buffer(NLINE, 4, NZ),
            buffer(RANK, RANK),
            buffer(RANK, RANK),
            buffer(RANK, RANK),
            buffer(8, ROWS_DEV),
            buffer(8, NZ),
            buffer(NLINE, 8, NZ),
            buffer(8, NZ),
            buffer(NPLANE, 8, NZ),
            dma((6,)),
            dma((5,)),
            dma((STEPS, 2)),
            dma((STEPS, 2)),
            dma((12,)),
            dma((12,)),
        ],
        compiler_params=pltpu.CompilerParams(
            collective_id=0, has_side_effects=True, vmem_limit_bytes=ROOM
        ),
    )(populations, cell_kind, sample_phase, snapshot_order, slab_map, weighted_modes)
    return pl.pallas_call(
        second_kernel,
        out_shape=(
            jax.ShapeDtypeStruct((19, CX, NY, NZ), f32),
            jax.ShapeDtypeStruct((ROWS_DEV, RANK), f32),
        ),
        in_specs=[hbm] * 5,
        out_specs=(hbm, hbm),
        scratch_shapes=[
            buffer(19, CX, NY, NZ),
            buffer(ROWS_DEV, RANK),
            buffer(4, 8, NZ),
            buffer(ROWS_DEV, 128),
            buffer(CX, NY, NZ),
            buffer(ROWS_DEV, MODES),
            buffer(RANK, RANK),
            buffer(RANK, RANK),
            buffer(RANK, RANK),
            buffer(RANK, 128),
            dma((4 + 19,)),
        ],
        compiler_params=pltpu.CompilerParams(vmem_limit_bytes=ROOM),
    )(weighted_modes, field, gram, q, small)


def solution(mesh):
    return jax.shard_map(
        local,
        mesh=mesh,
        in_specs=(
            P(None, ("group", "slab"), None, None),
            P(("group", "slab"), None, None),
            P(),
            P(),
            P(),
            P(("group", "slab"), None),
        ),
        out_specs=(P(None, ("group", "slab"), None, None), P(("group", "slab"), None)),
        check_vma=False,
    )
```

```python
import functools
import math

import jax
import jax.numpy as jnp
from jax import lax
from jax.experimental import pallas as pl
from jax.experimental.pallas import tpu as pltpu
from jax.sharding import PartitionSpec as P

MESH = pl.DeviceIdType.MESH
STEPS = 4
SUB = 4
OMEGA = 0.9
INLET = 0.05
BIG = 1e30

DIRS = [
    (0, 0, 0),
    (1, 0, 0),
    (-1, 0, 0),
    (0, 1, 0),
    (0, -1, 0),
    (0, 0, 1),
    (0, 0, -1),
    (1, 1, 0),
    (-1, -1, 0),
    (1, -1, 0),
    (-1, 1, 0),
    (1, 0, 1),
    (-1, 0, -1),
    (1, 0, -1),
    (-1, 0, 1),
    (0, 1, 1),
    (0, -1, -1),
    (0, 1, -1),
    (0, -1, 1),
]
WEIGHTS = [1.0 / 3.0] + [1.0 / 18.0] * 6 + [1.0 / 36.0] * 12
OPP = [0, 2, 1, 4, 3, 6, 5, 8, 7, 10, 9, 12, 11, 14, 13, 16, 15, 18, 17]
EAST = [i for i in range(19) if DIRS[i][0] == 1]
WEST = [i for i in range(19) if DIRS[i][0] == -1]
REST = [i for i in range(19) if DIRS[i][0] == 0]

CX, NY, NZ = 4, 16, 128
NLINE = 16
NPLANE = 8
RANK = 256
MODES = 252
ROWS_DEV = 1152
ROWS_ALL = 128 * ROWS_DEV
SCALE = math.sqrt(ROWS_ALL)
NEWTON = 2
ROOM = 60 * 1024 * 1024
LINE_FAR = [8, 7, 9, 6, 10, 5, 11, 4, 12, 3, 13, 2, 14, 1, 15]
PLANE_FAR = [4, 5, 3, 6, 2, 7, 1]
FAR_ALL = PLANE_FAR + [0]


def mm(a, b, dims):
    return lax.dot_general(
        a,
        b,
        (dims, ((), ())),
        precision=lax.Precision.HIGHEST,
        preferred_element_type=jnp.float32,
    )


def inflow_value(i):
    along = DIRS[i][0] * INLET
    return WEIGHTS[i] * (1.0 + 3.0 * along + 4.5 * along * along - 1.5 * INLET * INLET)


def moments(f):
    density = f[0]
    for i in range(1, 19):
        density = density + f[i]
    inverse = 1.0 / density
    speeds = []
    for axis in range(3):
        plus = [f[i] for i in range(19) if DIRS[i][axis] == 1]
        minus = [f[i] for i in range(19) if DIRS[i][axis] == -1]
        total = functools.reduce(lambda a, b: a + b, [a - b for a, b in zip(plus, minus)])
        speeds.append(total * inverse)
    return density, speeds


def collide(f, kind):
    density, u = moments(f)
    square = 1.0 - 1.5 * (u[0] * u[0] + u[1] * u[1] + u[2] * u[2])
    fluid = kind == 0
    inlet = kind == 2
    scaled = {w: (OMEGA * w) * density for w in (1.0 / 3.0, 1.0 / 18.0, 1.0 / 36.0)}
    fallback = {}
    post = [None] * 19
    for i in range(19):
        value = inflow_value(i)
        if value not in fallback:
            fallback[value] = jnp.where(inlet, value, BIG)
    for i in range(19):
        if post[i] is not None:
            continue
        w = scaled[WEIGHTS[i]]
        if i == 0:
            post[0] = jnp.where(fluid, (1.0 - OMEGA) * f[0] + w * square, fallback[inflow_value(0)])
            continue
        along = None
        for axis in range(3):
            if DIRS[i][axis] != 0:
                term = u[axis] if DIRS[i][axis] == 1 else -u[axis]
                along = term if along is None else along + term
        even = w * (square + 4.5 * along * along)
        odd = w * (3.0 * along)
        j = OPP[i]
        post[i] = jnp.where(fluid, (1.0 - OMEGA) * f[i] + (even + odd), fallback[inflow_value(i)])
        post[j] = jnp.where(fluid, (1.0 - OMEGA) * f[j] + (even - odd), fallback[inflow_value(j)])
    return post, u


def shifted(plane, i):
    _, north, upward = DIRS[i]
    if north:
        plane = pltpu.roll(plane, north % NY, 0)
    if upward:
        plane = pltpu.roll(plane, upward % NZ, 1)
    return plane


def lower_half(error, row, col):
    return jnp.where(row > col, error, jnp.where(row == col, 0.5 * error, 0.0))


def square_iota():
    row = lax.broadcasted_iota(jnp.int32, (RANK, RANK), 0)
    col = lax.broadcasted_iota(jnp.int32, (RANK, RANK), 1)
    return row, col, (row == col).astype(jnp.float32)


def unit_diagonal(gram):
    row, col, _ = square_iota()
    whole = jnp.where(jnp.logical_and(row == col, row >= MODES), 1.0, gram)
    diagonal = jnp.where(row == col, whole, 0.0)
    along_row = jnp.sum(diagonal, axis=0, keepdims=True)
    rs_row = 1.0 / jnp.sqrt(along_row)
    rs_col = 1.0 / jnp.sqrt(jnp.sum(diagonal, axis=1, keepdims=True))
    return whole * rs_row * rs_col, rs_row, along_row


def last_columns(lines, is_step):
    lane = lax.broadcasted_iota(jnp.int32, (1, RANK), 1)
    old = [jnp.where(lane < MODES, line, 0.0) for line in lines]
    gram = [[None] * 4 for _ in range(4)]
    for s in range(4):
        for t in range(s + 1):
            own = jnp.where(lane == MODES + t, lines[s], 0.0)
            gram[s][t] = jnp.sum(own - old[s] * old[t] * (1.0 / ROWS_ALL), axis=1, keepdims=True)
            gram[t][s] = gram[s][t]

    def chosen(k, values):
        result = values[3]
        for s in range(3):
            result = jnp.where(is_step(k, s), values[s], result)
        return result

    half = [[chosen(k, [gram[s][t] for s in range(4)]) for t in range(4)] for k in range(4)]
    entry = [[chosen(j, half[k]) for j in range(k + 1)] for k in range(4)]
    start = []
    for s in range(4):
        start.append(SCALE * (lane == MODES + s).astype(jnp.float32) - old[s] * (SCALE / ROWS_ALL))
    low = [[None] * 4 for _ in range(4)]
    over = [None] * 4
    result = []
    for k in range(4):
        for j in range(k + 1):
            value = entry[k][j]
            for m in range(j):
                value = value - low[k][m] * low[j][m]
            if k == j:
                over[k] = 1.0 / jnp.sqrt(value)
            else:
                low[k][j] = value * over[j]
        line = chosen(k, start)
        for m in range(k):
            line = line - low[k][m] * result[m]
        result.append(line * over[k])
    return result


def first_kernel(
    pop_hbm,
    kind_hbm,
    phase_hbm,
    order_hbm,
    table_hbm,
    modes_hbm,
    field_hbm,
    gram_hbm,
    q_hbm,
    small_hbm,
    field,
    gram,
    q,
    small,
    pop,
    kind_ref,
    phase,
    order,
    table,
    modes,
    east,
    west,
    rest,
    speeds,
    samples,
    early,
    final,
    picks,
    landed_a,
    landed_c,
    landed_b,
    ready_a,
    ready_c,
    ready_b,
    got_a,
    got_c,
    got_b,
    pack,
    slot_a,
    rows_a,
    slot_b,
    rows_b,
    column,
    square,
    scaled,
    inverse,
    snaps,
    tails,
    cross_own,
    cross_a,
    cross_mid,
    cross_b,
    load_sem,
    store_sem,
    halo_send,
    halo_recv,
    send_sem,
    recv_sem,
    go_sem,
):
    group = lax.axis_index("group")
    slab = lax.axis_index("slab")
    zpos = slab // NPLANE
    ppos = slab % NPLANE
    position = group * 128 + slab
    channel = group < 3
    has_west = jnp.logical_and(channel, position > 0)
    has_east = jnp.logical_and(channel, position < 383)
    west_id = ((position - 1) // 128, (position + 127) % 128)
    east_id = ((position + 1) // 128, (position + 1) % 128)
    ROUTE_A, ROUTE_C, ROUTE_B, LINE_A, LINE_C, LINE_B, GRAM_A, GRAM_B, GRAM_C, GRAM_D, CROSS_A, CROSS_B = range(12)
    odd = slab % 2

    barrier = pltpu.get_barrier_semaphore()

    def hello(target):
        pl.semaphore_signal(barrier, inc=1, device_id=target, device_id_type=MESH)

    loads = [
        pltpu.make_async_copy(a, b, load_sem.at[n])
        for n, (a, b) in enumerate(
            [
                (pop_hbm.at[:, 0], pop.at[:, 0]),
                (kind_hbm, kind_ref),
                (phase_hbm, phase),
                (table_hbm, table),
                (order_hbm, order),
                (modes_hbm, modes),
                (pop_hbm.at[:, CX - 1], pop.at[:, CX - 1]),
                (pop_hbm.at[:, 1 : CX - 1], pop.at[:, 1 : CX - 1]),
            ]
        )
    ]

    stores = [
        pltpu.make_async_copy(a, b, store_sem.at[n])
        for n, (a, b) in enumerate(
            [
                (field, field_hbm),
                (square, gram_hbm),
                (q.at[:, 0:128], q_hbm.at[:, 0:128]),
                (q.at[:, 128:RANK], q_hbm.at[:, 128:RANK]),
                (small, small_hbm),
            ]
        )
    ]

    @pl.when(channel)
    def _():
        for n in (0, 6, 1, 7, 2):
            loads[n].start()

    @pl.when(jnp.logical_not(channel))
    def _():
        loads[5].start()
        loads[4].start()
        loads[3].start()

    def line_peer(d):
        return (group, ((zpos + d) % NLINE) * NPLANE + ppos)

    def plane_peer(d):
        return (3, zpos * NPLANE + (ppos + d) % NPLANE)

    def push(source, target, peer, n):
        pltpu.make_async_remote_copy(
            src_ref=source,
            dst_ref=target,
            send_sem=send_sem.at[n],
            recv_sem=recv_sem.at[n],
            device_id=peer,
            device_id_type=MESH,
        ).start()

    def to_line(source, target, n):
        for d in LINE_FAR:
            push(source, target, line_peer(d), n)

    def to_plane(source, target, n):
        for d in PLANE_FAR:
            push(source, target, plane_peer(d), n)

    def arrived(ref, n):
        pltpu.make_async_copy(ref, ref, recv_sem.at[n]).wait()

    def left_here(ref, n):
        pltpu.make_async_copy(ref, ref, send_sem.at[n]).wait()

    def keep_post(post, x, slot):
        for n, i in enumerate(EAST):
            east[slot, x + 1, n] = post[i]
        for n, i in enumerate(WEST):
            west[slot, x + 1, n] = post[i]
        for n, i in enumerate(REST):
            rest[slot, x, n] = post[i]

    def streamed(slot, x):
        f = [None] * 19
        for n, i in enumerate(REST):
            if i == 0:
                f[0] = rest[slot, x, 0]
                continue
            source = shifted(rest[slot, x, n], i)
            f[i] = jnp.where(source >= 0.5 * BIG, rest[slot, x, REST.index(OPP[i])], source)
        for n, i in enumerate(EAST):
            source = shifted(east[slot, x, n], i)
            f[i] = jnp.where(source >= 0.5 * BIG, west[slot, x + 1, WEST.index(OPP[i])], source)
        for n, i in enumerate(WEST):
            source = shifted(west[slot, x + 2, n], i)
            f[i] = jnp.where(source >= 0.5 * BIG, east[slot, x + 1, EAST.index(OPP[i])], source)
        return f

    def keep_speeds(u, kind, x):
        for c in range(3):
            speeds[x, c] = jnp.where(kind == 1, 0.0, u[c])

    def halo(slot):
        go_east = pltpu.make_async_remote_copy(
            src_ref=east.at[slot, CX],
            dst_ref=east.at[slot, 0],
            send_sem=halo_send.at[slot, 0],
            recv_sem=halo_recv.at[slot, 0],
            device_id=east_id,
            device_id_type=MESH,
        )
        go_west = pltpu.make_async_remote_copy(
            src_ref=west.at[slot, 1],
            dst_ref=west.at[slot, CX + 1],
            send_sem=halo_send.at[slot, 1],
            recv_sem=halo_recv.at[slot, 1],
            device_id=west_id,
            device_id_type=MESH,
        )
        return go_east, go_west

    def send_side(slot, side):
        go_east, go_west = halo(slot)

        @pl.when(jnp.logical_and(has_east, side == 1))
        def _():
            go_east.start()

        @pl.when(jnp.logical_and(has_west, side == 0))
        def _():
            go_west.start()

    def take_side(slot, side):
        go_east, go_west = halo(slot)

        @pl.when(jnp.logical_and(has_east, side == 1))
        def _():
            go_west.wait_recv()

        @pl.when(jnp.logical_and(has_west, side == 0))
        def _():
            go_east.wait_recv()

    def sides(fn):
        def body(n, c):
            fn((odd + n) % 2)
            return c

        lax.fori_loop(0, 2, body, 0)

    def first_plane(x):
        post, _ = collide([pop[i, x] for i in range(19)], kind_ref[x])
        keep_post(post, x, 0)

    def middle_plane(slot, x):
        kind = kind_ref[x]
        post, u = collide(streamed(slot, x), kind)
        keep_speeds(u, kind, x)
        keep_post(post, x, slot + 1)

    def last_plane(slot, x):
        kind = kind_ref[x]
        f = streamed(slot, x)
        _, u = moments(f)
        keep_speeds(u, kind, x)
        for i in range(19):
            field[i, x] = jnp.where(kind == 1, pop[i, x], f[i])

    def pair(fn):
        def body(n, c):
            fn(n)
            return c

        lax.fori_loop(0, 2, body, 0)

    @pl.when(channel)
    def _():
        @pl.when(has_east)
        def _():
            hello(east_id)

        @pl.when(has_west)
        def _():
            hello(west_id)

        for d in FAR_ALL:
            hello((3, zpos * NPLANE + (ppos + d) % NPLANE))

        samples[...] = jnp.zeros((STEPS, 4, NZ), jnp.float32)

        @pl.when(position == 0)
        def _():
            east[:, 0] = jnp.full((STEPS, 5, NY, NZ), BIG, jnp.float32)

        @pl.when(position == 383)
        def _():
            west[:, CX + 1] = jnp.full((STEPS, 5, NY, NZ), BIG, jnp.float32)

        for n in (0, 6, 1):
            loads[n].wait()
        sides(lambda side: first_plane(3 * side))
        edge = jnp.logical_or(position == 0, position == 383)

        @pl.when(edge)
        def _():
            pl.semaphore_wait(barrier, 1)

        @pl.when(jnp.logical_not(edge))
        def _():
            pl.semaphore_wait(barrier, 2)

        sides(lambda side: send_side(0, side))
        loads[7].wait()
        pair(lambda n: first_plane(1 + n))
        loads[2].wait()

        lanes = lax.broadcasted_iota(jnp.int32, (NZ, NZ), 1)
        depth = lax.broadcasted_iota(jnp.int32, (NZ, NZ), 0)
        pick_z = (depth == phase[2] + SUB * (lanes % 32)).astype(jnp.float32)
        lane3 = lax.broadcasted_iota(jnp.int32, (3, NY, NZ), 2)
        row3 = lax.broadcasted_iota(jnp.int32, (3, NY, NZ), 1)
        pick_y = row3 == phase[1] + SUB * (lane3 // 32)

        def sample(step):
            plane = speeds[phase[0]].reshape(3 * NY, NZ)
            along = mm(plane, pick_z, ((1,), (0,))).reshape(3, NY, NZ)
            samples[step, 0:3] = jnp.sum(jnp.where(pick_y, along, 0.0), axis=1)

        def to_analysis(source, target, n):
            for d in FAR_ALL:
                push(source, target.at[group * NPLANE + ppos], (3, zpos * NPLANE + (ppos + d) % NPLANE), n)

        def one_step(slot, c):
            pair(lambda n: middle_plane(slot, 1 + n))

            def one_side(side):
                take_side(slot, side)
                middle_plane(slot, 3 * side)
                send_side(slot + 1, side)

            sides(one_side)
            sample(slot)
            return c

        lax.fori_loop(0, 2, one_step, 0)
        pl.semaphore_wait(go_sem, 8)
        to_analysis(samples.at[0:2], landed_a, ROUTE_A)
        one_step(2, 0)
        to_analysis(samples.at[2], landed_c, ROUTE_C)
        pair(lambda n: last_plane(STEPS - 1, 1 + n))

        def last_side(side):
            take_side(STEPS - 1, side)
            last_plane(STEPS - 1, 3 * side)

        sides(last_side)
        sample(STEPS - 1)
        to_analysis(samples.at[3], landed_b, ROUTE_B)
        stores[0].start()

        def sent(slot, c):
            go_east, go_west = halo(slot)

            @pl.when(has_east)
            def _():
                go_east.wait_send()

            @pl.when(has_west)
            def _():
                go_west.wait_send()

            return c

        lax.fori_loop(0, STEPS, sent, 0)
        left_here(landed_a.at[0:8], ROUTE_A)
        left_here(landed_c.at[0:8], ROUTE_C)
        left_here(landed_b.at[0:8], ROUTE_B)
        stores[0].wait()

    @pl.when(jnp.logical_not(channel))
    def _():
        for d in LINE_FAR:
            hello(line_peer(d))
        for d in PLANE_FAR:
            hello(plane_peer(d))

        square[...] = jnp.zeros((RANK, RANK), jnp.float32)
        loads[5].wait()
        square[0:MODES, 0:MODES] = mm(modes[...], modes[...], ((0,), (0,)))
        for p in range(NPLANE):
            for z in range(NLINE):
                down, across = 32 * p + 4 * (z // 2), 128 * (z % 2)
                pack[p, z] = square[down : down + 4, across : across + 128]
        pl.semaphore_wait(barrier, 15 + 7 + 24)

        slot_a[ppos] = pack[ppos]
        for d in PLANE_FAR:
            push(pack.at[(ppos + d) % NPLANE], slot_a.at[ppos], plane_peer(d), GRAM_A)

        for n in range(24):
            pl.semaphore_signal(
                go_sem,
                inc=1,
                device_id=(n // NPLANE, zpos * NPLANE + (ppos + n) % NPLANE),
                device_id_type=MESH,
            )

        loads[3].wait()

        def pick(n, c):
            found = jnp.int32(-1)
            wanted = 24 * (n // 3) + 3 * ppos + n % 3
            for g in range(3):
                for p in range(NPLANE):
                    row = table[g * 128 + zpos * NPLANE + p]
                    found = jnp.where(row == wanted, g * NPLANE + p, found)
            picks[n] = found
            return c

        lax.fori_loop(0, 48, pick, 0)

        def forward(landed, ready, got, from_sem, to_sem):
            arrived(landed, from_sem)

            def place(n, c):
                source = picks[n]
                ready[n] = jnp.where(source >= 0, landed[jnp.maximum(source, 0)], 0.0)
                return c

            lax.fori_loop(0, 48, place, 0)
            got[zpos] = ready[pl.ds(3 * zpos, 3)]
            for d in LINE_FAR:
                push(ready.at[pl.ds(3 * ((zpos + d) % NLINE), 3)], got.at[zpos], line_peer(d), to_sem)

        arrived(slot_a.at[0:7], GRAM_A)
        rows_a[...] = jnp.sum(slot_a[...], axis=0)
        slot_b[zpos] = rows_a[zpos]
        for d in LINE_FAR:
            push(rows_a.at[(zpos + d) % NLINE], slot_b.at[zpos], line_peer(d), GRAM_B)
        arrived(slot_b.at[0:15], GRAM_B)
        rows_b[...] = jnp.sum(slot_b[...], axis=0)
        column[zpos] = rows_b[...]
        to_line(rows_b, column.at[zpos], GRAM_C)
        forward(landed_a, ready_a, got_a, ROUTE_A, LINE_A)
        arrived(column.at[0:15], GRAM_C)
        gram[ppos] = column[...]
        to_plane(column, gram.at[ppos], GRAM_D)
        forward(landed_c, ready_c, got_c, ROUTE_C, LINE_C)
        arrived(gram.at[0:7], GRAM_D)
        forward(landed_b, ready_b, got_b, ROUTE_B, LINE_B)
        for p in range(NPLANE):
            for z in range(NLINE):
                down, across = 32 * p + 4 * (z // 2), 128 * (z % 2)
                square[down : down + 4, across : across + 128] = gram[p, z]
        stores[1].start()

        arrived(got_a.at[0:15], LINE_A)
        arrived(got_c.at[0:15], LINE_C)
        sum_a = jnp.sum(got_a[...], axis=0)
        sum_c = jnp.sum(got_c[...], axis=0)
        early[...] = jnp.zeros((3, 16, NZ), jnp.float32)
        for t in range(3):
            early[t, 0:4] = sum_a[t, 0]
            early[t, 4:8] = sum_a[t, 1]
            early[t, 8:12] = sum_c[t]
        where_to = lax.broadcasted_iota(jnp.int32, (16, NZ), 1)
        where_from = lax.broadcasted_iota(jnp.int32, (16, NZ), 0)
        for t in range(3):
            for c in range(3):
                n = 3 * t + c
                put = jnp.logical_and(where_from % 4 == c, where_to == 124 + where_from // 4)
                put = jnp.logical_and(put, where_from < 12).astype(jnp.float32)
                block = pl.ds(128 * n, 128)
                tails[block, :] = mm(early[t], put, ((0,), (0,)))
        snaps[...] = jnp.zeros((8, ROWS_DEV), jnp.float32)
        for t in range(3):
            for c in range(3):
                n = 3 * t + c
                for s in range(3):
                    snaps[s : s + 1, 128 * n : 128 * n + 128] = early[t, 4 * s + c : 4 * s + c + 1]

        row, col, eye = square_iota()
        matrix, rs_row, _ = unit_diagonal(square[...])
        scaled[...] = matrix
        inverse[...] = eye - lower_half(matrix - eye, row, col)

        def newton(n, size):
            here = inverse[...]
            error = mm(mm(here, scaled[...], ((1,), (0,))), here, ((1,), (1,))) - eye
            inverse[...] = here - mm(lower_half(error, row, col), here, ((1,), (0,)))
            return jnp.sum(jnp.sum(error * error, axis=0, keepdims=True), axis=1, keepdims=True)

        size = lax.fori_loop(0, NEWTON, newton, jnp.ones((1, 1), jnp.float32))
        good = jnp.broadcast_to(size < 1e-6, (RANK, RANK))
        factor = jnp.where(good, inverse[...], eye) * rs_row
        inverse[...] = factor * SCALE
        projected = mm(modes[...], inverse[:, 0:MODES], ((1,), (1,)))
        q[:, 0:128] = projected[:, 0:128]
        q[:, 128:RANK] = projected[:, 128:RANK] + tails[...]
        stores[2].start()
        loads[4].wait()
        small[...] = jnp.zeros((4, 8, NZ), jnp.float32)
        small[0] = jnp.broadcast_to(size, (8, NZ))
        for k in range(4):
            small[0, k + 1 : k + 2] = jnp.full((1, NZ), 1.0, jnp.float32) * order[k].astype(jnp.float32)

        product = mm(snaps[...], q[...], ((1,), (0,)))
        cross_own[0:3] = product[0:3, 0:128]
        cross_own[4:7] = product[0:3, 128:RANK]

        arrived(got_b.at[0:15], LINE_B)
        sum_b = jnp.sum(got_b[...], axis=0)
        final[...] = jnp.zeros((NZ, NZ), jnp.float32)
        for t in range(3):
            final[4 * t : 4 * t + 4] = sum_b[t]
        tall = final[...].T
        lane = lax.broadcasted_iota(jnp.int32, (NZ, NZ), 1)
        low_sum = jnp.zeros((8, NZ), jnp.float32)
        high_sum = jnp.zeros((8, NZ), jnp.float32)
        for t in range(3):
            for c in range(3):
                n = 3 * t + c
                block = pl.ds(128 * n, 128)
                wide = jnp.broadcast_to(tall[:, 4 * t + c : 4 * t + c + 1], (NZ, NZ))
                high = jnp.where(lane == NZ - 1, wide, q[block, 128:RANK])
                q[block, 128:RANK] = high
                low_sum = low_sum + jnp.sum((wide * q[block, 0:128]).reshape(16, 8, NZ), axis=0)
                high_sum = high_sum + jnp.sum((wide * high).reshape(16, 8, NZ), axis=0)
        cross_own[3:4] = jnp.sum(low_sum, axis=0, keepdims=True)
        cross_own[7:8] = jnp.sum(high_sum, axis=0, keepdims=True)

        cross_a[zpos] = cross_own[...]
        to_line(cross_own, cross_a.at[zpos], CROSS_A)
        stores[3].start()
        arrived(cross_a.at[0:15], CROSS_A)
        cross_mid[...] = jnp.sum(cross_a[...], axis=0)
        cross_b[ppos] = cross_mid[...]
        to_plane(cross_mid, cross_b.at[ppos], CROSS_B)
        arrived(cross_b.at[0:7], CROSS_B)
        both = jnp.sum(cross_b[...], axis=0)
        small[1] = both
        lines = [jnp.concatenate([both[s : s + 1], both[s + 4 : s + 5]], axis=1) for s in range(4)]
        for k, tail in enumerate(last_columns(lines, lambda k, s: order[k] == s)):
            small[2, k : k + 1] = tail[:, 0:128]
            small[3, k : k + 1] = tail[:, 128:RANK]
        stores[4].start()

        left_here(slot_a.at[0:7], GRAM_A)
        left_here(slot_b.at[0:15], GRAM_B)
        left_here(column.at[0:15], GRAM_C)
        left_here(gram.at[0:7], GRAM_D)
        left_here(got_a.at[0:15], LINE_A)
        left_here(got_c.at[0:15], LINE_C)
        left_here(got_b.at[0:15], LINE_B)
        left_here(cross_a.at[0:15], CROSS_A)
        left_here(cross_b.at[0:7], CROSS_B)
        for n in range(1, 5):
            stores[n].wait()


def second_kernel(
    modes_hbm, field, gram_hbm, q_hbm, small_hbm, lattice, basis, passing, q, small, ends, blank, modes, gram, left, inverse, pivots, sem
):
    group = lax.axis_index("group")

    @pl.when(group < 3)
    def _():
        load = pltpu.make_async_copy(field, passing, sem.at[0])
        load.start()
        q[...] = jnp.zeros((ROWS_DEV, RANK), jnp.float32)
        clear = pltpu.make_async_copy(q, basis, sem.at[1])
        clear.start()
        load.wait()
        store = pltpu.make_async_copy(passing, lattice, sem.at[2])
        store.start()
        store.wait()
        clear.wait()

    @pl.when(group == 3)
    def _():
        load_q = pltpu.make_async_copy(q_hbm, q, sem.at[0])
        load_small = pltpu.make_async_copy(small_hbm, small, sem.at[1])
        load_q.start()
        load_small.start()
        blank[...] = jnp.zeros((CX, NY, NZ), jnp.float32)
        clears = [pltpu.make_async_copy(blank, lattice.at[n], sem.at[4 + n]) for n in range(19)]
        for clear in clears:
            clear.start()
        lane = lax.broadcasted_iota(jnp.int32, (ROWS_DEV, 128), 1)
        load_small.wait()
        load_q.wait()

        @pl.when(jnp.logical_not(small[0, 0, 0] < 1e-6))
        def _():
            load = pltpu.make_async_copy(modes_hbm, modes, sem.at[2])
            load.start()
            load_gram = pltpu.make_async_copy(gram_hbm, gram, sem.at[3])
            load_gram.start()
            load_gram.wait()
            row, col, eye = square_iota()
            matrix, rs_row, diagonal = unit_diagonal(gram[...])
            left[...] = matrix
            inverse[...] = eye
            pivots[...] = jnp.ones((RANK, 128), jnp.float32)

            def eliminate(j, c):
                line = left[pl.ds(j, 1), :]
                mine = inverse[pl.ds(j, 1), :]
                along = lax.broadcasted_iota(jnp.int32, (1, RANK), 1)
                pivot = jnp.sum(jnp.where(along == j, line, 0.0), axis=1, keepdims=True)
                column = jnp.sum(jnp.where(col == j, left[...], 0.0), axis=1, keepdims=True)
                below = lax.broadcasted_iota(jnp.int32, (RANK, 1), 0) > j
                factor = jnp.where(below, column / pivot, 0.0)
                left[...] = left[...] - factor * line
                inverse[...] = inverse[...] - factor * mine
                pivots[pl.ds(j, 1), :] = jnp.broadcast_to(pivot, (1, 128))
                return c

            lax.fori_loop(0, RANK, eliminate, 0)
            inverse[...] = inverse[...] / jnp.sqrt(pivots[:, 0:1]) * rs_row
            raw = jnp.concatenate([small[1, 0:4], small[1, 4:8]], axis=1)
            along = lax.broadcasted_iota(jnp.int32, (4, RANK), 1)
            old = jnp.where(along < MODES, raw * jnp.sqrt(diagonal), 0.0)
            old = jnp.concatenate([old, jnp.zeros((4, RANK), jnp.float32)], axis=0)
            fresh = mm(old, inverse[...], ((1,), (1,)))[0:4]
            fresh = jnp.where(along < MODES, fresh, raw)

            def is_step(k, s):
                return small[0, k + 1 : k + 2, 0:1] == float(s)

            rows = last_columns([fresh[s : s + 1] for s in range(4)], is_step)
            for k in range(4):
                small[2, k : k + 1] = rows[k][:, 0:128]
                small[3, k : k + 1] = rows[k][:, 128:RANK]
            load.wait()
            inverse[...] = inverse[...] * SCALE
            whole = mm(modes[...], inverse[:, 0:MODES], ((1,), (1,)))
            wide = lax.broadcasted_iota(jnp.int32, (ROWS_DEV, RANK), 1)
            q[...] = jnp.where(wide < MODES, whole, q[...])

        first = pltpu.make_async_copy(q.at[:, 0:128], basis.at[:, 0:128], sem.at[0])
        first.start()
        rows = jnp.concatenate([small[2, 0:4], small[3, 0:4]], axis=1)
        rows = jnp.concatenate([jnp.zeros((124, RANK), jnp.float32), rows], axis=0)
        ends[...] = jnp.where(lane < 124, q[:, 128:RANK], mm(q[...], rows, ((1,), (1,))))
        second = pltpu.make_async_copy(ends, basis.at[:, 128:RANK], sem.at[1])
        second.start()
        for clear in clears:
            clear.wait()
        first.wait()
        second.wait()


def local(populations, cell_kind, snapshot_order, sample_phase, slab_map, weighted_modes):
    f32 = jnp.float32
    hbm = pl.BlockSpec(memory_space=pltpu.HBM)
    dma = pltpu.SemaphoreType.DMA

    def buffer(*shape):
        return pltpu.VMEM(shape, f32)

    field, gram, q, small = pl.pallas_call(
        first_kernel,
        out_shape=(
            jax.ShapeDtypeStruct((19, CX, NY, NZ), f32),
            jax.ShapeDtypeStruct((RANK, RANK), f32),
            jax.ShapeDtypeStruct((ROWS_DEV, RANK), f32),
            jax.ShapeDtypeStruct((4, 8, NZ), f32),
        ),
        in_specs=[hbm] * 6,
        out_specs=(hbm,) * 4,
        scratch_shapes=[
            buffer(19, CX, NY, NZ),
            buffer(NPLANE, NLINE, 4, NZ),
            buffer(ROWS_DEV, RANK),
            buffer(4, 8, NZ),
            buffer(19, CX, NY, NZ),
            pltpu.VMEM((CX, NY, NZ), jnp.int32),
            pltpu.SMEM((3,), jnp.int32),
            pltpu.SMEM((4,), jnp.int32),
            pltpu.SMEM((384,), jnp.int32),
            buffer(ROWS_DEV, MODES),
            buffer(STEPS, CX + 2, 5, NY, NZ),
            buffer(STEPS, CX + 2, 5, NY, NZ),
            buffer(STEPS, CX, 9, NY, NZ),
            buffer(CX, 3, NY, NZ),
            buffer(STEPS, 4, NZ),
            buffer(3, 16, NZ),
            buffer(NZ, NZ),
            pltpu.SMEM((48,), jnp.int32),
            buffer(24, 2, 4, NZ),
            buffer(24, 4, NZ),
            buffer(24, 4, NZ),
            buffer(48, 2, 4, NZ),
            buffer(48, 4, NZ),
            buffer(48, 4, NZ),
            buffer(NLINE, 3, 2, 4, NZ),
            buffer(NLINE, 3, 4, NZ),
            buffer(NLINE, 3, 4, NZ),
            buffer(NPLANE, NLINE, 4, NZ),
            buffer(NPLANE, NLINE, 4, NZ),
            buffer(NLINE, 4, NZ),
            buffer(NLINE, 4, NZ),
            buffer(4, NZ),
            buffer(NLINE, 4, NZ),
            buffer(RANK, RANK),
            buffer(RANK, RANK),
            buffer(RANK, RANK),
            buffer(8, ROWS_DEV),
            buffer(ROWS_DEV, 128),
            buffer(8, NZ),
            buffer(NLINE, 8, NZ),
            buffer(8, NZ),
            buffer(NPLANE, 8, NZ),
            dma((8,)),
            dma((5,)),
            dma((STEPS, 2)),
            dma((STEPS, 2)),
            dma((12,)),
            dma((12,)),
            pltpu.SemaphoreType.REGULAR,
        ],
        compiler_params=pltpu.CompilerParams(
            collective_id=0, has_side_effects=True, vmem_limit_bytes=ROOM
        ),
    )(populations, cell_kind, sample_phase, snapshot_order, slab_map, weighted_modes)
    return pl.pallas_call(
        second_kernel,
        out_shape=(
            jax.ShapeDtypeStruct((19, CX, NY, NZ), f32),
            jax.ShapeDtypeStruct((ROWS_DEV, RANK), f32),
        ),
        in_specs=[hbm] * 5,
        out_specs=(hbm, hbm),
        scratch_shapes=[
            buffer(19, CX, NY, NZ),
            buffer(ROWS_DEV, RANK),
            buffer(4, 8, NZ),
            buffer(ROWS_DEV, 128),
            buffer(CX, NY, NZ),
            buffer(ROWS_DEV, MODES),
            buffer(RANK, RANK),
            buffer(RANK, RANK),
            buffer(RANK, RANK),
            buffer(RANK, 128),
            dma((4 + 19,)),
        ],
        compiler_params=pltpu.CompilerParams(vmem_limit_bytes=ROOM),
    )(weighted_modes, field, gram, q, small)


def solution(mesh):
    return jax.shard_map(
        local,
        mesh=mesh,
        in_specs=(
            P(None, ("group", "slab"), None, None),
            P(("group", "slab"), None, None),
            P(),
            P(),
            P(),
            P(("group", "slab"), None),
        ),
        out_specs=(P(None, ("group", "slab"), None, None), P(("group", "slab"), None)),
        check_vma=False,
    )
```

```python
import functools
import math

import jax
import jax.numpy as jnp
from jax import lax
from jax.experimental import pallas as pl
from jax.experimental.pallas import tpu as pltpu
from jax.sharding import PartitionSpec as P

MESH = pl.DeviceIdType.MESH
STEPS = 4
SUB = 4
OMEGA = 0.9
INLET = 0.05
BIG = 1e30

DIRS = [
    (0, 0, 0),
    (1, 0, 0),
    (-1, 0, 0),
    (0, 1, 0),
    (0, -1, 0),
    (0, 0, 1),
    (0, 0, -1),
    (1, 1, 0),
    (-1, -1, 0),
    (1, -1, 0),
    (-1, 1, 0),
    (1, 0, 1),
    (-1, 0, -1),
    (1, 0, -1),
    (-1, 0, 1),
    (0, 1, 1),
    (0, -1, -1),
    (0, 1, -1),
    (0, -1, 1),
]
WEIGHTS = [1.0 / 3.0] + [1.0 / 18.0] * 6 + [1.0 / 36.0] * 12
OPP = [0, 2, 1, 4, 3, 6, 5, 8, 7, 10, 9, 12, 11, 14, 13, 16, 15, 18, 17]
EAST = [i for i in range(19) if DIRS[i][0] == 1]
WEST = [i for i in range(19) if DIRS[i][0] == -1]
REST = [i for i in range(19) if DIRS[i][0] == 0]

CX, NY, NZ = 4, 16, 128
NLINE = 16
NPLANE = 8
RANK = 256
MODES = 252
ROWS_DEV = 1152
ROWS_ALL = 128 * ROWS_DEV
SCALE = math.sqrt(ROWS_ALL)
ROOM = 60 * 1024 * 1024
LINE_FAR = [8, 7, 9, 6, 10, 5, 11, 4, 12, 3, 13, 2, 14, 1, 15]
PLANE_FAR = [4, 5, 3, 6, 2, 7, 1]
FAR_ALL = PLANE_FAR + [0]


def mm(a, b, dims):
    return lax.dot_general(
        a,
        b,
        (dims, ((), ())),
        precision=lax.Precision.HIGHEST,
        preferred_element_type=jnp.float32,
    )


def quick(a, b, dims):
    return lax.dot_general(
        a.astype(jnp.bfloat16),
        b.astype(jnp.bfloat16),
        (dims, ((), ())),
        preferred_element_type=jnp.float32,
    )


def inflow_value(i):
    along = DIRS[i][0] * INLET
    return WEIGHTS[i] * (1.0 + 3.0 * along + 4.5 * along * along - 1.5 * INLET * INLET)


def sums(f):
    density = f[0]
    for i in range(1, 19):
        density = density + f[i]
    totals = []
    for axis in range(3):
        plus = [f[i] for i in range(19) if DIRS[i][axis] == 1]
        minus = [f[i] for i in range(19) if DIRS[i][axis] == -1]
        totals.append(functools.reduce(lambda a, b: a + b, [a - b for a, b in zip(plus, minus)]))
    return density, totals


def moments(f):
    density, totals = sums(f)
    inverse = 1.0 / density
    return density, [total * inverse for total in totals]


def collide(f, kind):
    density, u = moments(f)
    square = 1.0 - 1.5 * (u[0] * u[0] + u[1] * u[1] + u[2] * u[2])
    fluid = kind == 0
    inlet = kind == 2
    scaled = {w: (OMEGA * w) * density for w in (1.0 / 3.0, 1.0 / 18.0, 1.0 / 36.0)}
    fallback = {}
    post = [None] * 19
    for i in range(19):
        value = inflow_value(i)
        if value not in fallback:
            fallback[value] = jnp.where(inlet, value, BIG)
    for i in range(19):
        if post[i] is not None:
            continue
        w = scaled[WEIGHTS[i]]
        if i == 0:
            post[0] = jnp.where(fluid, (1.0 - OMEGA) * f[0] + w * square, fallback[inflow_value(0)])
            continue
        along = None
        for axis in range(3):
            if DIRS[i][axis] != 0:
                term = u[axis] if DIRS[i][axis] == 1 else -u[axis]
                along = term if along is None else along + term
        even = w * (square + 4.5 * along * along)
        odd = w * (3.0 * along)
        j = OPP[i]
        post[i] = jnp.where(fluid, (1.0 - OMEGA) * f[i] + (even + odd), fallback[inflow_value(i)])
        post[j] = jnp.where(fluid, (1.0 - OMEGA) * f[j] + (even - odd), fallback[inflow_value(j)])
    return post, u


def shifted(plane, i):
    _, north, upward = DIRS[i]
    if north:
        plane = pltpu.roll(plane, north % NY, 0)
    if upward:
        plane = pltpu.roll(plane, upward % NZ, 1)
    return plane


def lower_half(error, row, col):
    return jnp.where(row > col, error, jnp.where(row == col, 0.5 * error, 0.0))


def square_iota():
    row = lax.broadcasted_iota(jnp.int32, (RANK, RANK), 0)
    col = lax.broadcasted_iota(jnp.int32, (RANK, RANK), 1)
    return row, col, (row == col).astype(jnp.float32)


def unit_diagonal(gram):
    row, col, _ = square_iota()
    whole = jnp.where(jnp.logical_and(row == col, row >= MODES), 1.0, gram)
    diagonal = jnp.where(row == col, whole, 0.0)
    along_row = jnp.sum(diagonal, axis=0, keepdims=True)
    rs_row = 1.0 / jnp.sqrt(along_row)
    rs_col = 1.0 / jnp.sqrt(jnp.sum(diagonal, axis=1, keepdims=True))
    return whole * rs_row * rs_col, rs_row, along_row


def last_columns(lines, is_step):
    lane = lax.broadcasted_iota(jnp.int32, (1, RANK), 1)
    old = [jnp.where(lane < MODES, line, 0.0) for line in lines]
    gram = [[None] * 4 for _ in range(4)]
    for s in range(4):
        for t in range(s + 1):
            own = jnp.where(lane == MODES + t, lines[s], 0.0)
            gram[s][t] = jnp.sum(own - old[s] * old[t] * (1.0 / ROWS_ALL), axis=1, keepdims=True)
            gram[t][s] = gram[s][t]

    def chosen(k, values):
        result = values[3]
        for s in range(3):
            result = jnp.where(is_step(k, s), values[s], result)
        return result

    half = [[chosen(k, [gram[s][t] for s in range(4)]) for t in range(4)] for k in range(4)]
    entry = [[chosen(j, half[k]) for j in range(k + 1)] for k in range(4)]
    start = []
    for s in range(4):
        start.append(SCALE * (lane == MODES + s).astype(jnp.float32) - old[s] * (SCALE / ROWS_ALL))
    low = [[None] * 4 for _ in range(4)]
    over = [None] * 4
    result = []
    for k in range(4):
        for j in range(k + 1):
            value = entry[k][j]
            for m in range(j):
                value = value - low[k][m] * low[j][m]
            if k == j:
                over[k] = 1.0 / jnp.sqrt(value)
            else:
                low[k][j] = value * over[j]
        line = chosen(k, start)
        for m in range(k):
            line = line - low[k][m] * result[m]
        result.append(line * over[k])
    return result


def first_kernel(
    pop_hbm,
    kind_hbm,
    phase_hbm,
    order_hbm,
    table_hbm,
    modes_hbm,
    field_hbm,
    gram_hbm,
    q_hbm,
    small_hbm,
    field,
    gram,
    q,
    small,
    pop,
    kind_ref,
    phase,
    order,
    table,
    modes,
    east,
    west,
    rest,
    speeds,
    samples,
    parts,
    across,
    ends,
    final,
    picks,
    picks_next,
    rows_next,
    landed_a,
    landed_b,
    ready_a,
    ready_b,
    got_a,
    got_b,
    pack,
    slot_a,
    rows_a,
    slot_b,
    rows_b,
    column,
    square,
    scaled,
    inverse,
    cross_own,
    cross_a,
    cross_mid,
    cross_b,
    load_sem,
    store_sem,
    halo_send,
    halo_recv,
    send_sem,
    recv_sem,
    go_sem,
):
    group = lax.axis_index("group")
    slab = lax.axis_index("slab")
    zpos = slab // NPLANE
    ppos = slab % NPLANE
    position = group * 128 + slab
    channel = group < 3
    has_west = jnp.logical_and(channel, position > 0)
    has_east = jnp.logical_and(channel, position < 383)
    west_id = ((position - 1) // 128, (position + 127) % 128)
    east_id = ((position + 1) // 128, (position + 1) % 128)
    ROUTE_A, ROUTE_B, LINE_A, LINE_B, GRAM_A, GRAM_B, GRAM_C, GRAM_D, CROSS_A, CROSS_B = range(10)
    odd = slab % 2

    barrier = pltpu.get_barrier_semaphore()

    def hello(target):
        pl.semaphore_signal(barrier, inc=1, device_id=target, device_id_type=MESH)

    loads = [
        pltpu.make_async_copy(a, b, load_sem.at[n])
        for n, (a, b) in enumerate(
            [
                (pop_hbm.at[:, 0], pop.at[:, 0]),
                (kind_hbm, kind_ref),
                (phase_hbm, phase),
                (table_hbm, table),
                (order_hbm, order),
                (modes_hbm, modes),
                (pop_hbm.at[:, CX - 1], pop.at[:, CX - 1]),
                (pop_hbm.at[:, 1 : CX - 1], pop.at[:, 1 : CX - 1]),
            ]
        )
    ]

    stores = [
        pltpu.make_async_copy(a, b, store_sem.at[n])
        for n, (a, b) in enumerate(
            [
                (field, field_hbm),
                (square, gram_hbm),
                (q.at[:, 0:128], q_hbm.at[:, 0:128]),
                (q.at[:, 128:RANK], q_hbm.at[:, 128:RANK]),
                (small, small_hbm),
            ]
        )
    ]

    @pl.when(channel)
    def _():
        for n in (0, 6, 1, 7, 2):
            loads[n].start()

    @pl.when(jnp.logical_not(channel))
    def _():
        loads[5].start()
        loads[4].start()
        loads[3].start()
        loads[2].start()

    def line_peer(d):
        return (group, ((zpos + d) % NLINE) * NPLANE + ppos)

    def plane_peer(d):
        return (3, zpos * NPLANE + (ppos + d) % NPLANE)

    def push(source, target, peer, n):
        pltpu.make_async_remote_copy(
            src_ref=source,
            dst_ref=target,
            send_sem=send_sem.at[n],
            recv_sem=recv_sem.at[n],
            device_id=peer,
            device_id_type=MESH,
        ).start()

    def to_line(source, target, n):
        for d in LINE_FAR:
            push(source, target, line_peer(d), n)

    def to_plane(source, target, n):
        for d in PLANE_FAR:
            push(source, target, plane_peer(d), n)

    def arrived(ref, n):
        pltpu.make_async_copy(ref, ref, recv_sem.at[n]).wait()

    def left_here(ref, n):
        pltpu.make_async_copy(ref, ref, send_sem.at[n]).wait()

    def keep_post(post, x, slot):
        for n, i in enumerate(EAST):
            east[slot, x + 1, n] = post[i]
        for n, i in enumerate(WEST):
            west[slot, x + 1, n] = post[i]
        for n, i in enumerate(REST):
            rest[slot, x, n] = post[i]

    def streamed(slot, x):
        f = [None] * 19
        for n, i in enumerate(REST):
            if i == 0:
                f[0] = rest[slot, x, 0]
                continue
            source = shifted(rest[slot, x, n], i)
            f[i] = jnp.where(source >= 0.5 * BIG, rest[slot, x, REST.index(OPP[i])], source)
        for n, i in enumerate(EAST):
            source = shifted(east[slot, x, n], i)
            f[i] = jnp.where(source >= 0.5 * BIG, west[slot, x + 1, WEST.index(OPP[i])], source)
        for n, i in enumerate(WEST):
            source = shifted(west[slot, x + 2, n], i)
            f[i] = jnp.where(source >= 0.5 * BIG, east[slot, x + 1, EAST.index(OPP[i])], source)
        return f

    def keep_speeds(u, kind, x):
        for c in range(3):
            speeds[x, c] = jnp.where(kind == 1, 0.0, u[c])

    def halo(slot):
        go_east = pltpu.make_async_remote_copy(
            src_ref=east.at[slot, CX],
            dst_ref=east.at[slot, 0],
            send_sem=halo_send.at[slot, 0],
            recv_sem=halo_recv.at[slot, 0],
            device_id=east_id,
            device_id_type=MESH,
        )
        go_west = pltpu.make_async_remote_copy(
            src_ref=west.at[slot, 1],
            dst_ref=west.at[slot, CX + 1],
            send_sem=halo_send.at[slot, 1],
            recv_sem=halo_recv.at[slot, 1],
            device_id=west_id,
            device_id_type=MESH,
        )
        return go_east, go_west

    def send_side(slot, side):
        go_east, go_west = halo(slot)

        @pl.when(jnp.logical_and(has_east, side == 1))
        def _():
            go_east.start()

        @pl.when(jnp.logical_and(has_west, side == 0))
        def _():
            go_west.start()

    def take_side(slot, side):
        go_east, go_west = halo(slot)

        @pl.when(jnp.logical_and(has_east, side == 1))
        def _():
            go_west.wait_recv()

        @pl.when(jnp.logical_and(has_west, side == 0))
        def _():
            go_east.wait_recv()

    def sides(fn):
        def body(n, c):
            fn((odd + n) % 2)
            return c

        lax.fori_loop(0, 2, body, 0)

    def first_plane(x):
        post, _ = collide([pop[i, x] for i in range(19)], kind_ref[x])
        keep_post(post, x, 0)

    def middle_plane(slot, x):
        kind = kind_ref[x]
        post, u = collide(streamed(slot, x), kind)
        keep_speeds(u, kind, x)
        keep_post(post, x, slot + 1)

    def keep_parts(f, kind, x):
        density, totals = sums(f)
        parts[x, 0] = jnp.where(kind == 1, 1.0, density)
        for c in range(3):
            parts[x, c + 1] = jnp.where(kind == 1, 0.0, totals[c])

    def last_plane(slot, x, keep):
        kind = kind_ref[x]
        f = streamed(slot, x)
        if keep:
            keep_parts(f, kind, x)
        for i in range(19):
            field[i, x] = jnp.where(kind == 1, pop[i, x], f[i])

    def edge_parts(slot, x):
        f = [None] * 19
        for n, i in enumerate(REST):
            if i == 0:
                f[0] = rest[slot, x, 0]
                continue
            source = shifted(rest[slot, x, n], i)
            f[i] = jnp.where(source >= 0.5 * BIG, rest[slot, x, REST.index(OPP[i])], source)
        for n, i in enumerate(EAST):
            back = west[slot, x + 1, WEST.index(OPP[i])]
            if x == 0:
                f[i] = jnp.where(shifted(east[slot - 1, 0, n], i) >= 0.5 * BIG, back, 0.0)
            else:
                source = shifted(east[slot, x, n], i)
                f[i] = jnp.where(source >= 0.5 * BIG, back, source)
        for n, i in enumerate(WEST):
            back = east[slot, x + 1, EAST.index(OPP[i])]
            if x == CX - 1:
                f[i] = jnp.where(shifted(west[slot - 1, CX + 1, n], i) >= 0.5 * BIG, back, 0.0)
            else:
                source = shifted(west[slot, x + 2, n], i)
                f[i] = jnp.where(source >= 0.5 * BIG, back, source)
        keep_parts(f, kind_ref[x], x)

    def out_parts(planes, dirs, wall):
        total = [jnp.zeros((NY, NZ), jnp.float32)] * 4
        for n, i in enumerate(dirs):
            source = planes[n]
            value = shifted(jnp.where(source >= 0.5 * BIG, 0.0, source), i)
            total[0] = total[0] + value
            for axis in range(3):
                if DIRS[i][axis] == 1:
                    total[axis + 1] = total[axis + 1] + value
                elif DIRS[i][axis] == -1:
                    total[axis + 1] = total[axis + 1] - value
        return [jnp.where(wall, 0.0, value) for value in total]

    def pair(fn):
        def body(n, c):
            fn(n)
            return c

        lax.fori_loop(0, 2, body, 0)

    @pl.when(channel)
    def _():
        @pl.when(has_east)
        def _():
            hello(east_id)

        @pl.when(has_west)
        def _():
            hello(west_id)

        for d in FAR_ALL:
            hello((3, zpos * NPLANE + (ppos + d) % NPLANE))

        samples[...] = jnp.zeros((2, 4, NZ), jnp.float32)
        ends[...] = jnp.zeros((3, 4, NZ), jnp.float32)

        @pl.when(position == 0)
        def _():
            east[:, 0] = jnp.full((STEPS, 5, NY, NZ), BIG, jnp.float32)

        @pl.when(position == 383)
        def _():
            west[:, CX + 1] = jnp.full((STEPS, 5, NY, NZ), BIG, jnp.float32)

        for n in (0, 6, 1):
            loads[n].wait()
        sides(lambda side: first_plane(3 * side))
        edge = jnp.logical_or(position == 0, position == 383)

        @pl.when(edge)
        def _():
            pl.semaphore_wait(barrier, 1)

        @pl.when(jnp.logical_not(edge))
        def _():
            pl.semaphore_wait(barrier, 2)

        sides(lambda side: send_side(0, side))
        loads[7].wait()
        pair(lambda n: first_plane(1 + n))
        loads[2].wait()

        lanes = lax.broadcasted_iota(jnp.int32, (NZ, NZ), 1)
        depth = lax.broadcasted_iota(jnp.int32, (NZ, NZ), 0)
        pick_z = (depth == phase[2] + SUB * (lanes % 32)).astype(jnp.float32)
        lane3 = lax.broadcasted_iota(jnp.int32, (3, NY, NZ), 2)
        row3 = lax.broadcasted_iota(jnp.int32, (3, NY, NZ), 1)
        pick_y = row3 == phase[1] + SUB * (lane3 // 32)

        def sample(step):
            plane = speeds[phase[0]].reshape(3 * NY, NZ)
            along = mm(plane, pick_z, ((1,), (0,))).reshape(3, NY, NZ)
            samples[step, 0:3] = jnp.sum(jnp.where(pick_y, along, 0.0), axis=1)

        def to_analysis(source, target, n):
            for d in FAR_ALL:
                push(source, target.at[group * NPLANE + ppos], (3, zpos * NPLANE + (ppos + d) % NPLANE), n)

        def one_step(slot, c, sampled=True):
            pair(lambda n: middle_plane(slot, 1 + n))

            def one_side(side):
                take_side(slot, side)
                middle_plane(slot, 3 * side)
                send_side(slot + 1, side)

            sides(one_side)
            if sampled:
                sample(slot)
            return c

        lax.fori_loop(0, 2, one_step, 0)
        pl.semaphore_wait(go_sem, 8)
        to_analysis(samples.at[0:2], landed_a, ROUTE_A)
        one_step(2, 0, sampled=False)
        last = STEPS - 1
        edge_parts(last, 0)
        edge_parts(last, CX - 1)
        to_east = out_parts([east[last, CX, n] for n in range(5)], EAST, west[last - 1, CX + 1, 0] >= 0.5 * BIG)
        to_west = out_parts([west[last, 1, n] for n in range(5)], WEST, east[last - 1, 0, 0] >= 0.5 * BIG)
        for c in range(4):
            across[c] = jnp.where(phase[0] == 0, to_east[c], jnp.where(phase[0] == CX - 1, to_west[c], 0.0))
        pair(lambda n: last_plane(last, 1 + n, True))
        lane11 = lax.broadcasted_iota(jnp.int32, (11, NY, NZ), 2)
        row11 = lax.broadcasted_iota(jnp.int32, (11, NY, NZ), 1)
        stack = [speeds[phase[0]].reshape(3 * NY, NZ), parts[phase[0]].reshape(4 * NY, NZ)]
        stack = jnp.concatenate(stack + [across[...].reshape(4 * NY, NZ)], axis=0)
        along = mm(stack, pick_z, ((1,), (0,))).reshape(11, NY, NZ)
        chosen = jnp.sum(jnp.where(row11 == phase[1] + SUB * (lane11 // 32), along, 0.0), axis=1)
        ends[0, 0:3] = chosen[0:3]
        ends[1] = chosen[3:7]
        ends[2] = chosen[7:11]
        to_analysis(ends, landed_b, ROUTE_B)

        def last_side(side):
            take_side(last, side)
            last_plane(last, 3 * side, False)

        sides(last_side)
        stores[0].start()

        def sent(slot, c):
            go_east, go_west = halo(slot)

            @pl.when(has_east)
            def _():
                go_east.wait_send()

            @pl.when(has_west)
            def _():
                go_west.wait_send()

            return c

        lax.fori_loop(0, STEPS, sent, 0)
        left_here(landed_a.at[0:8], ROUTE_A)
        left_here(landed_b.at[0:8], ROUTE_B)
        stores[0].wait()

    @pl.when(jnp.logical_not(channel))
    def _():
        for d in LINE_FAR:
            hello(line_peer(d))
        for d in PLANE_FAR:
            hello(plane_peer(d))

        square[...] = jnp.zeros((RANK, RANK), jnp.float32)
        loads[5].wait()
        square[0:MODES, 0:MODES] = mm(modes[...], modes[...], ((0,), (0,)))
        for p in range(NPLANE):
            for z in range(NLINE):
                down, across = 32 * p + 4 * (z // 2), 128 * (z % 2)
                pack[p, z] = square[down : down + 4, across : across + 128]
        pl.semaphore_wait(barrier, 15 + 7 + 24)

        slot_a[ppos] = pack[ppos]
        for d in PLANE_FAR:
            push(pack.at[(ppos + d) % NPLANE], slot_a.at[ppos], plane_peer(d), GRAM_A)

        for n in range(24):
            pl.semaphore_signal(
                go_sem,
                inc=1,
                device_id=(n // NPLANE, zpos * NPLANE + (ppos + n) % NPLANE),
                device_id_type=MESH,
            )

        loads[3].wait()
        loads[2].wait()

        def shift(n, c):
            home = (n // NPLANE) * 128 + zpos * NPLANE + n % NPLANE
            there = home + jnp.where(phase[0] == 0, 1, -1)
            inside = jnp.logical_and(there >= 0, there < 384)
            used = jnp.logical_and(inside, jnp.logical_or(phase[0] == 0, phase[0] == CX - 1))
            rows_next[n] = jnp.where(used, table[jnp.minimum(jnp.maximum(there, 0), 383)], -1)
            return c

        lax.fori_loop(0, 24, shift, 0)

        def pick(n, c):
            found = jnp.int32(-1)
            found_next = jnp.int32(-1)
            wanted = 24 * (n // 3) + 3 * ppos + n % 3
            for g in range(3):
                for p in range(NPLANE):
                    row = table[g * 128 + zpos * NPLANE + p]
                    found = jnp.where(row == wanted, g * NPLANE + p, found)
                    row_next = rows_next[g * NPLANE + p]
                    found_next = jnp.where(row_next == wanted, g * NPLANE + p, found_next)
            picks[n] = found
            picks_next[n] = found_next
            return c

        lax.fori_loop(0, 48, pick, 0)

        def forward(landed, ready, got, from_sem, to_sem, split=False):
            arrived(landed, from_sem)

            def place(n, c):
                source = picks[n]
                if split:
                    other = picks_next[n]
                    mine = jnp.maximum(source, 0)
                    ready[n, 0] = jnp.where(source >= 0, landed[mine, 0], 0.0)
                    own = jnp.where(source >= 0, landed[mine, 1], 0.0)
                    ready[n, 1] = own + jnp.where(other >= 0, landed[jnp.maximum(other, 0), 2], 0.0)
                else:
                    ready[n] = jnp.where(source >= 0, landed[jnp.maximum(source, 0)], 0.0)
                return c

            lax.fori_loop(0, 48, place, 0)
            got[zpos] = ready[pl.ds(3 * zpos, 3)]
            for d in LINE_FAR:
                push(ready.at[pl.ds(3 * ((zpos + d) % NLINE), 3)], got.at[zpos], line_peer(d), to_sem)

        arrived(slot_a.at[0:7], GRAM_A)
        rows_a[...] = jnp.sum(slot_a[...], axis=0)
        slot_b[zpos] = rows_a[zpos]
        for d in LINE_FAR:
            push(rows_a.at[(zpos + d) % NLINE], slot_b.at[zpos], line_peer(d), GRAM_B)
        arrived(slot_b.at[0:15], GRAM_B)
        rows_b[...] = jnp.sum(slot_b[...], axis=0)
        column[zpos] = rows_b[...]
        to_line(rows_b, column.at[zpos], GRAM_C)
        forward(landed_a, ready_a, got_a, ROUTE_A, LINE_A)
        arrived(column.at[0:15], GRAM_C)
        gram[ppos] = column[...]
        to_plane(column, gram.at[ppos], GRAM_D)
        forward(landed_b, ready_b, got_b, ROUTE_B, LINE_B, split=True)
        arrived(gram.at[0:7], GRAM_D)
        for p in range(NPLANE):
            for z in range(NLINE):
                down, across = 32 * p + 4 * (z // 2), 128 * (z % 2)
                square[down : down + 4, across : across + 128] = gram[p, z]
        stores[1].start()

        row, col, eye = square_iota()
        matrix, rs_row, _ = unit_diagonal(square[...])
        scaled[...] = matrix
        lower = lower_half(matrix - eye, row, col)
        upper = (matrix - eye) - lower
        mixed = quick(lower, matrix - eye, ((1,), (0,)))
        second = lower_half(quick(mixed - upper, upper, ((1,), (0,))) - mixed, row, col)
        inverse[...] = eye - lower - second + quick(second, lower, ((1,), (0,)))
        here = inverse[...]
        error = mm(mm(here, scaled[...], ((1,), (0,))), here, ((1,), (1,))) - eye
        inverse[...] = here - quick(lower_half(error, row, col), here, ((1,), (0,)))
        size = jnp.sum(jnp.sum(error * error, axis=0, keepdims=True), axis=1, keepdims=True)
        good = jnp.broadcast_to(size < 1e-6, (RANK, RANK))
        factor = jnp.where(good, inverse[...], eye) * rs_row
        inverse[...] = factor * SCALE
        q[...] = mm(modes[...], inverse[:, 0:MODES], ((1,), (1,)))
        stores[2].start()
        loads[4].wait()
        small[...] = jnp.zeros((4, 8, NZ), jnp.float32)
        small[0] = jnp.broadcast_to(size, (8, NZ))
        for k in range(4):
            small[0, k + 1 : k + 2] = jnp.full((1, NZ), 1.0, jnp.float32) * order[k].astype(jnp.float32)

        arrived(got_a.at[0:15], LINE_A)
        final[...] = jnp.zeros((NZ, NZ), jnp.float32)
        sum_a = jnp.sum(got_a[...], axis=0)
        for t in range(3):
            for s in range(2):
                final[16 * s + 4 * t : 16 * s + 4 * t + 4] = sum_a[t, s]
        arrived(got_b.at[0:15], LINE_B)
        sum_b = jnp.sum(got_b[...], axis=0)
        for t in range(3):
            final[32 + 4 * t : 36 + 4 * t] = sum_b[t, 0]
            final[48 + 4 * t : 51 + 4 * t] = sum_b[t, 1, 1:4] / sum_b[t, 1, 0:1]
        tall = final[...].T
        lane = lax.broadcasted_iota(jnp.int32, (NZ, NZ), 1)
        low_sum = [jnp.zeros((8, NZ), jnp.float32) for _ in range(STEPS)]
        high_sum = [jnp.zeros((8, NZ), jnp.float32) for _ in range(STEPS)]
        for n in range(9):
            block = pl.ds(128 * n, 128)
            spot = 4 * (n // 3) + n % 3
            wide = []
            for s in range(STEPS):
                wide.append(jnp.broadcast_to(tall[:, 16 * s + spot : 16 * s + spot + 1], (NZ, NZ)))
            low = q[block, 0:128]
            high = q[block, 128:RANK]
            for s in range(STEPS):
                high = jnp.where(lane == 124 + s, wide[s], high)
            q[block, 128:RANK] = high
            for s in range(STEPS):
                low_sum[s] = low_sum[s] + jnp.sum((wide[s] * low).reshape(16, 8, NZ), axis=0)
                high_sum[s] = high_sum[s] + jnp.sum((wide[s] * high).reshape(16, 8, NZ), axis=0)
        for s in range(STEPS):
            cross_own[s : s + 1] = jnp.sum(low_sum[s], axis=0, keepdims=True)
            cross_own[s + 4 : s + 5] = jnp.sum(high_sum[s], axis=0, keepdims=True)

        cross_a[zpos] = cross_own[...]
        to_line(cross_own, cross_a.at[zpos], CROSS_A)
        stores[3].start()
        arrived(cross_a.at[0:15], CROSS_A)
        cross_mid[...] = jnp.sum(cross_a[...], axis=0)
        cross_b[ppos] = cross_mid[...]
        to_plane(cross_mid, cross_b.at[ppos], CROSS_B)
        arrived(cross_b.at[0:7], CROSS_B)
        both = jnp.sum(cross_b[...], axis=0)
        small[1] = both
        lines = [jnp.concatenate([both[s : s + 1], both[s + 4 : s + 5]], axis=1) for s in range(4)]
        for k, tail in enumerate(last_columns(lines, lambda k, s: order[k] == s)):
            small[2, k : k + 1] = tail[:, 0:128]
            small[3, k : k + 1] = tail[:, 128:RANK]
        stores[4].start()

        left_here(slot_a.at[0:7], GRAM_A)
        left_here(slot_b.at[0:15], GRAM_B)
        left_here(column.at[0:15], GRAM_C)
        left_here(gram.at[0:7], GRAM_D)
        left_here(got_a.at[0:15], LINE_A)
        left_here(got_b.at[0:15], LINE_B)
        left_here(cross_a.at[0:15], CROSS_A)
        left_here(cross_b.at[0:7], CROSS_B)
        for n in range(1, 5):
            stores[n].wait()


def second_kernel(
    modes_hbm, field, gram_hbm, q_hbm, small_hbm, lattice, basis, passing, q, small, ends, blank, modes, gram, left, inverse, pivots, sem
):
    group = lax.axis_index("group")

    @pl.when(group < 3)
    def _():
        load = pltpu.make_async_copy(field, passing, sem.at[0])
        load.start()
        q[...] = jnp.zeros((ROWS_DEV, RANK), jnp.float32)
        clear = pltpu.make_async_copy(q, basis, sem.at[1])
        clear.start()
        load.wait()
        store = pltpu.make_async_copy(passing, lattice, sem.at[2])
        store.start()
        store.wait()
        clear.wait()

    @pl.when(group == 3)
    def _():
        load_q = pltpu.make_async_copy(q_hbm, q, sem.at[0])
        load_small = pltpu.make_async_copy(small_hbm, small, sem.at[1])
        load_q.start()
        load_small.start()
        blank[...] = jnp.zeros((CX, NY, NZ), jnp.float32)
        clears = [pltpu.make_async_copy(blank, lattice.at[n], sem.at[4 + n]) for n in range(19)]
        for clear in clears:
            clear.start()
        lane = lax.broadcasted_iota(jnp.int32, (ROWS_DEV, 128), 1)
        load_small.wait()
        load_q.wait()

        @pl.when(jnp.logical_not(small[0, 0, 0] < 1e-6))
        def _():
            load = pltpu.make_async_copy(modes_hbm, modes, sem.at[2])
            load.start()
            load_gram = pltpu.make_async_copy(gram_hbm, gram, sem.at[3])
            load_gram.start()
            load_gram.wait()
            row, col, eye = square_iota()
            matrix, rs_row, diagonal = unit_diagonal(gram[...])
            left[...] = matrix
            inverse[...] = eye
            pivots[...] = jnp.ones((RANK, 128), jnp.float32)

            def eliminate(j, c):
                line = left[pl.ds(j, 1), :]
                mine = inverse[pl.ds(j, 1), :]
                along = lax.broadcasted_iota(jnp.int32, (1, RANK), 1)
                pivot = jnp.sum(jnp.where(along == j, line, 0.0), axis=1, keepdims=True)
                column = jnp.sum(jnp.where(col == j, left[...], 0.0), axis=1, keepdims=True)
                below = lax.broadcasted_iota(jnp.int32, (RANK, 1), 0) > j
                factor = jnp.where(below, column / pivot, 0.0)
                left[...] = left[...] - factor * line
                inverse[...] = inverse[...] - factor * mine
                pivots[pl.ds(j, 1), :] = jnp.broadcast_to(pivot, (1, 128))
                return c

            lax.fori_loop(0, RANK, eliminate, 0)
            inverse[...] = inverse[...] / jnp.sqrt(pivots[:, 0:1]) * rs_row
            raw = jnp.concatenate([small[1, 0:4], small[1, 4:8]], axis=1)
            along = lax.broadcasted_iota(jnp.int32, (4, RANK), 1)
            old = jnp.where(along < MODES, raw * jnp.sqrt(diagonal), 0.0)
            old = jnp.concatenate([old, jnp.zeros((4, RANK), jnp.float32)], axis=0)
            fresh = mm(old, inverse[...], ((1,), (1,)))[0:4]
            fresh = jnp.where(along < MODES, fresh, raw)

            def is_step(k, s):
                return small[0, k + 1 : k + 2, 0:1] == float(s)

            rows = last_columns([fresh[s : s + 1] for s in range(4)], is_step)
            for k in range(4):
                small[2, k : k + 1] = rows[k][:, 0:128]
                small[3, k : k + 1] = rows[k][:, 128:RANK]
            load.wait()
            inverse[...] = inverse[...] * SCALE
            whole = mm(modes[...], inverse[:, 0:MODES], ((1,), (1,)))
            wide = lax.broadcasted_iota(jnp.int32, (ROWS_DEV, RANK), 1)
            q[...] = jnp.where(wide < MODES, whole, q[...])

        first = pltpu.make_async_copy(q.at[:, 0:128], basis.at[:, 0:128], sem.at[0])
        first.start()
        rows = jnp.concatenate([small[2, 0:4], small[3, 0:4]], axis=1)
        rows = jnp.concatenate([jnp.zeros((124, RANK), jnp.float32), rows], axis=0)
        ends[...] = jnp.where(lane < 124, q[:, 128:RANK], mm(q[...], rows, ((1,), (1,))))
        second = pltpu.make_async_copy(ends, basis.at[:, 128:RANK], sem.at[1])
        second.start()
        for clear in clears:
            clear.wait()
        first.wait()
        second.wait()


def local(populations, cell_kind, snapshot_order, sample_phase, slab_map, weighted_modes):
    f32 = jnp.float32
    hbm = pl.BlockSpec(memory_space=pltpu.HBM)
    dma = pltpu.SemaphoreType.DMA

    def buffer(*shape):
        return pltpu.VMEM(shape, f32)

    field, gram, q, small = pl.pallas_call(
        first_kernel,
        out_shape=(
            jax.ShapeDtypeStruct((19, CX, NY, NZ), f32),
            jax.ShapeDtypeStruct((RANK, RANK), f32),
            jax.ShapeDtypeStruct((ROWS_DEV, RANK), f32),
            jax.ShapeDtypeStruct((4, 8, NZ), f32),
        ),
        in_specs=[hbm] * 6,
        out_specs=(hbm,) * 4,
        scratch_shapes=[
            buffer(19, CX, NY, NZ),
            buffer(NPLANE, NLINE, 4, NZ),
            buffer(ROWS_DEV, RANK),
            buffer(4, 8, NZ),
            buffer(19, CX, NY, NZ),
            pltpu.VMEM((CX, NY, NZ), jnp.int32),
            pltpu.SMEM((3,), jnp.int32),
            pltpu.SMEM((4,), jnp.int32),
            pltpu.SMEM((384,), jnp.int32),
            buffer(ROWS_DEV, MODES),
            buffer(STEPS, CX + 2, 5, NY, NZ),
            buffer(STEPS, CX + 2, 5, NY, NZ),
            buffer(STEPS, CX, 9, NY, NZ),
            buffer(CX, 3, NY, NZ),
            buffer(2, 4, NZ),
            buffer(CX, 4, NY, NZ),
            buffer(4, NY, NZ),
            buffer(3, 4, NZ),
            buffer(NZ, NZ),
            pltpu.SMEM((48,), jnp.int32),
            pltpu.SMEM((48,), jnp.int32),
            pltpu.SMEM((24,), jnp.int32),
            buffer(24, 2, 4, NZ),
            buffer(24, 3, 4, NZ),
            buffer(48, 2, 4, NZ),
            buffer(48, 2, 4, NZ),
            buffer(NLINE, 3, 2, 4, NZ),
            buffer(NLINE, 3, 2, 4, NZ),
            buffer(NPLANE, NLINE, 4, NZ),
            buffer(NPLANE, NLINE, 4, NZ),
            buffer(NLINE, 4, NZ),
            buffer(NLINE, 4, NZ),
            buffer(4, NZ),
            buffer(NLINE, 4, NZ),
            buffer(RANK, RANK),
            buffer(RANK, RANK),
            buffer(RANK, RANK),
            buffer(8, NZ),
            buffer(NLINE, 8, NZ),
            buffer(8, NZ),
            buffer(NPLANE, 8, NZ),
            dma((8,)),
            dma((5,)),
            dma((STEPS, 2)),
            dma((STEPS, 2)),
            dma((10,)),
            dma((10,)),
            pltpu.SemaphoreType.REGULAR,
        ],
        compiler_params=pltpu.CompilerParams(
            collective_id=0, has_side_effects=True, vmem_limit_bytes=ROOM
        ),
    )(populations, cell_kind, sample_phase, snapshot_order, slab_map, weighted_modes)
    return pl.pallas_call(
        second_kernel,
        out_shape=(
            jax.ShapeDtypeStruct((19, CX, NY, NZ), f32),
            jax.ShapeDtypeStruct((ROWS_DEV, RANK), f32),
        ),
        in_specs=[hbm] * 5,
        out_specs=(hbm, hbm),
        scratch_shapes=[
            buffer(19, CX, NY, NZ),
            buffer(ROWS_DEV, RANK),
            buffer(4, 8, NZ),
            buffer(ROWS_DEV, 128),
            buffer(CX, NY, NZ),
            buffer(ROWS_DEV, MODES),
            buffer(RANK, RANK),
            buffer(RANK, RANK),
            buffer(RANK, RANK),
            buffer(RANK, 128),
            dma((4 + 19,)),
        ],
        compiler_params=pltpu.CompilerParams(vmem_limit_bytes=ROOM),
    )(weighted_modes, field, gram, q, small)


def solution(mesh):
    return jax.shard_map(
        local,
        mesh=mesh,
        in_specs=(
            P(None, ("group", "slab"), None, None),
            P(("group", "slab"), None, None),
            P(),
            P(),
            P(),
            P(("group", "slab"), None),
        ),
        out_specs=(P(None, ("group", "slab"), None, None), P(("group", "slab"), None)),
        check_vma=False,
    )
```

```python
import functools
import math

import jax
import jax.numpy as jnp
from jax import lax
from jax.experimental import pallas as pl
from jax.experimental.pallas import tpu as pltpu
from jax.sharding import PartitionSpec as P

MESH = pl.DeviceIdType.MESH
STEPS = 4
SUB = 4
OMEGA = 0.9
INLET = 0.05
BIG = 1e30

DIRS = [
    (0, 0, 0),
    (1, 0, 0),
    (-1, 0, 0),
    (0, 1, 0),
    (0, -1, 0),
    (0, 0, 1),
    (0, 0, -1),
    (1, 1, 0),
    (-1, -1, 0),
    (1, -1, 0),
    (-1, 1, 0),
    (1, 0, 1),
    (-1, 0, -1),
    (1, 0, -1),
    (-1, 0, 1),
    (0, 1, 1),
    (0, -1, -1),
    (0, 1, -1),
    (0, -1, 1),
]
WEIGHTS = [1.0 / 3.0] + [1.0 / 18.0] * 6 + [1.0 / 36.0] * 12
OPP = [0, 2, 1, 4, 3, 6, 5, 8, 7, 10, 9, 12, 11, 14, 13, 16, 15, 18, 17]
EAST = [i for i in range(19) if DIRS[i][0] == 1]
WEST = [i for i in range(19) if DIRS[i][0] == -1]
REST = [i for i in range(19) if DIRS[i][0] == 0]

CX, NY, NZ = 4, 16, 128
NLINE = 16
NPLANE = 8
RANK = 256
MODES = 252
ROWS_DEV = 1152
ROWS_ALL = 128 * ROWS_DEV
SCALE = math.sqrt(ROWS_ALL)
PIECES = 1
ROOM = 60 * 1024 * 1024
LINE_FAR = [8, 7, 9, 6, 10, 5, 11, 4, 12, 3, 13, 2, 14, 1, 15]
PLANE_FAR = [4, 5, 3, 6, 2, 7, 1]
FAR_ALL = PLANE_FAR + [0]


def mm(a, b, dims):
    return lax.dot_general(
        a,
        b,
        (dims, ((), ())),
        precision=lax.Precision.HIGHEST,
        preferred_element_type=jnp.float32,
    )


def quick(a, b, dims):
    return lax.dot_general(
        a.astype(jnp.bfloat16),
        b.astype(jnp.bfloat16),
        (dims, ((), ())),
        preferred_element_type=jnp.float32,
    )


def inflow_value(i):
    along = DIRS[i][0] * INLET
    return WEIGHTS[i] * (1.0 + 3.0 * along + 4.5 * along * along - 1.5 * INLET * INLET)


def sums(f):
    density = f[0]
    for i in range(1, 19):
        density = density + f[i]
    totals = []
    for axis in range(3):
        plus = [f[i] for i in range(19) if DIRS[i][axis] == 1]
        minus = [f[i] for i in range(19) if DIRS[i][axis] == -1]
        totals.append(functools.reduce(lambda a, b: a + b, [a - b for a, b in zip(plus, minus)]))
    return density, totals


def moments(f):
    density, totals = sums(f)
    inverse = 1.0 / density
    return density, [total * inverse for total in totals]


def collide(f, kind):
    density, u = moments(f)
    square = 1.0 - 1.5 * (u[0] * u[0] + u[1] * u[1] + u[2] * u[2])
    fluid = kind == 0
    inlet = kind == 2
    scaled = {w: (OMEGA * w) * density for w in (1.0 / 3.0, 1.0 / 18.0, 1.0 / 36.0)}
    fallback = {}
    post = [None] * 19
    for i in range(19):
        value = inflow_value(i)
        if value not in fallback:
            fallback[value] = jnp.where(inlet, value, BIG)
    for i in range(19):
        if post[i] is not None:
            continue
        w = scaled[WEIGHTS[i]]
        if i == 0:
            post[0] = jnp.where(fluid, (1.0 - OMEGA) * f[0] + w * square, fallback[inflow_value(0)])
            continue
        along = None
        for axis in range(3):
            if DIRS[i][axis] != 0:
                term = u[axis] if DIRS[i][axis] == 1 else -u[axis]
                along = term if along is None else along + term
        even = w * (square + 4.5 * along * along)
        odd = w * (3.0 * along)
        j = OPP[i]
        post[i] = jnp.where(fluid, (1.0 - OMEGA) * f[i] + (even + odd), fallback[inflow_value(i)])
        post[j] = jnp.where(fluid, (1.0 - OMEGA) * f[j] + (even - odd), fallback[inflow_value(j)])
    return post, u


def shifted(plane, i):
    _, north, upward = DIRS[i]
    if north:
        plane = pltpu.roll(plane, north % NY, 0)
    if upward:
        plane = pltpu.roll(plane, upward % NZ, 1)
    return plane


def lower_half(error, row, col):
    return jnp.where(row > col, error, jnp.where(row == col, 0.5 * error, 0.0))


def square_iota():
    row = lax.broadcasted_iota(jnp.int32, (RANK, RANK), 0)
    col = lax.broadcasted_iota(jnp.int32, (RANK, RANK), 1)
    return row, col, (row == col).astype(jnp.float32)


def unit_diagonal(gram):
    row, col, _ = square_iota()
    whole = jnp.where(jnp.logical_and(row == col, row >= MODES), 1.0, gram)
    diagonal = jnp.where(row == col, whole, 0.0)
    along_row = jnp.sum(diagonal, axis=0, keepdims=True)
    rs_row = 1.0 / jnp.sqrt(along_row)
    rs_col = 1.0 / jnp.sqrt(jnp.sum(diagonal, axis=1, keepdims=True))
    return whole * rs_row * rs_col, rs_row, along_row


def last_columns(lines, is_step):
    lane = lax.broadcasted_iota(jnp.int32, (1, RANK), 1)
    old = [jnp.where(lane < MODES, line, 0.0) for line in lines]
    gram = [[None] * 4 for _ in range(4)]
    for s in range(4):
        for t in range(s + 1):
            own = jnp.where(lane == MODES + t, lines[s], 0.0)
            gram[s][t] = jnp.sum(own - old[s] * old[t] * (1.0 / ROWS_ALL), axis=1, keepdims=True)
            gram[t][s] = gram[s][t]

    def chosen(k, values):
        result = values[3]
        for s in range(3):
            result = jnp.where(is_step(k, s), values[s], result)
        return result

    half = [[chosen(k, [gram[s][t] for s in range(4)]) for t in range(4)] for k in range(4)]
    entry = [[chosen(j, half[k]) for j in range(k + 1)] for k in range(4)]
    start = []
    for s in range(4):
        start.append(SCALE * (lane == MODES + s).astype(jnp.float32) - old[s] * (SCALE / ROWS_ALL))
    low = [[None] * 4 for _ in range(4)]
    over = [None] * 4
    result = []
    for k in range(4):
        for j in range(k + 1):
            value = entry[k][j]
            for m in range(j):
                value = value - low[k][m] * low[j][m]
            if k == j:
                over[k] = 1.0 / jnp.sqrt(value)
            else:
                low[k][j] = value * over[j]
        line = chosen(k, start)
        for m in range(k):
            line = line - low[k][m] * result[m]
        result.append(line * over[k])
    return result


def first_kernel(
    pop_hbm,
    kind_hbm,
    phase_hbm,
    order_hbm,
    table_hbm,
    modes_hbm,
    field_hbm,
    gram_hbm,
    q_hbm,
    small_hbm,
    field,
    gram,
    q,
    small,
    pop,
    kind_ref,
    phase,
    order,
    table,
    modes,
    east,
    west,
    rest,
    speeds,
    samples,
    parts,
    across,
    ends,
    final,
    picks,
    picks_next,
    rows_next,
    landed_a,
    landed_b,
    ready_a,
    ready_b,
    got_a,
    got_b,
    pack,
    slot_a,
    rows_a,
    slot_b,
    rows_b,
    column,
    square,
    scaled,
    inverse,
    cross_own,
    cross_a,
    cross_mid,
    cross_b,
    load_sem,
    store_sem,
    halo_send,
    halo_recv,
    send_sem,
    recv_sem,
    go_sem,
):
    group = lax.axis_index("group")
    slab = lax.axis_index("slab")
    zpos = slab // NPLANE
    ppos = slab % NPLANE
    position = group * 128 + slab
    channel = group < 3
    has_west = jnp.logical_and(channel, position > 0)
    has_east = jnp.logical_and(channel, position < 383)
    west_id = ((position - 1) // 128, (position + 127) % 128)
    east_id = ((position + 1) // 128, (position + 1) % 128)
    ROUTE_A, ROUTE_B, LINE_A, LINE_B, GRAM_A, GRAM_B, GRAM_C, GRAM_D, CROSS_A, CROSS_B = range(10)
    odd = slab % 2

    barrier = pltpu.get_barrier_semaphore()

    def hello(target):
        pl.semaphore_signal(barrier, inc=1, device_id=target, device_id_type=MESH)

    loads = [
        pltpu.make_async_copy(a, b, load_sem.at[n])
        for n, (a, b) in enumerate(
            [
                (pop_hbm.at[:, 0], pop.at[:, 0]),
                (kind_hbm, kind_ref),
                (phase_hbm, phase),
                (table_hbm, table),
                (order_hbm, order),
                (modes_hbm, modes),
                (pop_hbm.at[:, CX - 1], pop.at[:, CX - 1]),
                (pop_hbm.at[:, 1 : CX - 1], pop.at[:, 1 : CX - 1]),
            ]
        )
    ]

    stores = [
        pltpu.make_async_copy(a, b, store_sem.at[n])
        for n, (a, b) in enumerate(
            [
                (field, field_hbm),
                (square, gram_hbm),
                (q.at[:, 0:128], q_hbm.at[:, 0:128]),
                (q.at[:, 128:RANK], q_hbm.at[:, 128:RANK]),
                (small, small_hbm),
            ]
        )
    ]

    @pl.when(channel)
    def _():
        for n in (0, 6, 1, 7, 2):
            loads[n].start()

    @pl.when(jnp.logical_not(channel))
    def _():
        loads[5].start()
        loads[4].start()
        loads[3].start()
        loads[2].start()

    def line_peer(d):
        return (group, ((zpos + d) % NLINE) * NPLANE + ppos)

    def plane_peer(d):
        return (3, zpos * NPLANE + (ppos + d) % NPLANE)

    def push(source, target, peer, n):
        pltpu.make_async_remote_copy(
            src_ref=source,
            dst_ref=target,
            send_sem=send_sem.at[n],
            recv_sem=recv_sem.at[n],
            device_id=peer,
            device_id_type=MESH,
        ).start()

    def to_line(source, target, n):
        for d in LINE_FAR:
            push(source, target, line_peer(d), n)

    def to_plane(source, target, n):
        for d in PLANE_FAR:
            push(source, target, plane_peer(d), n)

    def arrived(ref, n):
        pltpu.make_async_copy(ref, ref, recv_sem.at[n]).wait()

    def left_here(ref, n):
        pltpu.make_async_copy(ref, ref, send_sem.at[n]).wait()

    def keep_post(post, x, slot):
        for n, i in enumerate(EAST):
            east[slot, x + 1, n] = post[i]
        for n, i in enumerate(WEST):
            west[slot, x + 1, n] = post[i]
        for n, i in enumerate(REST):
            rest[slot, x, n] = post[i]

    def streamed(slot, x):
        f = [None] * 19
        for n, i in enumerate(REST):
            if i == 0:
                f[0] = rest[slot, x, 0]
                continue
            source = shifted(rest[slot, x, n], i)
            f[i] = jnp.where(source >= 0.5 * BIG, rest[slot, x, REST.index(OPP[i])], source)
        for n, i in enumerate(EAST):
            source = shifted(east[slot, x, n], i)
            f[i] = jnp.where(source >= 0.5 * BIG, west[slot, x + 1, WEST.index(OPP[i])], source)
        for n, i in enumerate(WEST):
            source = shifted(west[slot, x + 2, n], i)
            f[i] = jnp.where(source >= 0.5 * BIG, east[slot, x + 1, EAST.index(OPP[i])], source)
        return f

    def keep_speeds(u, kind, x):
        for c in range(3):
            speeds[x, c] = jnp.where(kind == 1, 0.0, u[c])

    def halo(slot):
        go_east = pltpu.make_async_remote_copy(
            src_ref=east.at[slot, CX],
            dst_ref=east.at[slot, 0],
            send_sem=halo_send.at[slot, 0],
            recv_sem=halo_recv.at[slot, 0],
            device_id=east_id,
            device_id_type=MESH,
        )
        go_west = pltpu.make_async_remote_copy(
            src_ref=west.at[slot, 1],
            dst_ref=west.at[slot, CX + 1],
            send_sem=halo_send.at[slot, 1],
            recv_sem=halo_recv.at[slot, 1],
            device_id=west_id,
            device_id_type=MESH,
        )
        return go_east, go_west

    def send_side(slot, side):
        go_east, go_west = halo(slot)

        @pl.when(jnp.logical_and(has_east, side == 1))
        def _():
            go_east.start()

        @pl.when(jnp.logical_and(has_west, side == 0))
        def _():
            go_west.start()

    def take_side(slot, side):
        go_east, go_west = halo(slot)

        @pl.when(jnp.logical_and(has_east, side == 1))
        def _():
            go_west.wait_recv()

        @pl.when(jnp.logical_and(has_west, side == 0))
        def _():
            go_east.wait_recv()

    def sides(fn):
        def body(n, c):
            fn((odd + n) % 2)
            return c

        lax.fori_loop(0, 2, body, 0)

    def first_plane(x):
        post, _ = collide([pop[i, x] for i in range(19)], kind_ref[x])
        keep_post(post, x, 0)

    def middle_plane(slot, x):
        kind = kind_ref[x]
        post, u = collide(streamed(slot, x), kind)
        keep_speeds(u, kind, x)
        keep_post(post, x, slot + 1)

    def keep_parts(f, kind, x):
        density, totals = sums(f)
        parts[x, 0] = jnp.where(kind == 1, 1.0, density)
        for c in range(3):
            parts[x, c + 1] = jnp.where(kind == 1, 0.0, totals[c])

    def last_plane(slot, x):
        kind = kind_ref[x]
        f = streamed(slot, x)
        for i in range(19):
            field[i, x] = jnp.where(kind == 1, pop[i, x], f[i])

    def edge_parts(slot, x):
        f = [None] * 19
        for n, i in enumerate(REST):
            if i == 0:
                f[0] = rest[slot, x, 0]
                continue
            source = shifted(rest[slot, x, n], i)
            f[i] = jnp.where(source >= 0.5 * BIG, rest[slot, x, REST.index(OPP[i])], source)
        for n, i in enumerate(EAST):
            back = west[slot, x + 1, WEST.index(OPP[i])]
            if x == 0:
                f[i] = jnp.where(shifted(east[slot - 1, 0, n], i) >= 0.5 * BIG, back, 0.0)
            else:
                source = shifted(east[slot, x, n], i)
                f[i] = jnp.where(source >= 0.5 * BIG, back, source)
        for n, i in enumerate(WEST):
            back = east[slot, x + 1, EAST.index(OPP[i])]
            if x == CX - 1:
                f[i] = jnp.where(shifted(west[slot - 1, CX + 1, n], i) >= 0.5 * BIG, back, 0.0)
            else:
                source = shifted(west[slot, x + 2, n], i)
                f[i] = jnp.where(source >= 0.5 * BIG, back, source)
        keep_parts(f, kind_ref[x], x)

    def out_parts(planes, dirs, wall):
        total = [jnp.zeros((NY, NZ), jnp.float32)] * 4
        for n, i in enumerate(dirs):
            source = planes[n]
            value = shifted(jnp.where(source >= 0.5 * BIG, 0.0, source), i)
            total[0] = total[0] + value
            for axis in range(3):
                if DIRS[i][axis] == 1:
                    total[axis + 1] = total[axis + 1] + value
                elif DIRS[i][axis] == -1:
                    total[axis + 1] = total[axis + 1] - value
        return [jnp.where(wall, 0.0, value) for value in total]

    def pair(fn):
        def body(n, c):
            fn(n)
            return c

        lax.fori_loop(0, 2, body, 0)

    @pl.when(channel)
    def _():
        @pl.when(has_east)
        def _():
            hello(east_id)

        @pl.when(has_west)
        def _():
            hello(west_id)

        for d in FAR_ALL:
            hello((3, zpos * NPLANE + (ppos + d) % NPLANE))

        samples[...] = jnp.zeros((2, 4, NZ), jnp.float32)
        ends[...] = jnp.zeros((3, 4, NZ), jnp.float32)

        @pl.when(position == 0)
        def _():
            east[:, 0] = jnp.full((STEPS, 5, NY, NZ), BIG, jnp.float32)

        @pl.when(position == 383)
        def _():
            west[:, CX + 1] = jnp.full((STEPS, 5, NY, NZ), BIG, jnp.float32)

        for n in (0, 6, 1):
            loads[n].wait()
        sides(lambda side: first_plane(3 * side))
        edge = jnp.logical_or(position == 0, position == 383)

        @pl.when(edge)
        def _():
            pl.semaphore_wait(barrier, 1)

        @pl.when(jnp.logical_not(edge))
        def _():
            pl.semaphore_wait(barrier, 2)

        sides(lambda side: send_side(0, side))
        loads[7].wait()
        pair(lambda n: first_plane(1 + n))
        loads[2].wait()

        lanes = lax.broadcasted_iota(jnp.int32, (NZ, NZ), 1)
        depth = lax.broadcasted_iota(jnp.int32, (NZ, NZ), 0)
        pick_z = (depth == phase[2] + SUB * (lanes % 32)).astype(jnp.float32)
        lane3 = lax.broadcasted_iota(jnp.int32, (3, NY, NZ), 2)
        row3 = lax.broadcasted_iota(jnp.int32, (3, NY, NZ), 1)
        pick_y = row3 == phase[1] + SUB * (lane3 // 32)

        def sample(step):
            plane = speeds[phase[0]].reshape(3 * NY, NZ)
            along = mm(plane, pick_z, ((1,), (0,))).reshape(3, NY, NZ)
            samples[step, 0:3] = jnp.sum(jnp.where(pick_y, along, 0.0), axis=1)

        def to_analysis(source, target, n):
            for d in FAR_ALL:
                push(source, target.at[group * NPLANE + ppos], (3, zpos * NPLANE + (ppos + d) % NPLANE), n)

        def one_step(slot, c, sampled=True):
            pair(lambda n: middle_plane(slot, 1 + n))

            def one_side(side):
                take_side(slot, side)
                middle_plane(slot, 3 * side)
                send_side(slot + 1, side)

            sides(one_side)
            if sampled:
                sample(slot)
            return c

        lax.fori_loop(0, 2, one_step, 0)
        pl.semaphore_wait(go_sem, 8)
        to_analysis(samples.at[0:2], landed_a, ROUTE_A)
        one_step(2, 0, sampled=False)
        last = STEPS - 1
        edge_parts(last, 0)
        edge_parts(last, CX - 1)
        to_east = out_parts([east[last, CX, n] for n in range(5)], EAST, west[last - 1, CX + 1, 0] >= 0.5 * BIG)
        to_west = out_parts([west[last, 1, n] for n in range(5)], WEST, east[last - 1, 0, 0] >= 0.5 * BIG)
        for c in range(4):
            across[c] = jnp.where(phase[0] == 0, to_east[c], jnp.where(phase[0] == CX - 1, to_west[c], 0.0))
        for x in range(1, CX - 1):
            keep_parts(streamed(last, x), kind_ref[x], x)
        lane11 = lax.broadcasted_iota(jnp.int32, (11, NY, NZ), 2)
        row11 = lax.broadcasted_iota(jnp.int32, (11, NY, NZ), 1)
        stack = [speeds[phase[0]].reshape(3 * NY, NZ), parts[phase[0]].reshape(4 * NY, NZ)]
        stack = jnp.concatenate(stack + [across[...].reshape(4 * NY, NZ)], axis=0)
        along = mm(stack, pick_z, ((1,), (0,))).reshape(11, NY, NZ)
        chosen = jnp.sum(jnp.where(row11 == phase[1] + SUB * (lane11 // 32), along, 0.0), axis=1)
        ends[0, 0:3] = chosen[0:3]
        ends[1] = chosen[3:7]
        ends[2] = chosen[7:11]
        to_analysis(ends, landed_b, ROUTE_B)

        pair(lambda n: last_plane(last, 1 + n))

        def last_side(side):
            take_side(last, side)
            last_plane(last, 3 * side)

        sides(last_side)
        stores[0].start()

        def sent(slot, c):
            go_east, go_west = halo(slot)

            @pl.when(has_east)
            def _():
                go_east.wait_send()

            @pl.when(has_west)
            def _():
                go_west.wait_send()

            return c

        lax.fori_loop(0, STEPS, sent, 0)
        left_here(landed_a.at[0:8], ROUTE_A)
        left_here(landed_b.at[0:8], ROUTE_B)
        stores[0].wait()

    @pl.when(jnp.logical_not(channel))
    def _():
        for d in LINE_FAR:
            hello(line_peer(d))
        for d in PLANE_FAR:
            hello(plane_peer(d))

        square[...] = jnp.zeros((RANK, RANK), jnp.float32)
        loads[5].wait()
        square[0:MODES, 0:MODES] = mm(modes[...], modes[...], ((0,), (0,)))
        for p in range(NPLANE):
            for z in range(NLINE):
                down, across = 32 * p + 4 * (z // 2), 128 * (z % 2)
                pack[p, z] = square[down : down + 4, across : across + 128]
        pl.semaphore_wait(barrier, 15 + 7 + 24)

        slot_a[ppos] = pack[ppos]
        for d in PLANE_FAR:
            push(pack.at[(ppos + d) % NPLANE], slot_a.at[ppos], plane_peer(d), GRAM_A)

        for n in range(24):
            pl.semaphore_signal(
                go_sem,
                inc=1,
                device_id=(n // NPLANE, zpos * NPLANE + (ppos + n) % NPLANE),
                device_id_type=MESH,
            )

        def forward(landed, ready, got, from_sem, to_sem, split=False):
            arrived(landed, from_sem)

            def place(n):
                source = picks[n]
                if split:
                    other = picks_next[n]
                    mine = jnp.maximum(source, 0)
                    ready[n, 0] = jnp.where(source >= 0, landed[mine, 0], 0.0)
                    own = jnp.where(source >= 0, landed[mine, 1], 0.0)
                    ready[n, 1] = own + jnp.where(other >= 0, landed[jnp.maximum(other, 0), 2], 0.0)
                else:
                    ready[n] = jnp.where(source >= 0, landed[jnp.maximum(source, 0)], 0.0)

            for d in LINE_FAR + [0]:
                first = 3 * ((zpos + d) % NLINE)
                for t in range(3):
                    place(first + t)
                if d:
                    push(ready.at[pl.ds(first, 3)], got.at[zpos], line_peer(d), to_sem)
                else:
                    got[zpos] = ready[pl.ds(first, 3)]

        arrived(slot_a.at[0:7], GRAM_A)
        rows_a[...] = jnp.sum(slot_a[...], axis=0)
        slot_b[zpos] = rows_a[zpos]
        for d in LINE_FAR:
            push(rows_a.at[(zpos + d) % NLINE], slot_b.at[zpos], line_peer(d), GRAM_B)
        loads[3].wait()
        loads[2].wait()

        def shift(n, c):
            home = (n // NPLANE) * 128 + zpos * NPLANE + n % NPLANE
            there = home + jnp.where(phase[0] == 0, 1, -1)
            inside = jnp.logical_and(there >= 0, there < 384)
            used = jnp.logical_and(inside, jnp.logical_or(phase[0] == 0, phase[0] == CX - 1))
            rows_next[n] = jnp.where(used, table[jnp.minimum(jnp.maximum(there, 0), 383)], -1)
            return c

        lax.fori_loop(0, 24, shift, 0)

        def pick(n, c):
            found = jnp.int32(-1)
            found_next = jnp.int32(-1)
            wanted = 24 * (n // 3) + 3 * ppos + n % 3
            for g in range(3):
                for p in range(NPLANE):
                    row = table[g * 128 + zpos * NPLANE + p]
                    found = jnp.where(row == wanted, g * NPLANE + p, found)
                    row_next = rows_next[g * NPLANE + p]
                    found_next = jnp.where(row_next == wanted, g * NPLANE + p, found_next)
            picks[n] = found
            picks_next[n] = found_next
            return c

        lax.fori_loop(0, 48, pick, 0)

        arrived(slot_b.at[0:15], GRAM_B)
        rows_b[...] = jnp.sum(slot_b[...], axis=0)
        column[zpos] = rows_b[...]
        to_line(rows_b, column.at[zpos], GRAM_C)
        forward(landed_a, ready_a, got_a, ROUTE_A, LINE_A)
        arrived(column.at[0:15], GRAM_C)
        gram[ppos] = column[...]
        to_plane(column, gram.at[ppos], GRAM_D)
        forward(landed_b, ready_b, got_b, ROUTE_B, LINE_B, split=True)
        arrived(gram.at[0:7], GRAM_D)
        for p in range(NPLANE):
            for z in range(NLINE):
                down, across = 32 * p + 4 * (z // 2), 128 * (z % 2)
                square[down : down + 4, across : across + 128] = gram[p, z]
        stores[1].start()

        row, col, eye = square_iota()
        matrix, rs_row, _ = unit_diagonal(square[...])
        scaled[...] = matrix
        lower = lower_half(matrix - eye, row, col)
        upper = (matrix - eye) - lower
        mixed = quick(lower, matrix - eye, ((1,), (0,)))
        second = lower_half(quick(mixed - upper, upper, ((1,), (0,))) - mixed, row, col)
        inverse[...] = eye - lower - second + quick(second, lower, ((1,), (0,)))
        here = inverse[...]
        error = mm(mm(here, scaled[...], ((1,), (0,))), here, ((1,), (1,))) - eye
        inverse[...] = here - quick(lower_half(error, row, col), here, ((1,), (0,)))
        size = jnp.sum(jnp.sum(error * error, axis=0, keepdims=True), axis=1, keepdims=True)
        good = jnp.broadcast_to(size < 1e-6, (RANK, RANK))
        factor = jnp.where(good, inverse[...], eye) * rs_row
        inverse[...] = factor * SCALE
        q[...] = mm(modes[...], inverse[:, 0:MODES], ((1,), (1,)))
        stores[2].start()
        loads[4].wait()
        small[...] = jnp.zeros((4, 8, NZ), jnp.float32)
        small[0] = jnp.broadcast_to(size, (8, NZ))
        for k in range(4):
            small[0, k + 1 : k + 2] = jnp.full((1, NZ), 1.0, jnp.float32) * order[k].astype(jnp.float32)

        arrived(got_a.at[0:15], LINE_A)
        final[...] = jnp.zeros((NZ, NZ), jnp.float32)
        sum_a = jnp.sum(got_a[...], axis=0)
        for t in range(3):
            for s in range(2):
                final[16 * s + 4 * t : 16 * s + 4 * t + 4] = sum_a[t, s]
        arrived(got_b.at[0:15], LINE_B)
        sum_b = jnp.sum(got_b[...], axis=0)
        for t in range(3):
            final[32 + 4 * t : 36 + 4 * t] = sum_b[t, 0]
            final[48 + 4 * t : 51 + 4 * t] = sum_b[t, 1, 1:4] / sum_b[t, 1, 0:1]
        tall = final[...].T
        lane = lax.broadcasted_iota(jnp.int32, (NZ, NZ), 1)
        low_sum = [jnp.zeros((8, NZ), jnp.float32) for _ in range(STEPS)]
        high_sum = [jnp.zeros((8, NZ), jnp.float32) for _ in range(STEPS)]
        for n in range(9):
            block = pl.ds(128 * n, 128)
            spot = 4 * (n // 3) + n % 3
            wide = []
            for s in range(STEPS):
                wide.append(jnp.broadcast_to(tall[:, 16 * s + spot : 16 * s + spot + 1], (NZ, NZ)))
            low = q[block, 0:128]
            high = q[block, 128:RANK]
            for s in range(STEPS):
                high = jnp.where(lane == 124 + s, wide[s], high)
            q[block, 128:RANK] = high
            for s in range(STEPS):
                low_sum[s] = low_sum[s] + jnp.sum((wide[s] * low).reshape(16, 8, NZ), axis=0)
                high_sum[s] = high_sum[s] + jnp.sum((wide[s] * high).reshape(16, 8, NZ), axis=0)
        for s in range(STEPS):
            cross_own[s : s + 1] = jnp.sum(low_sum[s], axis=0, keepdims=True)
            cross_own[s + 4 : s + 5] = jnp.sum(high_sum[s], axis=0, keepdims=True)

        cross_a[zpos] = cross_own[...]
        to_line(cross_own, cross_a.at[zpos], CROSS_A)
        stores[3].start()
        arrived(cross_a.at[0:15], CROSS_A)
        cross_mid[...] = jnp.sum(cross_a[...], axis=0)
        cross_b[ppos] = cross_mid[...]
        to_plane(cross_mid, cross_b.at[ppos], CROSS_B)
        arrived(cross_b.at[0:7], CROSS_B)
        both = jnp.sum(cross_b[...], axis=0)
        small[1] = both
        lines = [jnp.concatenate([both[s : s + 1], both[s + 4 : s + 5]], axis=1) for s in range(4)]
        for k, tail in enumerate(last_columns(lines, lambda k, s: order[k] == s)):
            small[2, k : k + 1] = tail[:, 0:128]
            small[3, k : k + 1] = tail[:, 128:RANK]
        stores[4].start()

        left_here(slot_a.at[0:7], GRAM_A)
        left_here(slot_b.at[0:15], GRAM_B)
        left_here(column.at[0:15], GRAM_C)
        left_here(gram.at[0:7], GRAM_D)
        left_here(got_a.at[0:15], LINE_A)
        left_here(got_b.at[0:15], LINE_B)
        left_here(cross_a.at[0:15], CROSS_A)
        left_here(cross_b.at[0:7], CROSS_B)
        for n in range(1, 5):
            stores[n].wait()


def second_kernel(
    modes_hbm, field, gram_hbm, q_hbm, small_hbm, lattice, basis, passing, q, small, ends, modes, gram, left, inverse, pivots, sem
):
    group = lax.axis_index("group")

    @pl.when(group < 3)
    def _():
        load = pltpu.make_async_copy(field, passing, sem.at[0])
        load.start()
        q[...] = jnp.zeros((ROWS_DEV, RANK), jnp.float32)
        clear = pltpu.make_async_copy(q, basis, sem.at[1])
        clear.start()
        load.wait()
        store = pltpu.make_async_copy(passing, lattice, sem.at[2])
        store.start()
        store.wait()
        clear.wait()

    @pl.when(group == 3)
    def _():
        load_small = pltpu.make_async_copy(small_hbm, small, sem.at[0])
        load_small.start()
        blocks = [pl.ds(n * (ROWS_DEV // PIECES), ROWS_DEV // PIECES) for n in range(PIECES)]
        loads = [
            pltpu.make_async_copy(q_hbm.at[block], q.at[block], sem.at[4 + n]) for n, block in enumerate(blocks)
        ]
        for load in loads:
            load.start()
        passing[...] = jnp.zeros((19, CX, NY, NZ), jnp.float32)
        clear = pltpu.make_async_copy(passing, lattice, sem.at[1])
        load_small.wait()
        good = small[0, 0, 0] < 1e-6

        @pl.when(jnp.logical_not(good))
        def _():
            for load in loads:
                load.wait()
            load = pltpu.make_async_copy(modes_hbm, modes, sem.at[2])
            load.start()
            load_gram = pltpu.make_async_copy(gram_hbm, gram, sem.at[3])
            load_gram.start()
            load_gram.wait()
            row, col, eye = square_iota()
            matrix, rs_row, diagonal = unit_diagonal(gram[...])
            left[...] = matrix
            inverse[...] = eye
            pivots[...] = jnp.ones((RANK, 128), jnp.float32)

            def eliminate(j, c):
                line = left[pl.ds(j, 1), :]
                mine = inverse[pl.ds(j, 1), :]
                along = lax.broadcasted_iota(jnp.int32, (1, RANK), 1)
                pivot = jnp.sum(jnp.where(along == j, line, 0.0), axis=1, keepdims=True)
                column = jnp.sum(jnp.where(col == j, left[...], 0.0), axis=1, keepdims=True)
                below = lax.broadcasted_iota(jnp.int32, (RANK, 1), 0) > j
                factor = jnp.where(below, column / pivot, 0.0)
                left[...] = left[...] - factor * line
                inverse[...] = inverse[...] - factor * mine
                pivots[pl.ds(j, 1), :] = jnp.broadcast_to(pivot, (1, 128))
                return c

            lax.fori_loop(0, RANK, eliminate, 0)
            inverse[...] = inverse[...] / jnp.sqrt(pivots[:, 0:1]) * rs_row
            raw = jnp.concatenate([small[1, 0:4], small[1, 4:8]], axis=1)
            along = lax.broadcasted_iota(jnp.int32, (4, RANK), 1)
            old = jnp.where(along < MODES, raw * jnp.sqrt(diagonal), 0.0)
            old = jnp.concatenate([old, jnp.zeros((4, RANK), jnp.float32)], axis=0)
            fresh = mm(old, inverse[...], ((1,), (1,)))[0:4]
            fresh = jnp.where(along < MODES, fresh, raw)

            def is_step(k, s):
                return small[0, k + 1 : k + 2, 0:1] == float(s)

            rows = last_columns([fresh[s : s + 1] for s in range(4)], is_step)
            for k in range(4):
                small[2, k : k + 1] = rows[k][:, 0:128]
                small[3, k : k + 1] = rows[k][:, 128:RANK]
            load.wait()
            inverse[...] = inverse[...] * SCALE
            whole = mm(modes[...], inverse[:, 0:MODES], ((1,), (1,)))
            wide = lax.broadcasted_iota(jnp.int32, (ROWS_DEV, RANK), 1)
            q[...] = jnp.where(wide < MODES, whole, q[...])

        rows = jnp.concatenate([small[2, 0:4], small[3, 0:4]], axis=1)
        rows = jnp.concatenate([jnp.zeros((124, RANK), jnp.float32), rows], axis=0)
        lane = lax.broadcasted_iota(jnp.int32, (ROWS_DEV // PIECES, 128), 1)
        clear.start()
        stores = []
        for n, block in enumerate(blocks):

            @pl.when(good)
            def _():
                loads[n].wait()

            stores.append(
                pltpu.make_async_copy(q.at[block, 0:128], basis.at[block, 0:128], sem.at[4 + PIECES + n])
            )
            stores[-1].start()
            ends[block] = jnp.where(lane < 124, q[block, 128:RANK], mm(q[block], rows, ((1,), (1,))))
            stores.append(
                pltpu.make_async_copy(ends.at[block], basis.at[block, 128:RANK], sem.at[4 + 2 * PIECES + n])
            )
            stores[-1].start()
        clear.wait()
        for store in stores:
            store.wait()


def local(populations, cell_kind, snapshot_order, sample_phase, slab_map, weighted_modes):
    f32 = jnp.float32
    hbm = pl.BlockSpec(memory_space=pltpu.HBM)
    dma = pltpu.SemaphoreType.DMA

    def buffer(*shape):
        return pltpu.VMEM(shape, f32)

    field, gram, q, small = pl.pallas_call(
        first_kernel,
        out_shape=(
            jax.ShapeDtypeStruct((19, CX, NY, NZ), f32),
            jax.ShapeDtypeStruct((RANK, RANK), f32),
            jax.ShapeDtypeStruct((ROWS_DEV, RANK), f32),
            jax.ShapeDtypeStruct((4, 8, NZ), f32),
        ),
        in_specs=[hbm] * 6,
        out_specs=(hbm,) * 4,
        scratch_shapes=[
            buffer(19, CX, NY, NZ),
            buffer(NPLANE, NLINE, 4, NZ),
            buffer(ROWS_DEV, RANK),
            buffer(4, 8, NZ),
            buffer(19, CX, NY, NZ),
            pltpu.VMEM((CX, NY, NZ), jnp.int32),
            pltpu.SMEM((3,), jnp.int32),
            pltpu.SMEM((4,), jnp.int32),
            pltpu.SMEM((384,), jnp.int32),
            buffer(ROWS_DEV, MODES),
            buffer(STEPS, CX + 2, 5, NY, NZ),
            buffer(STEPS, CX + 2, 5, NY, NZ),
            buffer(STEPS, CX, 9, NY, NZ),
            buffer(CX, 3, NY, NZ),
            buffer(2, 4, NZ),
            buffer(CX, 4, NY, NZ),
            buffer(4, NY, NZ),
            buffer(3, 4, NZ),
            buffer(NZ, NZ),
            pltpu.SMEM((48,), jnp.int32),
            pltpu.SMEM((48,), jnp.int32),
            pltpu.SMEM((24,), jnp.int32),
            buffer(24, 2, 4, NZ),
            buffer(24, 3, 4, NZ),
            buffer(48, 2, 4, NZ),
            buffer(48, 2, 4, NZ),
            buffer(NLINE, 3, 2, 4, NZ),
            buffer(NLINE, 3, 2, 4, NZ),
            buffer(NPLANE, NLINE, 4, NZ),
            buffer(NPLANE, NLINE, 4, NZ),
            buffer(NLINE, 4, NZ),
            buffer(NLINE, 4, NZ),
            buffer(4, NZ),
            buffer(NLINE, 4, NZ),
            buffer(RANK, RANK),
            buffer(RANK, RANK),
            buffer(RANK, RANK),
            buffer(8, NZ),
            buffer(NLINE, 8, NZ),
            buffer(8, NZ),
            buffer(NPLANE, 8, NZ),
            dma((8,)),
            dma((5,)),
            dma((STEPS, 2)),
            dma((STEPS, 2)),
            dma((10,)),
            dma((10,)),
            pltpu.SemaphoreType.REGULAR,
        ],
        compiler_params=pltpu.CompilerParams(
            collective_id=0, has_side_effects=True, vmem_limit_bytes=ROOM
        ),
    )(populations, cell_kind, sample_phase, snapshot_order, slab_map, weighted_modes)
    return pl.pallas_call(
        second_kernel,
        out_shape=(
            jax.ShapeDtypeStruct((19, CX, NY, NZ), f32),
            jax.ShapeDtypeStruct((ROWS_DEV, RANK), f32),
        ),
        in_specs=[hbm] * 5,
        out_specs=(hbm, hbm),
        scratch_shapes=[
            buffer(19, CX, NY, NZ),
            buffer(ROWS_DEV, RANK),
            buffer(4, 8, NZ),
            buffer(ROWS_DEV, 128),
            buffer(ROWS_DEV, MODES),
            buffer(RANK, RANK),
            buffer(RANK, RANK),
            buffer(RANK, RANK),
            buffer(RANK, 128),
            dma((4 + 3 * PIECES,)),
        ],
        compiler_params=pltpu.CompilerParams(vmem_limit_bytes=ROOM),
    )(weighted_modes, field, gram, q, small)


def solution(mesh):
    return jax.shard_map(
        local,
        mesh=mesh,
        in_specs=(
            P(None, ("group", "slab"), None, None),
            P(("group", "slab"), None, None),
            P(),
            P(),
            P(),
            P(("group", "slab"), None),
        ),
        out_specs=(P(None, ("group", "slab"), None, None), P(("group", "slab"), None)),
        check_vma=False,
    )
```

```python
import functools
import math

import jax
import jax.numpy as jnp
from jax import lax
from jax.experimental import pallas as pl
from jax.experimental.pallas import tpu as pltpu
from jax.sharding import PartitionSpec as P

MESH = pl.DeviceIdType.MESH
STEPS = 4
SUB = 4
OMEGA = 0.9
INLET = 0.05
BIG = 1e30

DIRS = [
    (0, 0, 0),
    (1, 0, 0),
    (-1, 0, 0),
    (0, 1, 0),
    (0, -1, 0),
    (0, 0, 1),
    (0, 0, -1),
    (1, 1, 0),
    (-1, -1, 0),
    (1, -1, 0),
    (-1, 1, 0),
    (1, 0, 1),
    (-1, 0, -1),
    (1, 0, -1),
    (-1, 0, 1),
    (0, 1, 1),
    (0, -1, -1),
    (0, 1, -1),
    (0, -1, 1),
]
WEIGHTS = [1.0 / 3.0] + [1.0 / 18.0] * 6 + [1.0 / 36.0] * 12
OPP = [0, 2, 1, 4, 3, 6, 5, 8, 7, 10, 9, 12, 11, 14, 13, 16, 15, 18, 17]
EAST = [i for i in range(19) if DIRS[i][0] == 1]
WEST = [i for i in range(19) if DIRS[i][0] == -1]
REST = [i for i in range(19) if DIRS[i][0] == 0]

CX, NY, NZ = 4, 16, 128
NLINE = 16
NPLANE = 8
RANK = 256
MODES = 252
ROWS_DEV = 1152
ROWS_ALL = 128 * ROWS_DEV
SCALE = math.sqrt(ROWS_ALL)
PIECES = 1
ROOM = 60 * 1024 * 1024
LINE_FAR = [8, 7, 9, 6, 10, 5, 11, 4, 12, 3, 13, 2, 14, 1, 15]
PLANE_FAR = [4, 5, 3, 6, 2, 7, 1]
FAR_ALL = PLANE_FAR + [0]


def mm(a, b, dims):
    return lax.dot_general(
        a,
        b,
        (dims, ((), ())),
        precision=lax.Precision.HIGHEST,
        preferred_element_type=jnp.float32,
    )


def quick(a, b, dims):
    return lax.dot_general(
        a.astype(jnp.bfloat16),
        b.astype(jnp.bfloat16),
        (dims, ((), ())),
        preferred_element_type=jnp.float32,
    )


def inflow_value(i):
    along = DIRS[i][0] * INLET
    return WEIGHTS[i] * (1.0 + 3.0 * along + 4.5 * along * along - 1.5 * INLET * INLET)


def sums(f):
    density = f[0]
    for i in range(1, 19):
        density = density + f[i]
    totals = []
    for axis in range(3):
        plus = [f[i] for i in range(19) if DIRS[i][axis] == 1]
        minus = [f[i] for i in range(19) if DIRS[i][axis] == -1]
        totals.append(functools.reduce(lambda a, b: a + b, [a - b for a, b in zip(plus, minus)]))
    return density, totals


def moments(f):
    density, totals = sums(f)
    inverse = 1.0 / density
    return density, [total * inverse for total in totals]


def collide(f, kind):
    density, u = moments(f)
    square = 1.0 - 1.5 * (u[0] * u[0] + u[1] * u[1] + u[2] * u[2])
    fluid = kind == 0
    inlet = kind == 2
    scaled = {w: (OMEGA * w) * density for w in (1.0 / 3.0, 1.0 / 18.0, 1.0 / 36.0)}
    fallback = {}
    post = [None] * 19
    for i in range(19):
        value = inflow_value(i)
        if value not in fallback:
            fallback[value] = jnp.where(inlet, value, BIG)
    for i in range(19):
        if post[i] is not None:
            continue
        w = scaled[WEIGHTS[i]]
        if i == 0:
            post[0] = jnp.where(fluid, (1.0 - OMEGA) * f[0] + w * square, fallback[inflow_value(0)])
            continue
        along = None
        for axis in range(3):
            if DIRS[i][axis] != 0:
                term = u[axis] if DIRS[i][axis] == 1 else -u[axis]
                along = term if along is None else along + term
        even = w * (square + 4.5 * along * along)
        odd = w * (3.0 * along)
        j = OPP[i]
        post[i] = jnp.where(fluid, (1.0 - OMEGA) * f[i] + (even + odd), fallback[inflow_value(i)])
        post[j] = jnp.where(fluid, (1.0 - OMEGA) * f[j] + (even - odd), fallback[inflow_value(j)])
    return post, u


def shifted(plane, i):
    _, north, upward = DIRS[i]
    if north:
        plane = pltpu.roll(plane, north % NY, 0)
    if upward:
        plane = pltpu.roll(plane, upward % NZ, 1)
    return plane


def lower_half(error, row, col):
    return jnp.where(row > col, error, jnp.where(row == col, 0.5 * error, 0.0))


def square_iota():
    row = lax.broadcasted_iota(jnp.int32, (RANK, RANK), 0)
    col = lax.broadcasted_iota(jnp.int32, (RANK, RANK), 1)
    return row, col, (row == col).astype(jnp.float32)


def unit_diagonal(gram):
    row, col, _ = square_iota()
    whole = jnp.where(jnp.logical_and(row == col, row >= MODES), 1.0, gram)
    diagonal = jnp.where(row == col, whole, 0.0)
    along_row = jnp.sum(diagonal, axis=0, keepdims=True)
    rs_row = 1.0 / jnp.sqrt(along_row)
    rs_col = 1.0 / jnp.sqrt(jnp.sum(diagonal, axis=1, keepdims=True))
    return whole * rs_row * rs_col, rs_row, along_row


def last_columns(lines, is_step):
    lane = lax.broadcasted_iota(jnp.int32, (1, RANK), 1)
    old = [jnp.where(lane < MODES, line, 0.0) for line in lines]
    gram = [[None] * 4 for _ in range(4)]
    for s in range(4):
        for t in range(s + 1):
            own = jnp.where(lane == MODES + t, lines[s], 0.0)
            gram[s][t] = jnp.sum(own - old[s] * old[t] * (1.0 / ROWS_ALL), axis=1, keepdims=True)
            gram[t][s] = gram[s][t]

    def chosen(k, values):
        result = values[3]
        for s in range(3):
            result = jnp.where(is_step(k, s), values[s], result)
        return result

    half = [[chosen(k, [gram[s][t] for s in range(4)]) for t in range(4)] for k in range(4)]
    entry = [[chosen(j, half[k]) for j in range(k + 1)] for k in range(4)]
    start = []
    for s in range(4):
        start.append(SCALE * (lane == MODES + s).astype(jnp.float32) - old[s] * (SCALE / ROWS_ALL))
    low = [[None] * 4 for _ in range(4)]
    over = [None] * 4
    result = []
    for k in range(4):
        for j in range(k + 1):
            value = entry[k][j]
            for m in range(j):
                value = value - low[k][m] * low[j][m]
            if k == j:
                over[k] = 1.0 / jnp.sqrt(value)
            else:
                low[k][j] = value * over[j]
        line = chosen(k, start)
        for m in range(k):
            line = line - low[k][m] * result[m]
        result.append(line * over[k])
    return result


def first_kernel(
    pop_hbm,
    kind_hbm,
    phase_hbm,
    order_hbm,
    table_hbm,
    modes_hbm,
    field_hbm,
    gram_hbm,
    q_hbm,
    small_hbm,
    field,
    gram,
    q,
    small,
    pop,
    kind_ref,
    phase,
    order,
    table,
    modes,
    east,
    west,
    rest,
    speeds,
    samples,
    parts,
    across,
    ends,
    final,
    picks,
    picks_next,
    rows_next,
    landed_a,
    landed_b,
    ready_a,
    ready_b,
    got_a,
    got_b,
    pack,
    slot_a,
    rows_a,
    slot_b,
    rows_b,
    column,
    square,
    scaled,
    inverse,
    cross_own,
    cross_a,
    cross_mid,
    cross_b,
    load_sem,
    store_sem,
    halo_send,
    halo_recv,
    send_sem,
    recv_sem,
    go_sem,
):
    group = lax.axis_index("group")
    slab = lax.axis_index("slab")
    zpos = slab // NPLANE
    ppos = slab % NPLANE
    position = group * 128 + slab
    channel = group < 3
    has_west = jnp.logical_and(channel, position > 0)
    has_east = jnp.logical_and(channel, position < 383)
    west_id = ((position - 1) // 128, (position + 127) % 128)
    east_id = ((position + 1) // 128, (position + 1) % 128)
    ROUTE_A, ROUTE_B, LINE_A, LINE_B, GRAM_A, GRAM_B, GRAM_C, GRAM_D, CROSS_A, CROSS_B = range(10)
    odd = slab % 2

    barrier = pltpu.get_barrier_semaphore()

    def hello(target):
        pl.semaphore_signal(barrier, inc=1, device_id=target, device_id_type=MESH)

    loads = [
        pltpu.make_async_copy(a, b, load_sem.at[n])
        for n, (a, b) in enumerate(
            [
                (pop_hbm.at[:, 0], pop.at[:, 0]),
                (kind_hbm, kind_ref),
                (phase_hbm, phase),
                (table_hbm, table),
                (order_hbm, order),
                (modes_hbm, modes),
                (pop_hbm.at[:, CX - 1], pop.at[:, CX - 1]),
                (pop_hbm.at[:, 1 : CX - 1], pop.at[:, 1 : CX - 1]),
            ]
        )
    ]

    stores = [
        pltpu.make_async_copy(a, b, store_sem.at[n])
        for n, (a, b) in enumerate(
            [
                (field, field_hbm),
                (square, gram_hbm),
                (q.at[:, 0:128], q_hbm.at[:, 0:128]),
                (q.at[:, 128:RANK], q_hbm.at[:, 128:RANK]),
                (small, small_hbm),
            ]
        )
    ]

    @pl.when(channel)
    def _():
        for n in (0, 6, 1, 7, 2):
            loads[n].start()

    @pl.when(jnp.logical_not(channel))
    def _():
        loads[5].start()
        loads[4].start()
        loads[3].start()
        loads[2].start()

    def line_peer(d):
        return (group, ((zpos + d) % NLINE) * NPLANE + ppos)

    def plane_peer(d):
        return (3, zpos * NPLANE + (ppos + d) % NPLANE)

    def push(source, target, peer, n):
        pltpu.make_async_remote_copy(
            src_ref=source,
            dst_ref=target,
            send_sem=send_sem.at[n],
            recv_sem=recv_sem.at[n],
            device_id=peer,
            device_id_type=MESH,
        ).start()

    def to_line(source, target, n):
        for d in LINE_FAR:
            push(source, target, line_peer(d), n)

    def to_plane(source, target, n):
        for d in PLANE_FAR:
            push(source, target, plane_peer(d), n)

    def arrived(ref, n):
        pltpu.make_async_copy(ref, ref, recv_sem.at[n]).wait()

    def left_here(ref, n):
        pltpu.make_async_copy(ref, ref, send_sem.at[n]).wait()

    def keep_post(post, x, slot):
        for n, i in enumerate(EAST):
            east[slot, x + 1, n] = post[i]
        for n, i in enumerate(WEST):
            west[slot, x + 1, n] = post[i]
        for n, i in enumerate(REST):
            rest[slot, x, n] = post[i]

    def streamed(slot, x):
        f = [None] * 19
        for n, i in enumerate(REST):
            if i == 0:
                f[0] = rest[slot, x, 0]
                continue
            source = shifted(rest[slot, x, n], i)
            f[i] = jnp.where(source >= 0.5 * BIG, rest[slot, x, REST.index(OPP[i])], source)
        for n, i in enumerate(EAST):
            source = shifted(east[slot, x, n], i)
            f[i] = jnp.where(source >= 0.5 * BIG, west[slot, x + 1, WEST.index(OPP[i])], source)
        for n, i in enumerate(WEST):
            source = shifted(west[slot, x + 2, n], i)
            f[i] = jnp.where(source >= 0.5 * BIG, east[slot, x + 1, EAST.index(OPP[i])], source)
        return f

    def keep_speeds(u, kind, x):
        for c in range(3):
            speeds[x, c] = jnp.where(kind == 1, 0.0, u[c])

    def halo(slot):
        go_east = pltpu.make_async_remote_copy(
            src_ref=east.at[slot, CX],
            dst_ref=east.at[slot, 0],
            send_sem=halo_send.at[slot, 0],
            recv_sem=halo_recv.at[slot, 0],
            device_id=east_id,
            device_id_type=MESH,
        )
        go_west = pltpu.make_async_remote_copy(
            src_ref=west.at[slot, 1],
            dst_ref=west.at[slot, CX + 1],
            send_sem=halo_send.at[slot, 1],
            recv_sem=halo_recv.at[slot, 1],
            device_id=west_id,
            device_id_type=MESH,
        )
        return go_east, go_west

    def send_side(slot, side):
        go_east, go_west = halo(slot)

        @pl.when(jnp.logical_and(has_east, side == 1))
        def _():
            go_east.start()

        @pl.when(jnp.logical_and(has_west, side == 0))
        def _():
            go_west.start()

    def take_side(slot, side):
        go_east, go_west = halo(slot)

        @pl.when(jnp.logical_and(has_east, side == 1))
        def _():
            go_west.wait_recv()

        @pl.when(jnp.logical_and(has_west, side == 0))
        def _():
            go_east.wait_recv()

    def sides(fn):
        def body(n, c):
            fn((odd + n) % 2)
            return c

        lax.fori_loop(0, 2, body, 0)

    def first_plane(x):
        post, _ = collide([pop[i, x] for i in range(19)], kind_ref[x])
        keep_post(post, x, 0)

    def middle_plane(slot, x):
        kind = kind_ref[x]
        post, u = collide(streamed(slot, x), kind)
        keep_speeds(u, kind, x)
        keep_post(post, x, slot + 1)

    def keep_parts(f, kind, x):
        density, totals = sums(f)
        parts[x, 0] = jnp.where(kind == 1, 1.0, density)
        for c in range(3):
            parts[x, c + 1] = jnp.where(kind == 1, 0.0, totals[c])

    def last_plane(slot, x):
        kind = kind_ref[x]
        f = streamed(slot, x)
        for i in range(19):
            field[i, x] = jnp.where(kind == 1, pop[i, x], f[i])

    def edge_parts(slot, x):
        f = [None] * 19
        for n, i in enumerate(REST):
            if i == 0:
                f[0] = rest[slot, x, 0]
                continue
            source = shifted(rest[slot, x, n], i)
            f[i] = jnp.where(source >= 0.5 * BIG, rest[slot, x, REST.index(OPP[i])], source)
        for n, i in enumerate(EAST):
            back = west[slot, x + 1, WEST.index(OPP[i])]
            if x == 0:
                f[i] = jnp.where(shifted(east[slot - 1, 0, n], i) >= 0.5 * BIG, back, 0.0)
            else:
                source = shifted(east[slot, x, n], i)
                f[i] = jnp.where(source >= 0.5 * BIG, back, source)
        for n, i in enumerate(WEST):
            back = east[slot, x + 1, EAST.index(OPP[i])]
            if x == CX - 1:
                f[i] = jnp.where(shifted(west[slot - 1, CX + 1, n], i) >= 0.5 * BIG, back, 0.0)
            else:
                source = shifted(west[slot, x + 2, n], i)
                f[i] = jnp.where(source >= 0.5 * BIG, back, source)
        keep_parts(f, kind_ref[x], x)

    def out_parts(planes, dirs, wall):
        total = [jnp.zeros((NY, NZ), jnp.float32)] * 4
        for n, i in enumerate(dirs):
            source = planes[n]
            value = shifted(jnp.where(source >= 0.5 * BIG, 0.0, source), i)
            total[0] = total[0] + value
            for axis in range(3):
                if DIRS[i][axis] == 1:
                    total[axis + 1] = total[axis + 1] + value
                elif DIRS[i][axis] == -1:
                    total[axis + 1] = total[axis + 1] - value
        return [jnp.where(wall, 0.0, value) for value in total]

    def pair(fn):
        def body(n, c):
            fn(n)
            return c

        lax.fori_loop(0, 2, body, 0)

    @pl.when(channel)
    def _():
        @pl.when(has_east)
        def _():
            hello(east_id)

        @pl.when(has_west)
        def _():
            hello(west_id)

        for d in FAR_ALL:
            hello((3, zpos * NPLANE + (ppos + d) % NPLANE))

        samples[...] = jnp.zeros((2, 4, NZ), jnp.float32)
        ends[...] = jnp.zeros((3, 4, NZ), jnp.float32)

        @pl.when(position == 0)
        def _():
            east[:, 0] = jnp.full((STEPS, 5, NY, NZ), BIG, jnp.float32)

        @pl.when(position == 383)
        def _():
            west[:, CX + 1] = jnp.full((STEPS, 5, NY, NZ), BIG, jnp.float32)

        for n in (0, 6, 1):
            loads[n].wait()
        sides(lambda side: first_plane(3 * side))
        edge = jnp.logical_or(position == 0, position == 383)

        @pl.when(edge)
        def _():
            pl.semaphore_wait(barrier, 1)

        @pl.when(jnp.logical_not(edge))
        def _():
            pl.semaphore_wait(barrier, 2)

        sides(lambda side: send_side(0, side))
        loads[7].wait()
        pair(lambda n: first_plane(1 + n))
        loads[2].wait()

        lanes = lax.broadcasted_iota(jnp.int32, (NZ, NZ), 1)
        depth = lax.broadcasted_iota(jnp.int32, (NZ, NZ), 0)
        pick_z = (depth == phase[2] + SUB * (lanes % 32)).astype(jnp.float32)
        lane3 = lax.broadcasted_iota(jnp.int32, (3, NY, NZ), 2)
        row3 = lax.broadcasted_iota(jnp.int32, (3, NY, NZ), 1)
        pick_y = row3 == phase[1] + SUB * (lane3 // 32)

        def sample(step):
            plane = speeds[phase[0]].reshape(3 * NY, NZ)
            along = mm(plane, pick_z, ((1,), (0,))).reshape(3, NY, NZ)
            samples[step, 0:3] = jnp.sum(jnp.where(pick_y, along, 0.0), axis=1)

        def to_analysis(source, target, n):
            for d in FAR_ALL:
                push(source, target.at[group * NPLANE + ppos], (3, zpos * NPLANE + (ppos + d) % NPLANE), n)

        def one_step(slot, c, sampled=True):
            pair(lambda n: middle_plane(slot, 1 + n))

            def one_side(side):
                take_side(slot, side)
                middle_plane(slot, 3 * side)
                send_side(slot + 1, side)

            sides(one_side)
            if sampled:
                sample(slot)
            return c

        lax.fori_loop(0, 2, one_step, 0)
        pl.semaphore_wait(go_sem, 8)
        to_analysis(samples.at[0:2], landed_a, ROUTE_A)
        one_step(2, 0, sampled=False)
        last = STEPS - 1
        edge_parts(last, 0)
        edge_parts(last, CX - 1)
        to_east = out_parts([east[last, CX, n] for n in range(5)], EAST, west[last - 1, CX + 1, 0] >= 0.5 * BIG)
        to_west = out_parts([west[last, 1, n] for n in range(5)], WEST, east[last - 1, 0, 0] >= 0.5 * BIG)
        for c in range(4):
            across[c] = jnp.where(phase[0] == 0, to_east[c], jnp.where(phase[0] == CX - 1, to_west[c], 0.0))
        for x in range(1, CX - 1):
            keep_parts(streamed(last, x), kind_ref[x], x)
        lane11 = lax.broadcasted_iota(jnp.int32, (11, NY, NZ), 2)
        row11 = lax.broadcasted_iota(jnp.int32, (11, NY, NZ), 1)
        stack = [speeds[phase[0]].reshape(3 * NY, NZ), parts[phase[0]].reshape(4 * NY, NZ)]
        stack = jnp.concatenate(stack + [across[...].reshape(4 * NY, NZ)], axis=0)
        along = mm(stack, pick_z, ((1,), (0,))).reshape(11, NY, NZ)
        chosen = jnp.sum(jnp.where(row11 == phase[1] + SUB * (lane11 // 32), along, 0.0), axis=1)
        ends[0, 0:3] = chosen[0:3]
        ends[1] = chosen[3:7]
        ends[2] = chosen[7:11]
        to_analysis(ends, landed_b, ROUTE_B)

        pair(lambda n: last_plane(last, 1 + n))

        def last_side(side):
            take_side(last, side)
            last_plane(last, 3 * side)

        sides(last_side)
        stores[0].start()

        def sent(slot, c):
            go_east, go_west = halo(slot)

            @pl.when(has_east)
            def _():
                go_east.wait_send()

            @pl.when(has_west)
            def _():
                go_west.wait_send()

            return c

        lax.fori_loop(0, STEPS, sent, 0)
        left_here(landed_a.at[0:8], ROUTE_A)
        left_here(landed_b.at[0:8], ROUTE_B)
        stores[0].wait()

    @pl.when(jnp.logical_not(channel))
    def _():
        for d in LINE_FAR:
            hello(line_peer(d))
        for d in PLANE_FAR:
            hello(plane_peer(d))

        square[...] = jnp.zeros((RANK, RANK), jnp.float32)
        loads[5].wait()
        square[0:MODES, 0:MODES] = mm(modes[...], modes[...], ((0,), (0,)))
        for p in range(NPLANE):
            for z in range(NLINE):
                down, across = 32 * p + 4 * (z // 2), 128 * (z % 2)
                pack[p, z] = square[down : down + 4, across : across + 128]
        pl.semaphore_wait(barrier, 15 + 7 + 24)

        slot_a[ppos] = pack[ppos]
        for d in PLANE_FAR:
            push(pack.at[(ppos + d) % NPLANE], slot_a.at[ppos], plane_peer(d), GRAM_A)

        for n in range(24):
            pl.semaphore_signal(
                go_sem,
                inc=1,
                device_id=(n // NPLANE, zpos * NPLANE + (ppos + n) % NPLANE),
                device_id_type=MESH,
            )

        def forward(landed, ready, got, from_sem, to_sem, split=False):
            arrived(landed, from_sem)

            def place(n):
                source = picks[n]
                if split:
                    other = picks_next[n]
                    mine = jnp.maximum(source, 0)
                    ready[n, 0] = jnp.where(source >= 0, landed[mine, 0], 0.0)
                    own = jnp.where(source >= 0, landed[mine, 1], 0.0)
                    ready[n, 1] = own + jnp.where(other >= 0, landed[jnp.maximum(other, 0), 2], 0.0)
                else:
                    ready[n] = jnp.where(source >= 0, landed[jnp.maximum(source, 0)], 0.0)

            for d in LINE_FAR + [0]:
                first = 3 * ((zpos + d) % NLINE)
                for t in range(3):
                    place(first + t)
                if d:
                    push(ready.at[pl.ds(first, 3)], got.at[zpos], line_peer(d), to_sem)
                else:
                    got[zpos] = ready[pl.ds(first, 3)]

        arrived(slot_a.at[0:7], GRAM_A)
        rows_a[...] = jnp.sum(slot_a[...], axis=0)
        slot_b[zpos] = rows_a[zpos]
        for d in LINE_FAR:
            push(rows_a.at[(zpos + d) % NLINE], slot_b.at[zpos], line_peer(d), GRAM_B)
        loads[3].wait()
        loads[2].wait()

        def shift(n, c):
            home = (n // NPLANE) * 128 + zpos * NPLANE + n % NPLANE
            there = home + jnp.where(phase[0] == 0, 1, -1)
            inside = jnp.logical_and(there >= 0, there < 384)
            used = jnp.logical_and(inside, jnp.logical_or(phase[0] == 0, phase[0] == CX - 1))
            rows_next[n] = jnp.where(used, table[jnp.minimum(jnp.maximum(there, 0), 383)], -1)
            return c

        lax.fori_loop(0, 24, shift, 0)

        def pick(n, c):
            found = jnp.int32(-1)
            found_next = jnp.int32(-1)
            wanted = 24 * (n // 3) + 3 * ppos + n % 3
            for g in range(3):
                for p in range(NPLANE):
                    row = table[g * 128 + zpos * NPLANE + p]
                    found = jnp.where(row == wanted, g * NPLANE + p, found)
                    row_next = rows_next[g * NPLANE + p]
                    found_next = jnp.where(row_next == wanted, g * NPLANE + p, found_next)
            picks[n] = found
            picks_next[n] = found_next
            return c

        lax.fori_loop(0, 48, pick, 0)

        arrived(slot_b.at[0:15], GRAM_B)
        rows_b[...] = jnp.sum(slot_b[...], axis=0)
        column[zpos] = rows_b[...]
        to_line(rows_b, column.at[zpos], GRAM_C)
        forward(landed_a, ready_a, got_a, ROUTE_A, LINE_A)
        arrived(column.at[0:15], GRAM_C)
        gram[ppos] = column[...]
        to_plane(column, gram.at[ppos], GRAM_D)
        forward(landed_b, ready_b, got_b, ROUTE_B, LINE_B, split=True)
        arrived(gram.at[0:7], GRAM_D)
        for p in range(NPLANE):
            for z in range(NLINE):
                down, across = 32 * p + 4 * (z // 2), 128 * (z % 2)
                square[down : down + 4, across : across + 128] = gram[p, z]
        stores[1].start()

        row, col, eye = square_iota()
        matrix, rs_row, _ = unit_diagonal(square[...])
        scaled[...] = matrix
        lower = lower_half(matrix - eye, row, col)
        upper = (matrix - eye) - lower
        mixed = quick(lower, matrix - eye, ((1,), (0,)))
        second = lower_half(quick(mixed - upper, upper, ((1,), (0,))) - mixed, row, col)
        inverse[...] = eye - lower - second + quick(second, lower, ((1,), (0,)))
        here = inverse[...]
        error = mm(mm(here, scaled[...], ((1,), (0,))), here, ((1,), (1,))) - eye
        inverse[...] = here - quick(lower_half(error, row, col), here, ((1,), (0,)))
        size = jnp.sum(jnp.sum(error * error, axis=0, keepdims=True), axis=1, keepdims=True)
        good = jnp.broadcast_to(size < 1e-6, (RANK, RANK))
        factor = jnp.where(good, inverse[...], eye) * rs_row
        inverse[...] = factor * SCALE
        q[...] = mm(modes[...], inverse[:, 0:MODES], ((1,), (1,)))
        stores[2].start()
        loads[4].wait()
        small[...] = jnp.zeros((4, 8, NZ), jnp.float32)
        small[0] = jnp.broadcast_to(size, (8, NZ))
        for k in range(4):
            small[0, k + 1 : k + 2] = jnp.full((1, NZ), 1.0, jnp.float32) * order[k].astype(jnp.float32)

        lane = lax.broadcasted_iota(jnp.int32, (NZ, NZ), 1)

        def products(steps):
            tall = final[...].T
            low_sum = [jnp.zeros((8, NZ), jnp.float32) for _ in steps]
            high_sum = [jnp.zeros((8, NZ), jnp.float32) for _ in steps]
            for n in range(9):
                block = pl.ds(128 * n, 128)
                spot = 4 * (n // 3) + n % 3
                wide = []
                for s in steps:
                    wide.append(jnp.broadcast_to(tall[:, 16 * s + spot : 16 * s + spot + 1], (NZ, NZ)))
                low = q[block, 0:128]
                high = q[block, 128:RANK]
                for m, s in enumerate(steps):
                    high = jnp.where(lane == 124 + s, wide[m], high)
                q[block, 128:RANK] = high
                for m in range(len(steps)):
                    low_sum[m] = low_sum[m] + jnp.sum((wide[m] * low).reshape(16, 8, NZ), axis=0)
                    high_sum[m] = high_sum[m] + jnp.sum((wide[m] * high).reshape(16, 8, NZ), axis=0)
            for m, s in enumerate(steps):
                cross_own[s : s + 1] = jnp.sum(low_sum[m], axis=0, keepdims=True)
                cross_own[s + 4 : s + 5] = jnp.sum(high_sum[m], axis=0, keepdims=True)

        arrived(got_a.at[0:15], LINE_A)
        final[...] = jnp.zeros((NZ, NZ), jnp.float32)
        sum_a = jnp.sum(got_a[...], axis=0)
        for t in range(3):
            for s in range(2):
                final[16 * s + 4 * t : 16 * s + 4 * t + 4] = sum_a[t, s]
        products((0, 1))
        arrived(got_b.at[0:15], LINE_B)
        sum_b = jnp.sum(got_b[...], axis=0)
        for t in range(3):
            final[32 + 4 * t : 36 + 4 * t] = sum_b[t, 0]
            final[48 + 4 * t : 51 + 4 * t] = sum_b[t, 1, 1:4] / sum_b[t, 1, 0:1]
        products((2, 3))

        cross_a[zpos] = cross_own[...]
        to_line(cross_own, cross_a.at[zpos], CROSS_A)
        stores[3].start()
        arrived(cross_a.at[0:15], CROSS_A)
        cross_mid[...] = jnp.sum(cross_a[...], axis=0)
        cross_b[ppos] = cross_mid[...]
        to_plane(cross_mid, cross_b.at[ppos], CROSS_B)
        arrived(cross_b.at[0:7], CROSS_B)
        both = jnp.sum(cross_b[...], axis=0)
        small[1] = both
        lines = [jnp.concatenate([both[s : s + 1], both[s + 4 : s + 5]], axis=1) for s in range(4)]
        for k, tail in enumerate(last_columns(lines, lambda k, s: order[k] == s)):
            small[2, k : k + 1] = tail[:, 0:128]
            small[3, k : k + 1] = tail[:, 128:RANK]
        stores[4].start()

        left_here(slot_a.at[0:7], GRAM_A)
        left_here(slot_b.at[0:15], GRAM_B)
        left_here(column.at[0:15], GRAM_C)
        left_here(gram.at[0:7], GRAM_D)
        left_here(got_a.at[0:15], LINE_A)
        left_here(got_b.at[0:15], LINE_B)
        left_here(cross_a.at[0:15], CROSS_A)
        left_here(cross_b.at[0:7], CROSS_B)
        for n in range(1, 5):
            stores[n].wait()


def second_kernel(
    modes_hbm, field, gram_hbm, q_hbm, small_hbm, lattice, basis, passing, q, small, ends, modes, gram, left, inverse, pivots, sem
):
    group = lax.axis_index("group")

    @pl.when(group < 3)
    def _():
        load = pltpu.make_async_copy(field, passing, sem.at[0])
        load.start()
        q[...] = jnp.zeros((ROWS_DEV, RANK), jnp.float32)
        clear = pltpu.make_async_copy(q, basis, sem.at[1])
        clear.start()
        load.wait()
        store = pltpu.make_async_copy(passing, lattice, sem.at[2])
        store.start()
        store.wait()
        clear.wait()

    @pl.when(group == 3)
    def _():
        load_small = pltpu.make_async_copy(small_hbm, small, sem.at[0])
        load_small.start()
        blocks = [pl.ds(n * (ROWS_DEV // PIECES), ROWS_DEV // PIECES) for n in range(PIECES)]
        loads = [
            pltpu.make_async_copy(q_hbm.at[block], q.at[block], sem.at[4 + n]) for n, block in enumerate(blocks)
        ]
        for load in loads:
            load.start()
        passing[...] = jnp.zeros((19, CX, NY, NZ), jnp.float32)
        clear = pltpu.make_async_copy(passing, lattice, sem.at[1])
        load_small.wait()
        good = small[0, 0, 0] < 1e-6

        @pl.when(jnp.logical_not(good))
        def _():
            for load in loads:
                load.wait()
            load = pltpu.make_async_copy(modes_hbm, modes, sem.at[2])
            load.start()
            load_gram = pltpu.make_async_copy(gram_hbm, gram, sem.at[3])
            load_gram.start()
            load_gram.wait()
            row, col, eye = square_iota()
            matrix, rs_row, diagonal = unit_diagonal(gram[...])
            left[...] = matrix
            inverse[...] = eye
            pivots[...] = jnp.ones((RANK, 128), jnp.float32)

            def eliminate(j, c):
                line = left[pl.ds(j, 1), :]
                mine = inverse[pl.ds(j, 1), :]
                along = lax.broadcasted_iota(jnp.int32, (1, RANK), 1)
                pivot = jnp.sum(jnp.where(along == j, line, 0.0), axis=1, keepdims=True)
                column = jnp.sum(jnp.where(col == j, left[...], 0.0), axis=1, keepdims=True)
                below = lax.broadcasted_iota(jnp.int32, (RANK, 1), 0) > j
                factor = jnp.where(below, column / pivot, 0.0)
                left[...] = left[...] - factor * line
                inverse[...] = inverse[...] - factor * mine
                pivots[pl.ds(j, 1), :] = jnp.broadcast_to(pivot, (1, 128))
                return c

            lax.fori_loop(0, RANK, eliminate, 0)
            inverse[...] = inverse[...] / jnp.sqrt(pivots[:, 0:1]) * rs_row
            raw = jnp.concatenate([small[1, 0:4], small[1, 4:8]], axis=1)
            along = lax.broadcasted_iota(jnp.int32, (4, RANK), 1)
            old = jnp.where(along < MODES, raw * jnp.sqrt(diagonal), 0.0)
            old = jnp.concatenate([old, jnp.zeros((4, RANK), jnp.float32)], axis=0)
            fresh = mm(old, inverse[...], ((1,), (1,)))[0:4]
            fresh = jnp.where(along < MODES, fresh, raw)

            def is_step(k, s):
                return small[0, k + 1 : k + 2, 0:1] == float(s)

            rows = last_columns([fresh[s : s + 1] for s in range(4)], is_step)
            for k in range(4):
                small[2, k : k + 1] = rows[k][:, 0:128]
                small[3, k : k + 1] = rows[k][:, 128:RANK]
            load.wait()
            inverse[...] = inverse[...] * SCALE
            whole = mm(modes[...], inverse[:, 0:MODES], ((1,), (1,)))
            wide = lax.broadcasted_iota(jnp.int32, (ROWS_DEV, RANK), 1)
            q[...] = jnp.where(wide < MODES, whole, q[...])

        rows = jnp.concatenate([small[2, 0:4], small[3, 0:4]], axis=1)
        rows = jnp.concatenate([jnp.zeros((124, RANK), jnp.float32), rows], axis=0)
        lane = lax.broadcasted_iota(jnp.int32, (ROWS_DEV // PIECES, 128), 1)
        clear.start()
        stores = []
        for n, block in enumerate(blocks):

            @pl.when(good)
            def _():
                loads[n].wait()

            stores.append(
                pltpu.make_async_copy(q.at[block, 0:128], basis.at[block, 0:128], sem.at[4 + PIECES + n])
            )
            stores[-1].start()
            ends[block] = jnp.where(lane < 124, q[block, 128:RANK], mm(q[block], rows, ((1,), (1,))))
            stores.append(
                pltpu.make_async_copy(ends.at[block], basis.at[block, 128:RANK], sem.at[4 + 2 * PIECES + n])
            )
            stores[-1].start()
        clear.wait()
        for store in stores:
            store.wait()


def local(populations, cell_kind, snapshot_order, sample_phase, slab_map, weighted_modes):
    f32 = jnp.float32
    hbm = pl.BlockSpec(memory_space=pltpu.HBM)
    dma = pltpu.SemaphoreType.DMA

    def buffer(*shape):
        return pltpu.VMEM(shape, f32)

    field, gram, q, small = pl.pallas_call(
        first_kernel,
        out_shape=(
            jax.ShapeDtypeStruct((19, CX, NY, NZ), f32),
            jax.ShapeDtypeStruct((RANK, RANK), f32),
            jax.ShapeDtypeStruct((ROWS_DEV, RANK), f32),
            jax.ShapeDtypeStruct((4, 8, NZ), f32),
        ),
        in_specs=[hbm] * 6,
        out_specs=(hbm,) * 4,
        scratch_shapes=[
            buffer(19, CX, NY, NZ),
            buffer(NPLANE, NLINE, 4, NZ),
            buffer(ROWS_DEV, RANK),
            buffer(4, 8, NZ),
            buffer(19, CX, NY, NZ),
            pltpu.VMEM((CX, NY, NZ), jnp.int32),
            pltpu.SMEM((3,), jnp.int32),
            pltpu.SMEM((4,), jnp.int32),
            pltpu.SMEM((384,), jnp.int32),
            buffer(ROWS_DEV, MODES),
            buffer(STEPS, CX + 2, 5, NY, NZ),
            buffer(STEPS, CX + 2, 5, NY, NZ),
            buffer(STEPS, CX, 9, NY, NZ),
            buffer(CX, 3, NY, NZ),
            buffer(2, 4, NZ),
            buffer(CX, 4, NY, NZ),
            buffer(4, NY, NZ),
            buffer(3, 4, NZ),
            buffer(NZ, NZ),
            pltpu.SMEM((48,), jnp.int32),
            pltpu.SMEM((48,), jnp.int32),
            pltpu.SMEM((24,), jnp.int32),
            buffer(24, 2, 4, NZ),
            buffer(24, 3, 4, NZ),
            buffer(48, 2, 4, NZ),
            buffer(48, 2, 4, NZ),
            buffer(NLINE, 3, 2, 4, NZ),
            buffer(NLINE, 3, 2, 4, NZ),
            buffer(NPLANE, NLINE, 4, NZ),
            buffer(NPLANE, NLINE, 4, NZ),
            buffer(NLINE, 4, NZ),
            buffer(NLINE, 4, NZ),
            buffer(4, NZ),
            buffer(NLINE, 4, NZ),
            buffer(RANK, RANK),
            buffer(RANK, RANK),
            buffer(RANK, RANK),
            buffer(8, NZ),
            buffer(NLINE, 8, NZ),
            buffer(8, NZ),
            buffer(NPLANE, 8, NZ),
            dma((8,)),
            dma((5,)),
            dma((STEPS, 2)),
            dma((STEPS, 2)),
            dma((10,)),
            dma((10,)),
            pltpu.SemaphoreType.REGULAR,
        ],
        compiler_params=pltpu.CompilerParams(
            collective_id=0, has_side_effects=True, vmem_limit_bytes=ROOM
        ),
    )(populations, cell_kind, sample_phase, snapshot_order, slab_map, weighted_modes)
    return pl.pallas_call(
        second_kernel,
        out_shape=(
            jax.ShapeDtypeStruct((19, CX, NY, NZ), f32),
            jax.ShapeDtypeStruct((ROWS_DEV, RANK), f32),
        ),
        in_specs=[hbm] * 5,
        out_specs=(hbm, hbm),
        scratch_shapes=[
            buffer(19, CX, NY, NZ),
            buffer(ROWS_DEV, RANK),
            buffer(4, 8, NZ),
            buffer(ROWS_DEV, 128),
            buffer(ROWS_DEV, MODES),
            buffer(RANK, RANK),
            buffer(RANK, RANK),
            buffer(RANK, RANK),
            buffer(RANK, 128),
            dma((4 + 3 * PIECES,)),
        ],
        compiler_params=pltpu.CompilerParams(vmem_limit_bytes=ROOM),
    )(weighted_modes, field, gram, q, small)


def solution(mesh):
    return jax.shard_map(
        local,
        mesh=mesh,
        in_specs=(
            P(None, ("group", "slab"), None, None),
            P(("group", "slab"), None, None),
            P(),
            P(),
            P(),
            P(("group", "slab"), None),
        ),
        out_specs=(P(None, ("group", "slab"), None, None), P(("group", "slab"), None)),
        check_vma=False,
    )
```
